128 devices in a mesh: gx: 8 (over x, core), gy: 16 (over y, z).
Axes of the slice: x: 4, y: 4, z: 4, core: 2. Of those that a mesh axis runs over, the one named last changes fastest.
Arguments:
- source_term: float32 [384, 32768], P(('gx', 'gy')), may hold values from -4 to 4
- inverse_density: float32 [384, 32768], P(('gx', 'gy')), may hold values from 1 to 8
- box_counts: int32 [128], P(('gx', 'gy')), may hold values from 1 to 3, as said below
- ghost_from: int32 [384, 4], P(('gx', 'gy')), may hold values from -1 to 383, as said below
Outputs:
- correction: float32 [384, 32768], P(('gx', 'gy'))
- residual: float32 [384, 32768], P(('gx', 'gy'))
- residual_norm: float32 [], replicated
The draws below stay inside these ranges and needn't reach their ends.
Inputs may be any that keep to these rules, and one draw needn't show every extreme that they name: `box_counts`: every device owns at least one box and at least one device owns 3. `ghost_from`: entries name global slots (device times 3 plus local slot) of used slots; unused slots and faces on the domain's walls hold -1. Neighbours are mutual across the opposite face. The owner of a neighbour lies within 3 devices of the slot's owner in the order of gx+gy: across face 0 at or before it, across face 1 at or after it, across faces 2 and 3 at most one device away.
All inputs are finite; a program needn't handle non-finite values.
Results may differ from the reference program's by a relative error of at most 0.0003.
Values sent between devices are 32-bit elements; how exact they have to be, the bound alone decides.
No kernel may reach another device: no remote copies, remote signals or barrier semaphores. Data moves between devices by JAX's collectives and lax.ppermute only.
A program may use at most 192 MiB of HBM per device.

```python
import math
import jax
import jax.numpy as jnp
from jax import lax

EDGE = 32
SLOTS = 3
SWEEPS = 2
BOTTOM_ITERS = 8
BOX_SLOTS = 384
DEVICES = 128


def layout(key):
    first_key, second_key, third_key = jax.random.split(key, 3)
    picker = jax.random.randint(first_key, (DEVICES,), 0, 4)
    modest = jax.random.randint(second_key, (DEVICES,), 1, SLOTS)
    counts = jnp.where(picker == 0, SLOTS, modest)
    forced = jax.random.randint(third_key, (), 0, DEVICES)
    counts = jnp.where(jnp.arange(DEVICES) == forced, SLOTS, counts).astype(jnp.int32)
    starts = jnp.cumsum(counts) - counts
    box_total = jnp.sum(counts)
    slot_ids = jnp.arange(BOX_SLOTS, dtype=jnp.int32)
    device_ids = slot_ids // SLOTS
    local_ids = slot_ids % SLOTS
    used = local_ids < counts[device_ids]
    curve_pos = starts[device_ids] + local_ids
    column = curve_pos // 2
    row_in = jnp.where(column % 2 == 0, curve_pos % 2, 1 - curve_pos % 2)

    def place(column_at, row_at):
        return 2 * column_at + jnp.where(column_at % 2 == 0, row_at, 1 - row_at)
    west_pos = place(column - 1, row_in)
    east_pos = place(column + 1, row_in)
    south_pos = place(column, 0 * row_in)
    north_pos = place(column, 0 * row_in + 1)
    west_ok = column >= 1
    east_ok = east_pos < box_total
    south_ok = (row_in == 1) & (south_pos < box_total)
    north_ok = (row_in == 0) & (north_pos < box_total)

    def global_slot(target):
        owner_ids = jnp.sum((starts[None, :] <= target[:, None]).astype(jnp.int32), axis=1) - 1
        owner_ids = jnp.clip(owner_ids, 0, DEVICES - 1)
        return owner_ids * SLOTS + (target - starts[owner_ids])
    columns_out = []
    for target, exists in ((west_pos, west_ok), (east_pos, east_ok), (south_pos, south_ok), (north_pos, north_ok)):
        columns_out.append(jnp.where(used & exists, global_slot(target), -1))
    ghosts = jnp.stack(columns_out, axis=1).astype(jnp.int32)
    return (counts, ghosts)


def draw_box_counts(key, part):
    counts, ghosts = layout(key)
    return counts


def draw_ghost_from(key, part):
    counts, ghosts = layout(key)
    return ghosts


def draw_source_term(key, part):
    key = jax.random.fold_in(key, 11)
    values = 0.8 * jnp.clip(jax.random.normal(key, (BOX_SLOTS, EDGE ** 3), jnp.float32), -5.0, 5.0)
    return values


def block_scale(own_key, shape, shards, smallest, high):
    factor_of = 1.0
    for dim, shards_of in shards:
        steps = jax.random.uniform(jax.random.fold_in(jax.random.fold_in(own_key, 6), dim), (shards_of,), jnp.float32, smallest / len(shards), high / len(shards))
        factor_of = factor_of * jnp.repeat(jnp.exp(steps), shape[dim] // shards_of).reshape((-1,) + (1,) * (len(shape) - 1 - dim))
    return factor_of


def setup_inputs(seed: int = 0) -> dict:
    key_list = jax.random.split(jax.random.key(seed), 5)
    source_term = draw_source_term(jax.random.fold_in(key_list[4], 71), 0)
    inverse_density = jnp.clip(jnp.exp(math.log(8.0) - 2.0794415 * jax.random.uniform(key_list[1], (BOX_SLOTS, EDGE ** 3), jnp.float32) ** block_scale(key_list[1], (BOX_SLOTS, EDGE ** 3), ((0, 128),), -0.2, 0.2)), 1.0, 8.0)
    box_counts = draw_box_counts(jax.random.fold_in(key_list[4], 71), 0)
    ghost_from = draw_ghost_from(jax.random.fold_in(key_list[4], 71), 0)
    return dict(source_term=source_term, inverse_density=inverse_density, box_counts=box_counts, ghost_from=ghost_from)


RELAXATION = 2.0 / 3.0
OPPOSITE = (1, 0, 3, 2)

def face_table(level_field, box_edge):
    slot_total = level_field.shape[0]
    cube_view = level_field.reshape(slot_total, box_edge, box_edge, box_edge)
    side_area = box_edge * box_edge
    return jnp.stack([cube_view[:, 0].reshape(slot_total, side_area), cube_view[:, box_edge - 1].reshape(slot_total, side_area), cube_view[:, :, 0].reshape(slot_total, side_area), cube_view[:, :, box_edge - 1].reshape(slot_total, side_area)], axis=1)

def lookup(face_rows, ghost_from):
    flat_rows = face_rows.reshape(-1, face_rows.shape[2])
    opposite = jnp.array(OPPOSITE, jnp.int32)
    present = ghost_from >= 0
    position = jnp.where(present, ghost_from * 4 + opposite[None, :], 0).astype(jnp.int32)
    picked = flat_rows[position]
    return jnp.where(present[:, :, None], picked, jnp.zeros_like(picked))

def neighbours(level_field, ghost_faces, box_edge):
    slot_total = level_field.shape[0]
    cube_view = level_field.reshape(slot_total, box_edge, box_edge, box_edge)
    west_ghost = ghost_faces[:, 0].reshape(slot_total, 1, box_edge, box_edge)
    east_ghost = ghost_faces[:, 1].reshape(slot_total, 1, box_edge, box_edge)
    south_ghost = ghost_faces[:, 2].reshape(slot_total, box_edge, 1, box_edge)
    north_ghost = ghost_faces[:, 3].reshape(slot_total, box_edge, 1, box_edge)
    along_xdir = jnp.concatenate([west_ghost, cube_view, east_ghost], axis=1)
    along_ydir = jnp.concatenate([south_ghost, cube_view, north_ghost], axis=2)
    zero_layer = jnp.zeros_like(cube_view[:, :, :, :1])
    along_zdir = jnp.concatenate([zero_layer, cube_view, zero_layer], axis=3)
    return (along_xdir[:, :-2], along_xdir[:, 2:], along_ydir[:, :, :-2], along_ydir[:, :, 2:], along_zdir[:, :, :, :-2], along_zdir[:, :, :, 2:])

def weights(present_float, box_edge):
    ramp_cells = jnp.arange(box_edge)
    first_cell = ramp_cells == 0
    last_cell = ramp_cells == box_edge - 1
    across_face = present_float[:, :, None, None, None]
    west_weight = jnp.where(first_cell[None, :, None, None], across_face[:, 0], 1.0)
    east_weight = jnp.where(last_cell[None, :, None, None], across_face[:, 1], 1.0)
    south_weight = jnp.where(first_cell[None, None, :, None], across_face[:, 2], 1.0)
    north_weight = jnp.where(last_cell[None, None, :, None], across_face[:, 3], 1.0)
    below_weight = jnp.where(first_cell, 0.0, 1.0).astype(jnp.float32)
    above_weight = jnp.where(last_cell, 0.0, 1.0).astype(jnp.float32)
    return (west_weight, east_weight, south_weight, north_weight, below_weight, above_weight)

def operate(level_field, coefficient, ghost_faces, beta_faces, present_float, box_edge, level_scale):
    slot_total = level_field.shape[0]
    field_cube = level_field.reshape(slot_total, box_edge, box_edge, box_edge)
    beta_cube = coefficient.reshape(slot_total, box_edge, box_edge, box_edge)
    cell_sides = neighbours(level_field, ghost_faces, box_edge)
    beta_sides = neighbours(coefficient, beta_faces, box_edge)
    flux_sum = jnp.zeros_like(field_cube)
    for neighbour, beta_near, weight in zip(cell_sides, beta_sides, weights(present_float, box_edge)):
        flux_sum = flux_sum + 0.5 * (beta_cube + beta_near) * weight * (field_cube - neighbour)
    return (level_scale * flux_sum).reshape(level_field.shape)

def diagonal(coefficient, beta_faces, present_float, box_edge, level_scale):
    slot_total = coefficient.shape[0]
    beta_cube = coefficient.reshape(slot_total, box_edge, box_edge, box_edge)
    beta_sides = neighbours(coefficient, beta_faces, box_edge)
    coef_sum = jnp.zeros_like(beta_cube)
    for beta_near, weight in zip(beta_sides, weights(present_float, box_edge)):
        coef_sum = coef_sum + 0.5 * (beta_cube + beta_near) * weight
    return (level_scale * coef_sum).reshape(coefficient.shape)

def restrict(level_field, box_edge):
    half_edge = box_edge // 2
    slot_total = level_field.shape[0]
    blocks = level_field.reshape(slot_total, half_edge, 2, half_edge, 2, half_edge, 2)
    return lax.optimization_barrier(jnp.mean(blocks, axis=(2, 4, 6))).reshape(slot_total, half_edge ** 3)

def prolong(level_field, coarse_edge):
    slot_total = level_field.shape[0]
    blocks = level_field.reshape(slot_total, coarse_edge, 1, coarse_edge, 1, coarse_edge, 1)
    blocks = jnp.broadcast_to(blocks, (slot_total, coarse_edge, 2, coarse_edge, 2, coarse_edge, 2))
    return blocks.reshape(slot_total, (2 * coarse_edge) ** 3)

def smooth(level_field, target, apply_level, diag_level, sweep_total):
    for sweep_index in range(sweep_total):
        level_field = level_field + RELAXATION * (target - apply_level(level_field)) / diag_level
    return level_field

def make_level(coefficient, ghost_from, present_float, box_edge, level_scale):
    beta_faces = lookup(face_table(coefficient, box_edge), ghost_from)
    diag_level = diagonal(coefficient, beta_faces, present_float, box_edge, level_scale)

    def apply_level(level_field):
        ghost_faces = lookup(face_table(level_field, box_edge), ghost_from)
        return operate(level_field, coefficient, ghost_faces, beta_faces, present_float, box_edge, level_scale)
    return (apply_level, diag_level)

def keep_value(value):
    return value

def conjugate(shifted, apply_level, reduce_curve, reduce_norm):
    solution = jnp.zeros_like(shifted)
    remainder = shifted
    direction = shifted
    norm_now = reduce_norm(jnp.sum(remainder * remainder))
    for iteration in range(BOTTOM_ITERS):
        image = apply_level(direction)
        step_size = norm_now / reduce_curve(jnp.sum(direction * image))
        solution = solution + step_size * direction
        if iteration + 1 < BOTTOM_ITERS:
            remainder = remainder - step_size * image
            norm_next = reduce_norm(jnp.sum(remainder * remainder))
            direction = remainder + norm_next / norm_now * direction
            norm_now = norm_next
    return solution

def reference(source_term, inverse_density, box_counts, ghost_from):
    slot_total = source_term.shape[0]
    slot_ids = jnp.arange(slot_total, dtype=jnp.int32)
    owned = box_counts[slot_ids // SLOTS]
    valid_mask = (slot_ids % SLOTS < owned).astype(jnp.float32)[:, None]
    present_float = (ghost_from >= 0).astype(jnp.float32)
    source = source_term * valid_mask
    fine_edge = EDGE
    middle_edge = EDGE // 2
    bottom_edge = EDGE // 4
    middle_beta = restrict(inverse_density, fine_edge)
    bottom_beta = restrict(middle_beta, middle_edge)
    fine_apply, fine_diag = make_level(inverse_density, ghost_from, present_float, fine_edge, 1.0)
    middle_apply, middle_diag = make_level(middle_beta, ghost_from, present_float, middle_edge, 0.25)
    bottom_apply, bottom_diag = make_level(bottom_beta, ghost_from, present_float, bottom_edge, 0.0625)
    fine_field = RELAXATION * source / fine_diag
    fine_field = smooth(fine_field, source, fine_apply, fine_diag, SWEEPS - 1)
    middle_source = restrict(source - fine_apply(fine_field), fine_edge)
    middle_field = RELAXATION * middle_source / middle_diag
    middle_field = smooth(middle_field, middle_source, middle_apply, middle_diag, SWEEPS - 1)
    bottom_source = restrict(middle_source - middle_apply(middle_field), middle_edge)
    box_total = jnp.sum(box_counts).astype(jnp.float32)
    rhs_total = jnp.sum(bottom_source)
    shifted = (bottom_source - rhs_total / (box_total * bottom_edge ** 3)) * valid_mask
    solution = conjugate(shifted, bottom_apply, keep_value, keep_value)
    middle_field = middle_field + prolong(solution, bottom_edge)
    middle_field = smooth(middle_field, middle_source, middle_apply, middle_diag, SWEEPS)
    fine_field = fine_field + prolong(middle_field, middle_edge)
    fine_field = smooth(fine_field, source, fine_apply, fine_diag, SWEEPS)
    cell_total = box_total * fine_edge ** 3
    correction = (fine_field - jnp.sum(fine_field) / cell_total) * valid_mask
    residual = source - fine_apply(correction)
    residual_norm = jnp.sqrt(jnp.sum(residual * residual) / cell_total)
    return (correction, residual, residual_norm)
```

```python
import functools

import jax
import jax.numpy as jnp
from jax import lax
from jax.experimental import pallas as pl
from jax.experimental.pallas import tpu as pltpu
from jax.sharding import PartitionSpec as P

AX = ("gx", "gy")
DEVICES = 128
SLOTS = 3
BOTTOM_ITERS = 8
RELAXATION = 2.0 / 3.0
F32 = jnp.float32
I32 = jnp.int32

PLANES = (32, 16)


def iota(shape, dim):
    return lax.broadcasted_iota(I32, shape, dim)


def lanes():
    return iota((8, 128), 1)


def subs():
    return iota((8, 128), 0)


def roll(x, shift, axis):
    return pltpu.roll(x, shift, axis)


class Tile:
    def __init__(self, lv):
        self.zs, self.ys = 1 << lv, 32 << lv
        lane, sub = lanes(), subs()
        self.south_in = lane >= self.ys
        self.north_in = lane < 128 - self.ys
        self.first_row = sub == 0
        self.last_row = sub == 7
        self.south_edge = self.first_row & (lane < self.ys)
        self.z_low = (lane & 31) < self.zs

    def south(self, v, row):
        r = roll(v, self.ys, 1)
        return jnp.where(self.south_in, r, jnp.where(self.first_row, row, roll(r, 1, 0)))

    def north(self, v, edge):
        r = roll(v, 128 - self.ys, 1)
        return jnp.where(self.north_in, r, jnp.where(self.last_row, edge, roll(r, 7, 0)))

    def below(self, v):
        return roll(v, self.zs, 1)

    def above(self, v):
        return roll(v, 128 - self.zs, 1)


def pair_sum(t, lv):
    lane = lanes()
    zs, ys = 1 << lv, 32 << lv
    t = t + jnp.where((lane & zs) == 0, roll(t, 128 - zs, 1), roll(t, zs, 1))
    return t + jnp.where((lane & ys) == 0, roll(t, 128 - ys, 1), roll(t, ys, 1))


def pack_faces(v, s, lv, out, t0):
    n = PLANES[lv]
    out[s, t0] = v[s, 0]
    out[s, t0 + 1] = v[s, n - 1]
    y0 = v[s, :, 0, :]
    y7 = v[s, :, 7, :]
    if lv == 0:
        lane = iota((32, 128), 1)
        p = jnp.where(lane >= 96, roll(y0, 96, 1), roll(y7, 32, 1))
        lane = iota((16, 128), 1)
        q = jnp.where((lane < 32) | (lane >= 96), p[:16], roll(p[16:], 64, 1))
    else:
        lane = iota((16, 128), 1)
        q = roll(jnp.where(lane < 64, y0, y7), 64, 1)
    out[s, t0 + 2] = q[:8]
    out[s, t0 + 3] = q[8:]


def pick(tab, own, near, far, s, f, tile):
    src = tab[s * 4 + f]
    at = tab[12 + s * 4 + f]
    return jnp.where(src == 0, own[at, tile], jnp.where(src == 1, near[at, tile], far[at, tile]))


def take_ghosts(tab, win, s, lv, t0, gx, gy):
    own, near, far = win
    gx[s, 0] = pick(tab, own, near, far, s, 0, t0 + 1)
    gx[s, 1] = pick(tab, own, near, far, s, 1, t0)
    low = lanes() < 64
    for t in range(2):
        sv = pick(tab, own, near, far, s, 2, t0 + 2 + t)
        nv = pick(tab, own, near, far, s, 3, t0 + 2 + t)
        gy[s, 8 * t : 8 * t + 8, :] = jnp.where(low, sv, nv)
        if lv == 0:
            gy[s, 16 + 8 * t : 24 + 8 * t, :] = roll(jnp.where(low, nv, sv), 64, 1)


def planes_loop(n, body, carry, unroll=8):
    def chunk(c, carry):
        for u in range(unroll):
            carry = body(c * unroll + u, carry, u == unroll - 1)
        return carry

    return lax.fori_loop(0, n // unroll, chunk, carry)


def following(ref, s, i, n, edge, at_end):
    if not at_end:
        return ref[s, i + 1]
    return jnp.where(i == n - 1, edge, ref[s, jnp.minimum(i + 1, n - 1)])


def make_weights(b, gx, gy, pres, lv, cx, cy, cz, wn, rd, extra):
    n = PLANES[lv]
    h = 0.5 * 0.25**lv
    tl = Tile(lv)
    first = []
    for s in range(SLOTS):
        v = b[s, 0]
        w = h * (v + gx[s, 0]) * pres[s * 4]
        cx[s, 0] = w
        first.append((v, w))

    def body(i, carry, at_end):
        out = []
        for s in range(SLOTS):
            v, w = carry[s]
            nxt = following(b, s, i, n, gx[s, 1], at_end)
            wnext = h * (v + nxt)
            if at_end:
                wnext = wnext * jnp.where(i == n - 1, pres[s * 4 + 1], 1.0)
            row = gy[s, pl.ds(i, 1), :]
            wy = h * (v + tl.south(v, row))
            wy = jnp.where(tl.south_edge, wy * pres[s * 4 + 2], wy)
            wrow = h * (v + row) * pres[s * 4 + 3]
            wz = jnp.where(tl.z_low, 0.0, h * (v + tl.below(v)))
            d = (w + wnext) + (wy + tl.north(wy, wrow)) + (wz + tl.above(wz))
            r = RELAXATION / d
            cx[s, i + 1] = wnext
            cy[s, i] = wy
            cz[s, i] = wz
            wn[s, pl.ds(i, 1), :] = wrow[7:8, :]
            rd[s, i] = r
            extra(s, i, r)
            out.append((nxt, wnext))
        return tuple(out)

    planes_loop(n, body, tuple(first))


def apply_level(v, gx, gy, lv, cx, cy, cz, wn, emit):
    n = PLANES[lv]
    tl = Tile(lv)
    first = []
    for s in range(SLOTS):
        v0 = v[s, 0]
        first.append((v0, cx[s, 0] * (v0 - gx[s, 0])))

    def body(i, carry, at_end):
        out = []
        for s in range(SLOTS):
            here, fx = carry[s]
            nxt = following(v, s, i, n, gx[s, 1], at_end)
            fnext = cx[s, i + 1] * (nxt - here)
            row = gy[s, pl.ds(i, 1), :]
            wrow = wn[s, pl.ds(i, 1), :]
            fy = cy[s, i] * (here - tl.south(here, row))
            fn = tl.north(fy, wrow * (row - here))
            fz = cz[s, i] * (here - tl.below(here))
            emit(s, i, here, (fx - fnext) + (fy - fn) + (fz - tl.above(fz)))
            out.append((nxt, fnext))
        return tuple(out)

    planes_loop(n, body, tuple(first))


def restrict_planes(v, s, lv, scale):
    out = []
    for c in range(PLANES[lv] // 2):
        out.append(pair_sum(v[s, 2 * c] + v[s, 2 * c + 1], lv) * scale)
    return out


def pack_bottom(planes, out):
    lane = lanes()
    at = (lane & 7) * 4
    part = lane >> 3
    top = None
    for s in range(2):
        for i in range(8):
            g = jnp.take_along_axis(planes[s][i], at, axis=1)
            top = g if top is None else jnp.where(part == s * 8 + i, g, top)
    low = None
    for i in range(8):
        g = jnp.take_along_axis(planes[2][i], at, axis=1)
        low = g if low is None else jnp.where((part & 7) == i, g, low)
    low = jnp.where(lane < 64, low, roll(low, 4, 0))
    out[0:8, :] = top
    out[8:12, :] = low[0:4]


def k_start(mask, src, inv, note, s_out, b_out, b1_out, faces, gathered):
    bottom = []
    for s in range(SLOTS):
        s_out[s] = src[:, s, :].reshape(32, 8, 128) * mask[s]
        b_out[s] = inv[:, s, :].reshape(32, 8, 128)
        for c, t in enumerate(restrict_planes(b_out, s, 0, 0.125)):
            b1_out[s, c] = t
        bottom.append(restrict_planes(b1_out, s, 1, 0.125))
        pack_faces(b_out, s, 0, faces, 0)
        pack_faces(b1_out, s, 1, faces, 4)
    pack_bottom(bottom, gathered)
    gathered[12:24, :] = jnp.zeros((12, 128), F32)
    gathered[12:13, :] = note[...]


def k_weights(tab, pres, s_in, b, b1, own, near, far, cx, cy, cz, wn, rd, u, cx1, cy1, cz1, wn1, rd1, faces, gx, gy, gx1, gy1):
    win = (own, near, far)
    for s in range(SLOTS):
        take_ghosts(tab, win, s, 0, 0, gx, gy)
        take_ghosts(tab, win, s, 1, 4, gx1, gy1)

    def first(s, i, r):
        u[s, i] = s_in[s, i] * r

    make_weights(b, gx, gy, pres, 0, cx, cy, cz, wn, rd, first)
    make_weights(b1, gx1, gy1, pres, 1, cx1, cy1, cz1, wn1, rd1, lambda s, i, r: None)
    for s in range(SLOTS):
        pack_faces(u, s, 0, faces, 0)


def k_sweep(lv, tab, t, u, own, near, far, cx, cy, cz, wn, rd, out, faces, gx, gy):
    for s in range(SLOTS):
        take_ghosts(tab, (own, near, far), s, lv, 0, gx, gy)

    def emit(s, i, here, av):
        out[s, i] = here + (t[s, i] - av) * rd[s, i]

    apply_level(u, gx, gy, lv, cx, cy, cz, wn, emit)
    for s in range(SLOTS):
        pack_faces(out, s, lv, faces, 0)


def k_down(tab, t, u, own, near, far, cx, cy, cz, wn, rd1, f1, u1, faces, gx, gy, res):
    for s in range(SLOTS):
        take_ghosts(tab, (own, near, far), s, 0, 0, gx, gy)

    def emit(s, i, here, av):
        res[s, i] = t[s, i] - av

    apply_level(u, gx, gy, 0, cx, cy, cz, wn, emit)
    for s in range(SLOTS):
        for c, p in enumerate(restrict_planes(res, s, 0, 0.125)):
            f1[s, c] = p
            u1[s, c] = p * rd1[s, c]
        pack_faces(u1, s, 1, faces, 0)


def k_bottom_rhs(tab, t, u, own, near, far, cx, cy, cz, wn, packed, gx, gy, res):
    for s in range(SLOTS):
        take_ghosts(tab, (own, near, far), s, 1, 0, gx, gy)

    def emit(s, i, here, av):
        res[s, i] = t[s, i] - av

    apply_level(u, gx, gy, 1, cx, cy, cz, wn, emit)
    pack_bottom([restrict_planes(res, s, 1, 0.125) for s in range(SLOTS)], packed)


def total(v):
    return jnp.sum(v, axis=(0, 1), keepdims=True)


def unpack_bottom(rows, put):
    for r in range(12):
        t = rows[:, r, :].T
        for half in range(2):
            s, j = (half, r) if r < 8 else (2, r - 8 + 4 * half)
            for i in range(8):
                put(s, j, i, t[half * 64 + i * 8 : half * 64 + i * 8 + 8, :])


def face_gather(v, dev_at, slot_at, place, s):
    out = jnp.take_along_axis(place(0), dev_at, axis=1)
    for other in range(1, SLOTS):
        g = jnp.take_along_axis(place(other), dev_at, axis=1)
        out = jnp.where(slot_at == other, g, out)
    return out


def k_bottom(tab, t, u, gx0, gy0, cx1, cy1, cz1, wn1, rd1, beta_rows, rhs_rows, out, faces, boxes_out,
             p, r, x, q, cx, cy, cz, back, sq, v1, gx, gy):
    note = beta_rows[:, 12, :].T
    at, slot, pres = [], [], []
    for f in range(12):
        gf = jnp.broadcast_to(note[f : f + 1, :], (8, 128))
        has = gf >= 0.0
        gf = jnp.where(has, gf, 0.0)
        dv = ((gf + 0.5) * (1.0 / 3.0)).astype(I32)
        at.append(dv)
        slot.append(gf.astype(I32) - 3 * dv)
        pres.append(jnp.where(has, 1.0, 0.0))
    counts = note[12:13, :]
    boxes = jnp.sum(counts, axis=1, keepdims=True)
    boxes_out[...] = jnp.broadcast_to(boxes, (8, 128))

    def fill_ghosts():
        def along(m, _):
            for s in range(SLOTS):
                for f, (src, dst) in enumerate(((7, 0), (0, 9))):
                    k = s * 4 + f
                    p[s, m + 1, dst] = face_gather(p, at[k], slot[k], lambda o: p[o, m + 1, src + 1], s)
                for f, (src, dst) in enumerate(((7, 0), (0, 9))):
                    k = s * 4 + 2 + f
                    p[s, dst, m + 1] = face_gather(p, at[k], slot[k], lambda o: p[o, src + 1, m + 1], s)
            return 0

        lax.fori_loop(0, 8, along, 0)

    def put_beta(s, j, i, tile):
        p[s, j + 1, i + 1] = tile

    unpack_bottom(beta_rows, put_beta)
    fill_ghosts()
    h = 0.5 * 0.0625
    low = subs() == 0

    def weights(m, _):
        for s in range(SLOTS):
            for i in range(9):
                w = h * (p[s, m + 1, i] + p[s, m + 1, i + 1])
                if i == 0:
                    w = w * pres[s * 4]
                if i == 8:
                    w = w * pres[s * 4 + 1]
                cx[s, m, i] = w
                w = h * (p[s, i, m + 1] + p[s, i + 1, m + 1])
                if i == 0:
                    w = w * pres[s * 4 + 2]
                if i == 8:
                    w = w * pres[s * 4 + 3]
                cy[s, i, m] = w
            for i in range(8):
                b = p[s, m + 1, i + 1]
                cz[s, m, i] = jnp.where(low, 0.0, h * (b + roll(b, 1, 0)))
        return 0

    lax.fori_loop(0, 8, weights, 0)

    def put_rhs(s, j, i, tile):
        r[s, j, i] = tile

    unpack_bottom(rhs_rows, put_rhs)

    def each(fn, init):
        def step(j, acc):
            for s in range(SLOTS):
                for i in range(8):
                    acc = fn(s, j, i, acc)
            return acc

        return lax.fori_loop(0, 8, step, init)

    zero = jnp.zeros((8, 128), F32)
    mean = total(each(lambda s, j, i, acc: acc + r[s, j, i], zero)) / (boxes * 512.0)
    valid = [jnp.where(jnp.broadcast_to(counts, (8, 128)) > s + 0.5, 1.0, 0.0) for s in range(SLOTS)]

    def shift(s, j, i, acc):
        v = (r[s, j, i] - mean) * valid[s]
        r[s, j, i] = v
        p[s, j + 1, i + 1] = v
        x[s, j, i] = zero
        return acc + v * v

    rr = total(each(shift, zero))

    def image(s, j, i, acc):
        here = p[s, j + 1, i + 1]
        a = cx[s, j, i] * (here - p[s, j + 1, i]) + cx[s, j, i + 1] * (here - p[s, j + 1, i + 2])
        b = cy[s, j, i] * (here - p[s, j, i + 1]) + cy[s, j + 1, i] * (here - p[s, j + 2, i + 1])
        fz = cz[s, j, i] * (here - roll(here, 1, 0))
        v = a + b + (fz - roll(fz, 7, 0))
        q[s, j, i] = v
        return acc + here * v

    def iteration(it, rr):
        fill_ghosts()
        alpha = rr / total(each(image, zero))

        def step(s, j, i, acc):
            x[s, j, i] = x[s, j, i] + alpha * p[s, j + 1, i + 1]
            v = r[s, j, i] - alpha * q[s, j, i]
            r[s, j, i] = v
            return acc + v * v

        rr_next = total(each(step, zero))
        ratio = rr_next / rr

        def turn(s, j, i, acc):
            p[s, j + 1, i + 1] = r[s, j, i] + ratio * p[s, j + 1, i + 1]
            return acc

        each(turn, 0)
        return rr_next

    rr = lax.fori_loop(0, BOTTOM_ITERS - 1, iteration, rr)
    fill_ghosts()
    alpha = rr / total(each(image, zero))

    def last(s, j, i, acc):
        x[s, j, i] = x[s, j, i] + alpha * p[s, j + 1, i + 1]
        return acc

    each(last, 0)

    for row in range(12):
        for half in range(2):
            s, j = (half, row) if row < 8 else (2, row - 8 + 4 * half)
            for i in range(8):
                sq[half * 64 + i * 8 : half * 64 + i * 8 + 8, :] = x[s, j, i]
        tr = sq[...].T
        if row < 8:
            back[:, row, :] = tr
            back[:, 8 + row, :] = roll(tr, 64, 1)
        else:
            back[:, 8 + row, :] = tr
            back[:, 12 + row, :] = roll(tr, 64, 1)

    lane, sub = lanes(), subs()
    kat = (lane & 31) >> 2

    def box(dev, s):
        return back[dev, pl.ds(pl.multiple_of(8 * s, 8), 8), :]

    for s in range(SLOTS):
        mine = box(tab[48], s)
        for i in range(8):
            g = jnp.take_along_axis(mine, kat + i * 8, axis=1)
            v1[s, 2 * i] = u[s, 2 * i] + g
            v1[s, 2 * i + 1] = u[s, 2 * i + 1] + g
        for f, i in ((0, 7), (1, 0)):
            nb = box(tab[24 + s * 4 + f], tab[36 + s * 4 + f])
            gx[s, f] = gx0[s, f] + jnp.take_along_axis(nb, kat + i * 8, axis=1)
        sb = jnp.broadcast_to(box(tab[24 + s * 4 + 2], tab[36 + s * 4 + 2])[7:8, :], (8, 128))
        nb = jnp.broadcast_to(box(tab[24 + s * 4 + 3], tab[36 + s * 4 + 3])[0:1, :], (8, 128))
        for part in range(2):
            idx = kat + (part * 4 + (sub >> 1)) * 8
            g = jnp.where(lane < 64, jnp.take_along_axis(sb, idx, axis=1), jnp.take_along_axis(nb, idx, axis=1))
            gy[s, 8 * part : 8 * part + 8, :] = gy0[s, 8 * part : 8 * part + 8, :] + g

    def emit(s, i, here, av):
        out[s, i] = here + (t[s, i] - av) * rd1[s, i]

    apply_level(v1, gx, gy, 1, cx1, cy1, cz1, wn1, emit)
    for s in range(SLOTS):
        pack_faces(out, s, 1, faces, 0)


def k_up(tab, t, u0, gx0, gy0, u1, own, near, far, cx, cy, cz, wn, rd, out, faces, v, gx, gy, gx1, gy1):
    for s in range(SLOTS):
        take_ghosts(tab, (own, near, far), s, 1, 0, gx1, gy1)
        for f in range(2):
            gx[s, f] = gx0[s, f] + gx1[s, f]
        for i in range(16):
            c = u1[s, i]
            v[s, 2 * i] = u0[s, 2 * i] + c
            v[s, 2 * i + 1] = u0[s, 2 * i + 1] + c
            gy[s, 2 * i : 2 * i + 2, :] = gy0[s, 2 * i : 2 * i + 2, :] + gy1[s, i : i + 1, :]

    def emit(s, i, here, av):
        out[s, i] = here + (t[s, i] - av) * rd[s, i]

    apply_level(v, gx, gy, 0, cx, cy, cz, wn, emit)
    for s in range(SLOTS):
        pack_faces(out, s, 0, faces, 0)


def k_residual(tab, t, u, own, near, far, cx, cy, cz, wn, res_out, sums, gx, gy, res):
    for s in range(SLOTS):
        take_ghosts(tab, (own, near, far), s, 0, 0, gx, gy)

    def emit(s, i, here, av):
        res[s, i] = t[s, i] - av

    apply_level(u, gx, gy, 0, cx, cy, cz, wn, emit)
    su = jnp.zeros((8, 128), F32)
    sr = jnp.zeros((8, 128), F32)
    for s in range(SLOTS):
        for i in range(32):
            w = res[s, i]
            sr = sr + w * w
            su = su + u[s, i]
        res_out[:, s, :] = res[s].reshape(256, 128)
    lane = iota((1, 128), 1)
    sums[...] = jnp.where(lane == 0, total(su), jnp.where(lane == 1, total(sr), 0.0))


def k_finish(mask, u, sums, boxes, corr, norm):
    tot = jnp.sum(sums[...], axis=0, keepdims=True)
    cells = boxes[0:1, 0:1] * 32768.0
    mean = tot[:, 0:1] / cells
    for s in range(SLOTS):
        corr[:, s, :] = ((u[s] - mean) * mask[s]).reshape(256, 128)
    norm[...] = jnp.broadcast_to(jnp.sqrt(tot[:, 1:2] / cells), (1, 128))


VMEM = pl.BlockSpec(memory_space=pltpu.VMEM)
SMEM = pl.BlockSpec(memory_space=pltpu.SMEM)


def call(kernel, smem, args, outs, scratch=(), vmem=24):
    shape = lambda s: jax.ShapeDtypeStruct(s, F32)
    return pl.pallas_call(
        kernel,
        out_shape=[shape(s) for s in outs],
        in_specs=[SMEM] * smem + [VMEM] * (len(args) - smem),
        out_specs=[VMEM] * len(outs),
        scratch_shapes=[pltpu.VMEM(s, F32) for s in scratch],
        compiler_params=pltpu.CompilerParams(vmem_limit_bytes=vmem * 1024 * 1024),
    )(*args)


def swapped(block, pairs):
    route = sorted([(a, b) for a, b in pairs] + [(b, a) for a, b in pairs])
    return lax.ppermute(block, AX, route)


def exchange(faces):
    tiles = faces.shape[1]
    got = [faces]
    for m in (1, 2, 3):
        got.append(swapped(faces, [(i, i ^ m) for i in range(DEVICES) if i < i ^ m]))
    own = jnp.concatenate(got, axis=0)
    sides = []
    for odd in (0, 1):
        pairs = [(i, i + 4) for i in range(DEVICES - 4) if (i // 4) % 2 == odd]
        sides.append(swapped(own, pairs))
    return own, sides[0], sides[1]


def to_all(rows):
    spread = jnp.broadcast_to(rows[None], (DEVICES,) + rows.shape)
    return lax.all_to_all(spread, AX, 0, 0)


def shards(source_term, inverse_density, box_counts, ghost_from):
    dev = lax.axis_index(AX).astype(I32)
    mask = (jnp.arange(SLOTS, dtype=I32) < box_counts[0]).astype(F32)
    flat = ghost_from.reshape(-1)
    present = flat >= 0
    pres = present.astype(F32)
    at = jnp.where(present, flat, dev * SLOTS)
    owner = at // SLOTS
    local = at - owner * SLOTS
    block = dev // 4
    ahead = owner // 4 - block
    even = (block & 1) == 0
    src = jnp.where(ahead == 0, 0, jnp.where((ahead == 1) == even, 1, 2))
    tab = jnp.concatenate(
        [src, ((owner & 3) ^ (dev & 3)) * SLOTS + local, owner, local, jnp.full((16,), dev)]
    ).astype(I32)
    note = jnp.concatenate([flat, box_counts, jnp.zeros((115,), I32)]).astype(F32).reshape(1, 128)

    view = lambda a: a.reshape(SLOTS, 256, 128).transpose(1, 0, 2)
    fine = (SLOTS, 32, 8, 128)
    mid = (SLOTS, 16, 8, 128)
    face = (SLOTS, 4, 8, 128)
    gx, gyf, gym = (SLOTS, 2, 8, 128), (SLOTS, 32, 128), (SLOTS, 16, 128)
    source, beta, beta1, faces, notes = call(
        k_start, 1, (mask, view(source_term), view(inverse_density), note),
        [fine, fine, mid, (SLOTS, 8, 8, 128), (24, 128)],
    )
    beta_rows = lax.all_gather(notes, AX)
    win = exchange(faces)
    cx, cy, cz, wn, rd, u, cx1, cy1, cz1, wn1, rd1, faces = call(
        k_weights, 2, (tab, pres, source, beta, beta1) + win,
        [(SLOTS, 33, 8, 128), fine, fine, gyf, fine, fine, (SLOTS, 17, 8, 128), mid, mid, gym, mid, face],
        [gx, gyf, gx, gym],
    )
    fine_w, mid_w = (cx, cy, cz, wn), (cx1, cy1, cz1, wn1)

    def sweep(lv, t, u, faces, w, d):
        return call(
            functools.partial(k_sweep, lv), 1, (tab, t, u) + exchange(faces) + w + (d,),
            [(fine, mid)[lv], face], [gx, (gyf, gym)[lv]],
        )

    u, faces = sweep(0, source, u, faces, fine_w, rd)
    f1, u1, faces, gx0, gy0 = call(
        k_down, 1, (tab, source, u) + exchange(faces) + fine_w + (rd1,), [mid, mid, face, gx, gyf], [fine],
    )
    u1, faces = sweep(1, f1, u1, faces, mid_w, rd1)
    rows, gx1, gy1 = call(
        k_bottom_rhs, 1, (tab, f1, u1) + exchange(faces) + mid_w, [(12, 128), gx, gym], [mid],
    )
    cube = (SLOTS, 8, 8, 8, 128)
    u1, faces, boxes = call(
        k_bottom, 1, (tab, f1, u1, gx1, gy1) + mid_w + (rd1, beta_rows, to_all(rows)), [mid, face, (8, 128)],
        [(SLOTS, 10, 10, 8, 128), cube, cube, cube, (SLOTS, 8, 9, 8, 128), (SLOTS, 9, 8, 8, 128), cube,
         (DEVICES, 24, 128), (128, 128), mid, gx, gym],
    )
    u1, faces = sweep(1, f1, u1, faces, mid_w, rd1)
    u, faces = call(
        k_up, 1, (tab, source, u, gx0, gy0, u1) + exchange(faces) + fine_w + (rd,), [fine, face],
        [fine, gx, gyf, gx, gym],
    )
    u, faces = sweep(0, source, u, faces, fine_w, rd)
    residual, sums = call(
        k_residual, 1, (tab, source, u) + exchange(faces) + fine_w, [(256, SLOTS, 128), (1, 128)], [gx, gyf, fine],
    )
    parts = to_all(sums).reshape(DEVICES, 128)
    correction, norm = call(k_finish, 1, (mask, u, parts, boxes), [(256, SLOTS, 128), (1, 128)])
    back = lambda a: a.transpose(1, 0, 2).reshape(SLOTS, 32768)
    return back(correction), back(residual), norm[0, 0]


def solution(mesh):
    rows = P(AX, None)
    return jax.shard_map(
        shards, mesh=mesh, in_specs=(rows, rows, P(AX), rows), out_specs=(rows, rows, P()), check_vma=False
    )
```

```python
import functools

import jax
import jax.numpy as jnp
from jax import lax
from jax.experimental import pallas as pl
from jax.experimental.pallas import tpu as pltpu
from jax.sharding import PartitionSpec as P

AX = ("gx", "gy")
DEVICES = 128
SLOTS = 3
BOTTOM_ITERS = 8
RELAXATION = 2.0 / 3.0
F32 = jnp.float32
I32 = jnp.int32

PLANES = (32, 16)


def iota(shape, dim):
    return lax.broadcasted_iota(I32, shape, dim)


def lanes():
    return iota((8, 128), 1)


def subs():
    return iota((8, 128), 0)


def roll(x, shift, axis):
    return pltpu.roll(x, shift, axis)


def lane_take(x, at):
    return jnp.take_along_axis(x, at, axis=1, mode="promise_in_bounds")


class Tile:
    def __init__(self, lv):
        self.zs, self.ys = 1 << lv, 32 << lv
        lane, sub = lanes(), subs()
        self.south_in = lane >= self.ys
        self.north_in = lane < 128 - self.ys
        self.first_row = sub == 0
        self.last_row = sub == 7
        self.south_edge = self.first_row & (lane < self.ys)
        self.z_low = (lane & 31) < self.zs

    def south(self, v, row):
        r = roll(v, self.ys, 1)
        return jnp.where(self.south_in, r, jnp.where(self.first_row, row, roll(r, 1, 0)))

    def north(self, v, edge):
        r = roll(v, 128 - self.ys, 1)
        return jnp.where(self.north_in, r, jnp.where(self.last_row, edge, roll(r, 7, 0)))

    def below(self, v):
        return roll(v, self.zs, 1)

    def above(self, v):
        return roll(v, 128 - self.zs, 1)


def pair_sum(t, lv):
    lane = lanes()
    zs, ys = 1 << lv, 32 << lv
    t = t + jnp.where((lane & zs) == 0, roll(t, 128 - zs, 1), roll(t, zs, 1))
    return t + jnp.where((lane & ys) == 0, roll(t, 128 - ys, 1), roll(t, ys, 1))


BOXES = 36
TWO_FACES = ((0, 2), (0, 3), (1, 2), (1, 3), (2, 0), (2, 1), (3, 0), (3, 1))


class Part:
    def __init__(self, lv, own=0, side=0):
        self.lv, self.own, self.side = lv, own, side
        self.tiles = (8, 3)[lv]
        self.ys = (4, 1)[lv]
        self.own_tiles = SLOTS * self.tiles
        self.side_tiles = (42, 18)[lv]


def pack_faces(v, s, part, out):
    lv = part.lv
    n = PLANES[lv]
    base = part.own + s * part.tiles
    planes = [v[s, 0], v[s, 1], v[s, n - 2], v[s, n - 1]]
    y0 = v[s, :, 0, :]
    y7 = v[s, :, 7, :]
    lane = iota((n, 128), 1)
    if lv == 0:
        for m in range(4):
            out[base + m] = planes[m]
        q = roll(jnp.where(lane >= 64, y7, y0), 64, 1)
    else:
        odd_k, odd_j = (lanes() & 1) == 1, (lanes() & 32) == 32
        out[base] = jnp.where(
            odd_k, jnp.where(odd_j, planes[3], planes[2]), jnp.where(odd_j, planes[1], planes[0])
        )
        q = jnp.where(
            lane < 32, y7, jnp.where(lane < 64, roll(y7, 96, 1), jnp.where(lane < 96, roll(y0, 64, 1), y0))
        )
    for t in range(n // 8):
        out[base + part.ys + t] = q[8 * t : 8 * t + 8]


def k_relay(parts, notes, par, *refs):
    got, (near, far) = refs[:4], refs[4:]
    even = par[0] == 1
    place = par[1]

    def of(m, t):
        low = jnp.where((m & 1) == 0, got[0][t], got[1][t])
        high = jnp.where((m & 1) == 0, got[2][t], got[3][t])
        return jnp.where(m < 2, low, high)

    def put(at, fwd, bwd):
        near[at] = jnp.where(even, fwd, bwd)
        far[at] = jnp.where(even, bwd, fwd)

    for part in parts:
        for s in range(SLOTS):
            base = part.own + s * part.tiles
            for m in range(4):
                box = m * SLOTS + s
                if part.lv == 0:
                    for x in range(2):
                        put(part.side + box * 2 + x, got[m][base + 2 + x], got[m][base + x])
                else:
                    put(part.side + box, got[m][base], got[m][base])
            if part.lv == 0:
                for x in range(2):
                    put(part.side + 24 + s * 6 + x, of(place ^ 3, base + x), of(place, base + 2 + x))
            for t in range(part.tiles - part.ys):
                at = part.side + (24 + s * 6 + 2 + t if part.lv == 0 else 12 + s * 2 + t)
                put(at, of(place ^ 3, base + part.ys + t), of(place, base + part.ys + t))
    if notes:
        own, side = notes
        for m in range(4):
            near[side + m] = got[m][own]
            far[side + m] = got[m][own]


def pick(tab, win, k, own, side):
    r = tab[k]
    low = jnp.where((r & 1) == 0, win[0][own], win[1][own])
    high = jnp.where((r & 1) == 0, win[2][own], win[3][own])
    beside = jnp.where((r & 1) == 0, win[4][side], win[5][side])
    return jnp.where(r < 4, jnp.where(r < 2, low, high), beside)


def pick_plane(tab, win, k, part, p):
    slot, m, delta = tab[BOXES + k], tab[2 * BOXES + k], tab[3 * BOXES + k]
    own = part.own + slot * part.tiles
    box = m * SLOTS + slot
    if part.lv == 0:
        x = p & 1
        direct = -1 if p >= 2 else 1
        side = part.side + jnp.where(delta == direct, box * 2 + x, 24 + slot * 6 + x)
        return pick(tab, win, k, own + p, side)
    lane = lanes()
    t = pick(tab, win, k, own, part.side + box)
    t = jnp.where(((lane & 1) == p >> 1) & ((lane & 32) == (p & 1) * 32), t, 0.0)
    return pair_sum(t, 0)


def pick_rows(tab, win, k, part, t):
    slot = tab[BOXES + k]
    own = part.own + slot * part.tiles + part.ys + t
    side = part.side + (24 + slot * 6 + 2 + t if part.lv == 0 else 12 + slot * 2 + t)
    return pick(tab, win, k, own, side)


def near_rows(y):
    lane = iota(y.shape, 1)
    return jnp.where(lane < 32, roll(y, 96, 1), jnp.where(lane < 96, y, roll(y, 32, 1)))


def take_ghosts(tab, win, part, xg, yg, ends):
    ys = 32 << part.lv
    low = iota((1, 128), 1) < 64
    for s in range(SLOTS):
        for g, (f, p) in enumerate(((0, 2), (0, 3), (1, 0), (1, 1))):
            xg[s, g] = pick_plane(tab, win, s * 4 + f, part, p)
        for t in range(part.tiles - part.ys):
            sv = pick_rows(tab, win, s * 4 + 2, part, t)
            nv = pick_rows(tab, win, s * 4 + 3, part, t)
            yg[s, 8 * t : 8 * t + 8, :] = jnp.where(lanes() < 64, sv, nv)

        def corner(q, p):
            return pick_plane(tab, win, 12 + s * 8 + q, part, p)

        for e, p in ((0, 3), (1, 0)):
            sp = corner(2 * e, p)[7:8]
            np = corner(2 * e + 1, p)[0:1]
            ends[s, e : e + 1, :] = jnp.where(low, roll(sp, ys, 1), roll(np, 128 - ys, 1))
            sp = corner(4 + e, p)[7:8]
            np = corner(6 + e, p)[0:1]
            ends[s, 2 + e : 3 + e, :] = jnp.where(low, roll(sp, 64, 1), roll(np, 64, 1))


def set_near(yg, gy, n):
    for s in range(SLOTS):
        for t in range(n // 8):
            gy[s, 8 * t : 8 * t + 8, :] = near_rows(yg[s, 8 * t : 8 * t + 8, :])


def planes_loop(n, body, carry, unroll=8):
    def chunk(c, carry):
        for u in range(unroll):
            carry = body(c * unroll + u, carry, u == unroll - 1)
        return carry

    return lax.fori_loop(0, n // unroll, chunk, carry)


def following(ref, s, i, n, edge, at_end):
    if not at_end:
        return ref[s, i + 1]
    return jnp.where(i == n - 1, edge, ref[s, jnp.minimum(i + 1, n - 1)])


def slab_sides(y, v, s, ends, n):
    lane = iota((n, 128), 1)
    row = iota((n, 128), 0)
    inner = jnp.where(lane < 64, roll(v[s, :, 0, :], 32, 1), roll(v[s, :, 7, :], 96, 1))
    outer = jnp.where(lane < 64, roll(y, 32, 1), roll(y, 96, 1))
    down = jnp.where(row == 0, ends[s, 2:3, :], roll(y, 1, 0))
    up = jnp.where(row == n - 1, ends[s, 3:4, :], roll(y, n - 1, 0))
    return outer, inner, down, up


def make_weights(b, xg, yg, ends, gy, tab, lv, w, extra):
    cx, cy, cz, wn, rd, slab = w
    n = PLANES[lv]
    h = 0.5 * 0.25**lv
    tl = Tile(lv)
    set_near(yg, gy, n)

    def has(k):
        return jnp.where(tab[4 * BOXES + k] == 1, 1.0, 0.0)

    def plane(s, i, here, w, nxt, wnext, row, south, north):
        wy = h * (here + tl.south(here, row))
        wy = jnp.where(tl.south_edge, wy * south, wy)
        wrow = h * (here + row) * north
        wz = jnp.where(tl.z_low, 0.0, h * (here + tl.below(here)))
        d = (w + wnext) + (wy + tl.north(wy, wrow)) + (wz + tl.above(wz))
        r = RELAXATION / d
        cx[s, i + 2] = wnext
        cy[s, i + 1] = wy
        cz[s, i + 1] = wz
        wn[s, pl.ds(i + 1, 1), :] = wrow[7:8, :]
        rd[s, i + 1] = r
        return r

    first = []
    for s in range(SLOTS):
        here, v = xg[s, 1], b[s, 0]
        w = h * (here + xg[s, 0])
        cx[s, 0] = w
        wnext = h * (here + v) * has(s * 4)
        plane(s, -1, here, w, v, wnext, ends[s, 0:1, :], has(12 + s * 8), has(13 + s * 8))
        first.append((v, wnext))

    def body(i, carry, at_end):
        out = []
        for s in range(SLOTS):
            v, w = carry[s]
            nxt = following(b, s, i, n, xg[s, 2], at_end)
            wnext = h * (v + nxt)
            if at_end:
                wnext = wnext * jnp.where(i == n - 1, has(s * 4 + 1), 1.0)
            r = plane(s, i, v, w, nxt, wnext, gy[s, pl.ds(i, 1), :], has(s * 4 + 2), has(s * 4 + 3))
            extra(s, i, r)
            out.append((nxt, wnext))
        return tuple(out)

    last = planes_loop(n, body, tuple(first))
    lane = iota((n, 128), 1)
    row = iota((n, 128), 0)
    for s in range(SLOTS):
        here, w = last[s]
        far = xg[s, 3]
        plane(s, n, here, w, far, h * (here + far), ends[s, 1:2, :], has(14 + s * 8), has(15 + s * 8))
        y = yg[s]
        outer, inner, down, up = (h * (y + t) for t in slab_sides(y, b, s, ends, n))
        k = 12 + s * 8
        down = down * jnp.where(row == 0, jnp.where(lane < 64, has(k + 4), has(k + 6)), 1.0)
        up = up * jnp.where(row == n - 1, jnp.where(lane < 64, has(k + 5), has(k + 7)), 1.0)
        zs = tl.zs
        wz = jnp.where((lane & 31) < zs, 0.0, h * (y + roll(y, zs, 1)))
        d = (outer + inner) + (down + up) + (wz + roll(wz, 128 - zs, 1))
        for m, t in enumerate((outer, inner, down, up, wz, RELAXATION / d)):
            slab[s, m] = t


def apply_level(v, before, after, gy, ends, lv, w, emit, wide=None):
    cx, cy, cz, wn = w[:4]
    n = PLANES[lv]
    tl = Tile(lv)

    def plane(s, i, here, fx, nxt, row):
        fnext = cx[s, i + 2] * (nxt - here)
        wrow = wn[s, pl.ds(i + 1, 1), :]
        fy = cy[s, i + 1] * (here - tl.south(here, row))
        fn = tl.north(fy, wrow * (row - here))
        fz = cz[s, i + 1] * (here - tl.below(here))
        return (fx - fnext) + (fy - fn) + (fz - tl.above(fz)), fnext

    first = []
    for s in range(SLOTS):
        v0, west = v[s, 0], before(s, 0)
        if wide:
            fx = cx[s, 0] * (west - before(s, 1))
            av, fx = plane(s, -1, west, fx, v0, ends[s, 0:1, :])
            wide(s, 0, west, av)
        else:
            fx = cx[s, 1] * (v0 - west)
        first.append((v0, fx))

    def body(i, carry, at_end):
        out = []
        for s in range(SLOTS):
            here, fx = carry[s]
            nxt = following(v, s, i, n, after(s, 0), at_end)
            av, fnext = plane(s, i, here, fx, nxt, gy[s, pl.ds(i, 1), :])
            emit(s, i, here, av)
            out.append((nxt, fnext))
        return tuple(out)

    last = planes_loop(n, body, tuple(first))
    if wide:
        for s in range(SLOTS):
            here, fx = last[s]
            av, fx = plane(s, n, here, fx, after(s, 1), ends[s, 1:2, :])
            wide(s, 1, here, av)


def apply_slab(yg, v, s, ends, lv, slab):
    n = PLANES[lv]
    zs = 1 << lv
    y = yg[s]
    outer, inner, down, up = slab_sides(y, v, s, ends, n)
    fz = slab[s, 4] * (y - roll(y, zs, 1))
    a = slab[s, 0] * (y - outer) + slab[s, 1] * (y - inner)
    b = slab[s, 2] * (y - down) + slab[s, 3] * (y - up)
    return y, a + b + (fz - roll(fz, 128 - zs, 1))


def sweep_wide(v, xg, yg, ends, gy, lv, w, first, first_x, first_y, out, out_x, out_y):
    rd, slab = w[4:]
    n = PLANES[lv]
    set_near(yg, gy, n)

    def emit(s, i, here, av):
        out[s, i] = here + (first[s, i] - av * rd[s, i + 1])

    def wide(s, e, here, av):
        out_x[s, e] = here + (first_x(s, e) - av * rd[s, (n + 1) * e])

    apply_level(v, lambda s, g: xg[s, 1 - g], lambda s, g: xg[s, 2 + g], gy, ends, lv, w, emit, wide)
    for s in range(SLOTS):
        y, a = apply_slab(yg, v, s, ends, lv, slab)
        out_y[s] = y + (first_y(s) - a * slab[s, 5])


def apply_near(v, gx, yg, gy, lv, w, emit):
    set_near(yg, gy, PLANES[lv])
    apply_level(v, lambda s, g: gx[s, 0], lambda s, g: gx[s, 1], gy, None, lv, w, emit)


def restrict_planes(v, s, lv, scale):
    out = []
    for c in range(PLANES[lv] // 2):
        out.append(pair_sum(v[s, 2 * c] + v[s, 2 * c + 1], lv) * scale)
    return out


def pack_bottom(planes, out):
    lane = lanes()
    at = (lane & 7) * 4
    part = lane >> 3
    top = None
    for s in range(2):
        for i in range(8):
            g = lane_take(planes[s][i], at)
            top = g if top is None else jnp.where(part == s * 8 + i, g, top)
    low = None
    for i in range(8):
        g = lane_take(planes[2][i], at)
        low = g if low is None else jnp.where((part & 7) == i, g, low)
    low = jnp.where(lane < 64, low, roll(low, 4, 0))
    out[0:8, :] = top
    out[8:12, :] = low[0:4]


PART0, PART1 = Part(0), Part(1)
FIRST = (Part(0), Part(1, 24, 42))
FIRST_NOTES = (33, 60)


def k_start(mask, src, inv, note, codes, s_out, b_out, b1_out, faces, gathered):
    bottom = []
    for s in range(SLOTS):
        s_out[s] = src[:, s, :].reshape(32, 8, 128) * mask[s]
        b_out[s] = inv[:, s, :].reshape(32, 8, 128)
        for c, t in enumerate(restrict_planes(b_out, s, 0, 0.125)):
            b1_out[s, c] = t
        bottom.append(restrict_planes(b1_out, s, 1, 0.125))
        pack_faces(b_out, s, FIRST[0], faces)
        pack_faces(b1_out, s, FIRST[1], faces)
    faces[FIRST_NOTES[0]] = jnp.broadcast_to(codes[...], (8, 128))
    pack_bottom(bottom, gathered)
    gathered[12:24, :] = jnp.zeros((12, 128), F32)
    gathered[12:13, :] = note[...]


def fill_table(par, notes, tab):
    even, place, block = par[0], par[1], par[2]

    def entry(k, code):
        owner = code >> 2
        delta = jnp.where(code >= 0, (owner >> 2) - block, 0)
        m = jnp.where(code >= 0, (owner & 3) ^ place, 0)
        slot = jnp.where(code >= 0, code & 3, 0)
        r = jnp.where(delta == 0, m, jnp.where(delta == 2 * even - 1, 4, 5))
        for x, value in enumerate((r, slot, m, delta, jnp.where(code >= 0, 1, 0))):
            tab[x * BOXES + k] = value
        return (jnp.where(r < 4, 0, r - 3) * 4 + m) * 12 + slot * 4

    for s in range(SLOTS):
        codes = [notes[s * 4 + f] for f in range(4)]
        rows = [entry(s * 4 + f, codes[f]) for f in range(4)]
        for q, (f, g) in enumerate(TWO_FACES):
            entry(12 + s * 8 + q, jnp.where(codes[f] >= 0, notes[rows[f] + g], -1))


def k_weights(par, notes, s_in, b, b1, *refs):
    win, refs = refs[:6], refs[6:]
    w, u, w1, faces, tab, (xg, yg, ends, gy, xg1, yg1, ends1, gy1) = (
        refs[:6], refs[6], refs[7:13], refs[13], refs[14], refs[15:]
    )
    fill_table(par, notes, tab)
    take_ghosts(tab, win, FIRST[0], xg, yg, ends)
    take_ghosts(tab, win, FIRST[1], xg1, yg1, ends1)

    def first(s, i, r):
        u[s, i] = s_in[s, i] * r

    make_weights(b, xg, yg, ends, gy, tab, 0, w, first)
    make_weights(b1, xg1, yg1, ends1, gy1, tab, 1, w1, lambda s, i, r: None)
    for s in range(SLOTS):
        pack_faces(u, s, PART0, faces)


def k_down(tab, t, u, *refs):
    win, w, rd1 = refs[:6], refs[6:12], refs[12]
    out, out_x, out_y, first_x, first_y, f1, u1, faces, xg, yg, ends, gy, res = refs[13:]
    take_ghosts(tab, win, PART0, xg, yg, ends)
    for s in range(SLOTS):
        for e in range(2):
            first_x[s, e] = xg[s, 1 + e]
        first_y[s] = yg[s]
    sweep_wide(u, xg, yg, ends, gy, 0, w, u, lambda s, e: xg[s, 1 + e], lambda s: yg[s], out, out_x, out_y)

    def emit(s, i, here, av):
        res[s, i] = t[s, i] - av

    apply_near(out, out_x, out_y, gy, 0, w, emit)
    for s in range(SLOTS):
        for c, p in enumerate(restrict_planes(res, s, 0, 0.125)):
            f1[s, c] = p
            u1[s, c] = p * rd1[s, c + 1]
        pack_faces(u1, s, PART1, faces)


def k_bottom_rhs(tab, t, u, *refs):
    win, w = refs[:6], refs[6:12]
    out, out_x, out_y, first_x, first_y, packed, xg, yg, ends, gy, res = refs[12:]
    take_ghosts(tab, win, PART1, xg, yg, ends)
    for s in range(SLOTS):
        for e in range(2):
            first_x[s, e] = xg[s, 1 + e]
        first_y[s] = yg[s]
    sweep_wide(u, xg, yg, ends, gy, 1, w, u, lambda s, e: xg[s, 1 + e], lambda s: yg[s], out, out_x, out_y)

    def emit(s, i, here, av):
        res[s, i] = t[s, i] - av

    apply_near(out, out_x, out_y, gy, 1, w, emit)
    pack_bottom([restrict_planes(res, s, 1, 0.125) for s in range(SLOTS)], packed)


def total(v):
    return jnp.sum(v, axis=(0, 1), keepdims=True)


def unpack_bottom(rows, put):
    for r in range(12):
        t = rows[:, r, :].T
        for half in range(2):
            s, j = (half, r) if r < 8 else (2, r - 8 + 4 * half)
            for i in range(8):
                put(s, j, i, t[half * 64 + i * 8 : half * 64 + i * 8 + 8, :])


def face_gather(v, dev_at, slot_at, place, s):
    out = lane_take(place(0), dev_at)
    for other in range(1, SLOTS):
        g = lane_take(place(other), dev_at)
        out = jnp.where(slot_at == other, g, out)
    return out


def k_bottom(place, first, u, gx0, gy0, *refs):
    w1, (beta_rows, rhs_rows) = refs[:6], refs[6:8]
    out, faces, boxes_out, p, r, x, q, cx, cy, cz, back, sq, v1, gx, yg, gy = refs[8:]
    note = beta_rows[:, 12, :].T
    at, slot, pres = [], [], []
    for f in range(12):
        gf = jnp.broadcast_to(note[f : f + 1, :], (8, 128))
        has = gf >= 0.0
        gf = jnp.where(has, gf, 0.0)
        dv = ((gf + 0.5) * (1.0 / 3.0)).astype(I32)
        at.append(dv)
        slot.append(gf.astype(I32) - 3 * dv)
        pres.append(jnp.where(has, 1.0, 0.0))
    counts = note[12:13, :]
    boxes = jnp.sum(counts, axis=1, keepdims=True)
    boxes_out[...] = jnp.broadcast_to(boxes, (8, 128))

    def fill_ghosts():
        def along(m, _):
            for s in range(SLOTS):
                for f, (src, dst) in enumerate(((7, 0), (0, 9))):
                    k = s * 4 + f
                    p[s, m + 1, dst] = face_gather(p, at[k], slot[k], lambda o: p[o, m + 1, src + 1], s)
                for f, (src, dst) in enumerate(((7, 0), (0, 9))):
                    k = s * 4 + 2 + f
                    p[s, dst, m + 1] = face_gather(p, at[k], slot[k], lambda o: p[o, src + 1, m + 1], s)
            return 0

        lax.fori_loop(0, 8, along, 0)

    def put_beta(s, j, i, tile):
        p[s, j + 1, i + 1] = tile

    unpack_bottom(beta_rows, put_beta)
    fill_ghosts()
    h = 0.5 * 0.0625
    low = subs() == 0

    def weights(m, _):
        for s in range(SLOTS):
            for i in range(9):
                w = h * (p[s, m + 1, i] + p[s, m + 1, i + 1])
                if i == 0:
                    w = w * pres[s * 4]
                if i == 8:
                    w = w * pres[s * 4 + 1]
                cx[s, m, i] = w
                w = h * (p[s, i, m + 1] + p[s, i + 1, m + 1])
                if i == 0:
                    w = w * pres[s * 4 + 2]
                if i == 8:
                    w = w * pres[s * 4 + 3]
                cy[s, i, m] = w
            for i in range(8):
                b = p[s, m + 1, i + 1]
                cz[s, m, i] = jnp.where(low, 0.0, h * (b + roll(b, 1, 0)))
        return 0

    lax.fori_loop(0, 8, weights, 0)

    def put_rhs(s, j, i, tile):
        r[s, j, i] = tile

    unpack_bottom(rhs_rows, put_rhs)

    def each(fn, init):
        def step(j, acc):
            for s in range(SLOTS):
                for i in range(8):
                    acc = fn(s, j, i, acc)
            return acc

        return lax.fori_loop(0, 8, step, init)

    zero = jnp.zeros((8, 128), F32)
    mean = total(each(lambda s, j, i, acc: acc + r[s, j, i], zero)) / (boxes * 512.0)
    valid = [jnp.where(jnp.broadcast_to(counts, (8, 128)) > s + 0.5, 1.0, 0.0) for s in range(SLOTS)]

    def shift(s, j, i, acc):
        v = (r[s, j, i] - mean) * valid[s]
        r[s, j, i] = v
        p[s, j + 1, i + 1] = v
        x[s, j, i] = zero
        return acc + v * v

    rr = total(each(shift, zero))

    def image(s, j, i, acc):
        here = p[s, j + 1, i + 1]
        a = cx[s, j, i] * (here - p[s, j + 1, i]) + cx[s, j, i + 1] * (here - p[s, j + 1, i + 2])
        b = cy[s, j, i] * (here - p[s, j, i + 1]) + cy[s, j + 1, i] * (here - p[s, j + 2, i + 1])
        fz = cz[s, j, i] * (here - roll(here, 1, 0))
        v = a + b + (fz - roll(fz, 7, 0))
        q[s, j, i] = v
        return acc + here * v

    def iteration(it, rr):
        fill_ghosts()
        alpha = rr / total(each(image, zero))

        def step(s, j, i, acc):
            x[s, j, i] = x[s, j, i] + alpha * p[s, j + 1, i + 1]
            v = r[s, j, i] - alpha * q[s, j, i]
            r[s, j, i] = v
            return acc + v * v

        rr_next = total(each(step, zero))
        ratio = rr_next / rr

        def turn(s, j, i, acc):
            p[s, j + 1, i + 1] = r[s, j, i] + ratio * p[s, j + 1, i + 1]
            return acc

        each(turn, 0)
        return rr_next

    rr = lax.fori_loop(0, BOTTOM_ITERS - 1, iteration, rr)
    fill_ghosts()
    alpha = rr / total(each(image, zero))

    def last(s, j, i, acc):
        x[s, j, i] = x[s, j, i] + alpha * p[s, j + 1, i + 1]
        return acc

    each(last, 0)

    for row in range(12):
        for half in range(2):
            s, j = (half, row) if row < 8 else (2, row - 8 + 4 * half)
            for i in range(8):
                sq[half * 64 + i * 8 : half * 64 + i * 8 + 8, :] = x[s, j, i]
        tr = sq[...].T
        if row < 8:
            back[:, row, :] = tr
            back[:, 8 + row, :] = roll(tr, 64, 1)
        else:
            back[:, 8 + row, :] = tr
            back[:, 12 + row, :] = roll(tr, 64, 1)

    lane, sub = lanes(), subs()
    kat = (lane & 31) >> 2

    def box(dev, s):
        return back[dev, pl.ds(pl.multiple_of(8 * s, 8), 8), :]

    for s in range(SLOTS):
        mine = box(place[24], s)
        for i in range(8):
            g = lane_take(mine, kat + i * 8)
            v1[s, 2 * i] = u[s, 2 * i] + g
            v1[s, 2 * i + 1] = u[s, 2 * i + 1] + g
        near = [box(place[s * 4 + f], place[12 + s * 4 + f]) for f in range(4)]
        for f, i in ((0, 7), (1, 0)):
            gx[s, f] = gx0[s, f] + lane_take(near[f], kat + i * 8)
        sb = jnp.broadcast_to(near[2][7:8, :], (8, 128))
        nb = jnp.broadcast_to(near[3][0:1, :], (8, 128))
        for part in range(2):
            idx = kat + (part * 4 + (sub >> 1)) * 8
            g = jnp.where(lane < 64, lane_take(sb, idx), lane_take(nb, idx))
            yg[s, 8 * part : 8 * part + 8, :] = gy0[s, 8 * part : 8 * part + 8, :] + g

    def emit(s, i, here, av):
        out[s, i] = here + (first[s, i] - av * w1[4][s, i + 1])

    apply_near(v1, gx, yg, gy, 1, w1, emit)
    for s in range(SLOTS):
        pack_faces(out, s, PART1, faces)


def k_up(tab, first1, first1_x, first1_y, u1, first, u0, u0_x, u0_y, *refs):
    win, w1, w = refs[:6], refs[6:12], refs[12:18]
    out, faces, c, c_x, c_y, xg, yg, ends, gy1, v, gx, y0, gy = refs[18:]
    take_ghosts(tab, win, PART1, xg, yg, ends)
    sweep_wide(u1, xg, yg, ends, gy1, 1, w1, first1, lambda s, e: first1_x[s, e], lambda s: first1_y[s], c, c_x, c_y)
    for s in range(SLOTS):
        for f in range(2):
            gx[s, f] = u0_x[s, f] + c_x[s, f]
        for i in range(16):
            t = c[s, i]
            v[s, 2 * i] = u0[s, 2 * i] + t
            v[s, 2 * i + 1] = u0[s, 2 * i + 1] + t
            y0[s, 2 * i : 2 * i + 2, :] = u0_y[s, 2 * i : 2 * i + 2, :] + c_y[s, i : i + 1, :]

    def emit(s, i, here, av):
        out[s, i] = here + (first[s, i] - av * w[4][s, i + 1])

    apply_near(v, gx, y0, gy, 0, w, emit)
    for s in range(SLOTS):
        pack_faces(out, s, PART0, faces)


def k_residual(tab, t, u, first, first_x, first_y, *refs):
    win, w = refs[:6], refs[6:12]
    out, res_out, sums, out_x, out_y, xg, yg, ends, gy, res = refs[12:]
    take_ghosts(tab, win, PART0, xg, yg, ends)
    sweep_wide(u, xg, yg, ends, gy, 0, w, first, lambda s, e: first_x[s, e], lambda s: first_y[s], out, out_x, out_y)

    def emit(s, i, here, av):
        res[s, i] = t[s, i] - av

    apply_near(out, out_x, out_y, gy, 0, w, emit)
    su = jnp.zeros((8, 128), F32)
    sr = jnp.zeros((8, 128), F32)
    for s in range(SLOTS):
        for i in range(32):
            d = res[s, i]
            sr = sr + d * d
            su = su + out[s, i]
        res_out[:, s, :] = res[s].reshape(256, 128)
    lane = iota((1, 128), 1)
    sums[...] = jnp.where(lane == 0, total(su), jnp.where(lane == 1, total(sr), 0.0))


def k_finish(mask, u, sums, boxes, corr, norm):
    tot = jnp.sum(sums[...], axis=0, keepdims=True)
    cells = boxes[0:1, 0:1] * 32768.0
    mean = tot[:, 0:1] / cells
    for s in range(SLOTS):
        corr[:, s, :] = ((u[s] - mean) * mask[s]).reshape(256, 128)
    norm[...] = jnp.broadcast_to(jnp.sqrt(tot[:, 1:2] / cells), (1, 128))


VMEM = pl.BlockSpec(memory_space=pltpu.VMEM)
SMEM = pl.BlockSpec(memory_space=pltpu.SMEM)


def call(kernel, smem, args, outs, scratch=(), vmem=24, tables=()):
    shape = lambda s: jax.ShapeDtypeStruct(s, F32)
    return pl.pallas_call(
        kernel,
        out_shape=[shape(s) for s in outs] + [jax.ShapeDtypeStruct(s, I32) for s in tables],
        in_specs=[SMEM] * smem + [VMEM] * (len(args) - smem),
        out_specs=[VMEM] * len(outs) + [SMEM] * len(tables),
        scratch_shapes=[pltpu.VMEM(s, F32) for s in scratch],
        compiler_params=pltpu.CompilerParams(vmem_limit_bytes=vmem * 1024 * 1024),
    )(*args)


def swapped(block, pairs):
    route = sorted([(a, b) for a, b in pairs] + [(b, a) for a, b in pairs])
    return lax.ppermute(block, AX, route)


def exchange(par, faces, parts, notes=()):
    got = [faces]
    for m in (1, 2, 3):
        got.append(swapped(faces, [(i, i ^ m) for i in range(DEVICES) if i < i ^ m]))
    tiles = parts[-1].side + parts[-1].side_tiles + (4 if notes else 0)
    sides = call(functools.partial(k_relay, parts, notes), 1, (par, *got), [(tiles, 8, 128)] * 2)
    for odd in (0, 1):
        pairs = [(i, i + 4) for i in range(DEVICES - 4) if (i // 4) % 2 == odd]
        got.append(swapped(sides[odd], pairs))
    return tuple(got)


def to_all(rows):
    spread = jnp.broadcast_to(rows[None], (DEVICES,) + rows.shape)
    return lax.all_to_all(spread, AX, 0, 0)


def shards(source_term, inverse_density, box_counts, ghost_from):
    dev = lax.axis_index(AX).astype(I32)
    mask = (jnp.arange(SLOTS, dtype=I32) < box_counts[0]).astype(F32)
    flat = ghost_from.reshape(-1)
    present = flat >= 0
    at = jnp.where(present, flat, dev * SLOTS)
    owner = at // SLOTS
    local = at - owner * SLOTS
    place = jnp.concatenate([owner, local, jnp.full((8,), dev)]).astype(I32)
    par = jnp.stack([1 - ((dev >> 2) & 1), dev & 3, dev >> 2])
    row = lambda a: jnp.concatenate([a, jnp.zeros((128 - a.shape[0],), I32)]).astype(F32).reshape(1, 128)
    note = row(jnp.concatenate([flat, box_counts]))
    codes = row(jnp.where(present, owner * 4 + local, -1))

    view = lambda a: a.reshape(SLOTS, 256, 128).transpose(1, 0, 2)
    fine, mid = (SLOTS, 32, 8, 128), (SLOTS, 16, 8, 128)
    gx, xg, ends = (SLOTS, 2, 8, 128), (SLOTS, 4, 8, 128), (SLOTS, 8, 128)
    gyf, gym = (SLOTS, 32, 128), (SLOTS, 16, 128)
    face0, face1 = (PART0.own_tiles, 8, 128), (PART1.own_tiles, 8, 128)

    def weight_shapes(n):
        wide = (SLOTS, n + 2, 8, 128)
        return [(SLOTS, n + 3, 8, 128), wide, wide, (SLOTS, n + 2, 128), wide, (SLOTS, 6, n, 128)]

    source, beta, beta1, faces, notes = call(
        k_start, 1, (mask, view(source_term), view(inverse_density), note, codes),
        [fine, fine, mid, (FIRST_NOTES[0] + 1, 8, 128), (24, 128)],
    )
    beta_rows = lax.all_gather(notes, AX)
    win = exchange(par, faces, FIRST, FIRST_NOTES)
    own, side = FIRST_NOTES
    codes = jnp.concatenate([a[own : own + 1, 0, :12] for a in win[:4]] + [a[side:, 0, :12] for a in win[4:]])
    outs = call(
        k_weights, 2, (par, codes.reshape(-1).astype(I32), source, beta, beta1) + win,
        weight_shapes(32) + [fine] + weight_shapes(16) + [face0],
        [xg, gyf, ends, gyf, xg, gym, ends, gym], tables=[(5 * BOXES,)],
    )
    w, first, w1, faces, tab = tuple(outs[:6]), outs[6], tuple(outs[7:13]), outs[13], outs[14]
    u, u_x, u_y, first_x, first_y, f1, first1, faces = call(
        k_down, 1, (tab, source, first) + exchange(par, faces, [PART0]) + w + (w1[4],),
        [fine, gx, gyf, gx, gyf, mid, mid, face1], [xg, gyf, ends, gyf, fine],
    )
    u1, u1_x, u1_y, first1_x, first1_y, rows = call(
        k_bottom_rhs, 1, (tab, f1, first1) + exchange(par, faces, [PART1]) + w1,
        [mid, gx, gym, gx, gym, (12, 128)], [xg, gym, ends, gym, mid],
    )
    cube = (SLOTS, 8, 8, 8, 128)
    u1, faces, boxes = call(
        k_bottom, 1, (place, first1, u1, u1_x, u1_y) + w1 + (beta_rows, to_all(rows)), [mid, face1, (8, 128)],
        [(SLOTS, 10, 10, 8, 128), cube, cube, cube, (SLOTS, 8, 9, 8, 128), (SLOTS, 9, 8, 8, 128), cube,
         (DEVICES, 24, 128), (128, 128), mid, gx, gym, gym],
    )
    u, faces = call(
        k_up, 1,
        (tab, first1, first1_x, first1_y, u1, first, u, u_x, u_y) + exchange(par, faces, [PART1]) + w1 + w,
        [fine, face0], [mid, gx, gym, xg, gym, ends, gym, fine, gx, gyf, gyf],
    )
    u, residual, sums = call(
        k_residual, 1, (tab, source, u, first, first_x, first_y) + exchange(par, faces, [PART0]) + w,
        [fine, (256, SLOTS, 128), (1, 128)], [gx, gyf, xg, gyf, ends, gyf, fine],
    )
    parts = to_all(sums).reshape(DEVICES, 128)
    correction, norm = call(k_finish, 1, (mask, u, parts, boxes), [(256, SLOTS, 128), (1, 128)])
    back = lambda a: a.transpose(1, 0, 2).reshape(SLOTS, 32768)
    return back(correction), back(residual), norm[0, 0]


def solution(mesh):
    rows = P(AX, None)
    return jax.shard_map(
        shards, mesh=mesh, in_specs=(rows, rows, P(AX), rows), out_specs=(rows, rows, P()), check_vma=False
    )
```

```python
import functools

import jax
import jax.numpy as jnp
from jax import lax
from jax.experimental import pallas as pl
from jax.experimental.pallas import tpu as pltpu
from jax.sharding import PartitionSpec as P

AX = ("gx", "gy")
DEVICES = 128
SLOTS = 3
BOTTOM_ITERS = 8
RELAXATION = 2.0 / 3.0
F32 = jnp.float32
I32 = jnp.int32

PLANES = (32, 16)


def iota(shape, dim):
    return lax.broadcasted_iota(I32, shape, dim)


def lanes():
    return iota((8, 128), 1)


def subs():
    return iota((8, 128), 0)


def roll(x, shift, axis):
    return pltpu.roll(x, shift, axis)


def lane_take(x, at):
    return jnp.take_along_axis(x, at, axis=1, mode="promise_in_bounds")


class Tile:
    def __init__(self, lv):
        self.zs, self.ys = 1 << lv, 32 << lv
        lane, sub = lanes(), subs()
        self.south_in = lane >= self.ys
        self.north_in = lane < 128 - self.ys
        self.first_row = sub == 0
        self.last_row = sub == 7
        self.south_edge = self.first_row & (lane < self.ys)
        self.z_low = (lane & 31) < self.zs

    def south(self, v, row):
        r = roll(v, self.ys, 1)
        return jnp.where(self.south_in, r, jnp.where(self.first_row, row, roll(r, 1, 0)))

    def north(self, v, edge):
        r = roll(v, 128 - self.ys, 1)
        return jnp.where(self.north_in, r, jnp.where(self.last_row, edge, roll(r, 7, 0)))

    def below(self, v):
        return roll(v, self.zs, 1)

    def above(self, v):
        return roll(v, 128 - self.zs, 1)


def pair_sum(t, lv):
    lane = lanes()
    zs, ys = 1 << lv, 32 << lv
    t = t + jnp.where((lane & zs) == 0, roll(t, 128 - zs, 1), roll(t, zs, 1))
    return t + jnp.where((lane & ys) == 0, roll(t, 128 - ys, 1), roll(t, ys, 1))


BOXES = 36
TWO_FACES = ((0, 2), (0, 3), (1, 2), (1, 3), (2, 0), (2, 1), (3, 0), (3, 1))


class Part:
    def __init__(self, lv, own=0, side=0):
        self.lv, self.own, self.side = lv, own, side
        self.tiles = (8, 3)[lv]
        self.ys = (4, 1)[lv]
        self.own_tiles = SLOTS * self.tiles
        self.side_tiles = (42, 18)[lv]


def pack_faces(v, s, part, out):
    lv = part.lv
    n = PLANES[lv]
    base = part.own + s * part.tiles
    planes = [v[s, 0], v[s, 1], v[s, n - 2], v[s, n - 1]]
    y0 = v[s, :, 0, :]
    y7 = v[s, :, 7, :]
    lane = iota((n, 128), 1)
    if lv == 0:
        for m in range(4):
            out[base + m] = planes[m]
        q = roll(jnp.where(lane >= 64, y7, y0), 64, 1)
    else:
        odd_k, odd_j = (lanes() & 1) == 1, (lanes() & 32) == 32
        out[base] = jnp.where(
            odd_k, jnp.where(odd_j, planes[3], planes[2]), jnp.where(odd_j, planes[1], planes[0])
        )
        q = jnp.where(
            lane < 32, y7, jnp.where(lane < 64, roll(y7, 96, 1), jnp.where(lane < 96, roll(y0, 64, 1), y0))
        )
    for t in range(n // 8):
        out[base + part.ys + t] = q[8 * t : 8 * t + 8]


def k_relay(parts, notes, *refs):
    got, (near, far) = refs[:4], refs[4:]
    _, even, place, _ = place_of_device()
    even = even == 1

    def of(m, t):
        low = jnp.where((m & 1) == 0, got[0][t], got[1][t])
        high = jnp.where((m & 1) == 0, got[2][t], got[3][t])
        return jnp.where(m < 2, low, high)

    def put(at, fwd, bwd):
        near[at] = jnp.where(even, fwd, bwd)
        far[at] = jnp.where(even, bwd, fwd)

    for part in parts:
        for s in range(SLOTS):
            base = part.own + s * part.tiles
            for m in range(4):
                box = m * SLOTS + s
                if part.lv == 0:
                    for x in range(2):
                        put(part.side + box * 2 + x, got[m][base + 2 + x], got[m][base + x])
                else:
                    put(part.side + box, got[m][base], got[m][base])
            if part.lv == 0:
                for x in range(2):
                    put(part.side + 24 + s * 6 + x, of(place ^ 3, base + x), of(place, base + 2 + x))
            for t in range(part.tiles - part.ys):
                at = part.side + (24 + s * 6 + 2 + t if part.lv == 0 else 12 + s * 2 + t)
                put(at, of(place ^ 3, base + part.ys + t), of(place, base + part.ys + t))
    if notes:
        own, side = notes
        for m in range(4):
            near[side + m] = got[m][own]
            far[side + m] = got[m][own]


def pick(tab, win, k, own, side):
    r = tab[k]
    low = jnp.where((r & 1) == 0, win[0][own], win[1][own])
    high = jnp.where((r & 1) == 0, win[2][own], win[3][own])
    beside = jnp.where((r & 1) == 0, win[4][side], win[5][side])
    return jnp.where(r < 4, jnp.where(r < 2, low, high), beside)


def pick_plane(tab, win, k, part, p):
    slot, m, delta = tab[BOXES + k], tab[2 * BOXES + k], tab[3 * BOXES + k]
    own = part.own + slot * part.tiles
    box = m * SLOTS + slot
    if part.lv == 0:
        x = p & 1
        direct = -1 if p >= 2 else 1
        side = part.side + jnp.where(delta == direct, box * 2 + x, 24 + slot * 6 + x)
        return pick(tab, win, k, own + p, side)
    lane = lanes()
    t = pick(tab, win, k, own, part.side + box)
    t = jnp.where(((lane & 1) == p >> 1) & ((lane & 32) == (p & 1) * 32), t, 0.0)
    return pair_sum(t, 0)


def pick_rows(tab, win, k, part, t):
    slot = tab[BOXES + k]
    own = part.own + slot * part.tiles + part.ys + t
    side = part.side + (24 + slot * 6 + 2 + t if part.lv == 0 else 12 + slot * 2 + t)
    return pick(tab, win, k, own, side)


def near_rows(y):
    lane = iota(y.shape, 1)
    return jnp.where(lane < 32, roll(y, 96, 1), jnp.where(lane < 96, y, roll(y, 32, 1)))


def take_ghosts(tab, win, part, xg, yg, ends):
    ys = 32 << part.lv
    low = iota((1, 128), 1) < 64
    for s in range(SLOTS):
        for g, (f, p) in enumerate(((0, 2), (0, 3), (1, 0), (1, 1))):
            xg[s, g] = pick_plane(tab, win, s * 4 + f, part, p)
        for t in range(part.tiles - part.ys):
            sv = pick_rows(tab, win, s * 4 + 2, part, t)
            nv = pick_rows(tab, win, s * 4 + 3, part, t)
            yg[s, 8 * t : 8 * t + 8, :] = jnp.where(lanes() < 64, sv, nv)

        def corner(q, p):
            return pick_plane(tab, win, 12 + s * 8 + q, part, p)

        for e, p in ((0, 3), (1, 0)):
            sp = corner(2 * e, p)[7:8]
            np = corner(2 * e + 1, p)[0:1]
            ends[s, e : e + 1, :] = jnp.where(low, roll(sp, ys, 1), roll(np, 128 - ys, 1))
            sp = corner(4 + e, p)[7:8]
            np = corner(6 + e, p)[0:1]
            ends[s, 2 + e : 3 + e, :] = jnp.where(low, roll(sp, 64, 1), roll(np, 64, 1))


def set_near(yg, gy, n):
    for s in range(SLOTS):
        for t in range(n // 8):
            gy[s, 8 * t : 8 * t + 8, :] = near_rows(yg[s, 8 * t : 8 * t + 8, :])


def planes_loop(n, body, carry, unroll=8):
    def chunk(c, carry):
        for u in range(unroll):
            carry = body(c * unroll + u, carry, u == unroll - 1)
        return carry

    return lax.fori_loop(0, n // unroll, chunk, carry)


def following(ref, s, i, n, edge, at_end):
    if not at_end:
        return ref[s, i + 1]
    return jnp.where(i == n - 1, edge, ref[s, jnp.minimum(i + 1, n - 1)])


def slab_sides(y, v, s, ends, n):
    lane = iota((n, 128), 1)
    row = iota((n, 128), 0)
    inner = jnp.where(lane < 64, roll(v[s, :, 0, :], 32, 1), roll(v[s, :, 7, :], 96, 1))
    outer = jnp.where(lane < 64, roll(y, 32, 1), roll(y, 96, 1))
    down = jnp.where(row == 0, ends[s, 2:3, :], roll(y, 1, 0))
    up = jnp.where(row == n - 1, ends[s, 3:4, :], roll(y, n - 1, 0))
    return outer, inner, down, up


def make_weights(b, xg, yg, ends, gy, tab, lv, w, extra):
    cx, cy, cz, wn, rd, slab = w
    n = PLANES[lv]
    h = 0.5 * 0.25**lv
    tl = Tile(lv)
    set_near(yg, gy, n)

    def has(k):
        return jnp.where(tab[4 * BOXES + k] == 1, 1.0, 0.0)

    def plane(s, i, here, w, nxt, wnext, row, south, north):
        wy = h * (here + tl.south(here, row))
        wy = jnp.where(tl.south_edge, wy * south, wy)
        wrow = h * (here + row) * north
        wz = jnp.where(tl.z_low, 0.0, h * (here + tl.below(here)))
        d = (w + wnext) + (wy + tl.north(wy, wrow)) + (wz + tl.above(wz))
        r = RELAXATION / d
        cx[s, i + 2] = wnext
        cy[s, i + 1] = wy
        cz[s, i + 1] = wz
        wn[s, pl.ds(i + 1, 1), :] = wrow[7:8, :]
        rd[s, i + 1] = r
        return r

    first = []
    for s in range(SLOTS):
        here, v = xg[s, 1], b[s, 0]
        w = h * (here + xg[s, 0])
        cx[s, 0] = w
        wnext = h * (here + v) * has(s * 4)
        plane(s, -1, here, w, v, wnext, ends[s, 0:1, :], has(12 + s * 8), has(13 + s * 8))
        first.append((v, wnext))

    def body(i, carry, at_end):
        out = []
        for s in range(SLOTS):
            v, w = carry[s]
            nxt = following(b, s, i, n, xg[s, 2], at_end)
            wnext = h * (v + nxt)
            if at_end:
                wnext = wnext * jnp.where(i == n - 1, has(s * 4 + 1), 1.0)
            r = plane(s, i, v, w, nxt, wnext, gy[s, pl.ds(i, 1), :], has(s * 4 + 2), has(s * 4 + 3))
            extra(s, i, r)
            out.append((nxt, wnext))
        return tuple(out)

    last = planes_loop(n, body, tuple(first))
    lane = iota((n, 128), 1)
    row = iota((n, 128), 0)
    for s in range(SLOTS):
        here, w = last[s]
        far = xg[s, 3]
        plane(s, n, here, w, far, h * (here + far), ends[s, 1:2, :], has(14 + s * 8), has(15 + s * 8))
        y = yg[s]
        outer, inner, down, up = (h * (y + t) for t in slab_sides(y, b, s, ends, n))
        k = 12 + s * 8
        down = down * jnp.where(row == 0, jnp.where(lane < 64, has(k + 4), has(k + 6)), 1.0)
        up = up * jnp.where(row == n - 1, jnp.where(lane < 64, has(k + 5), has(k + 7)), 1.0)
        zs = tl.zs
        wz = jnp.where((lane & 31) < zs, 0.0, h * (y + roll(y, zs, 1)))
        d = (outer + inner) + (down + up) + (wz + roll(wz, 128 - zs, 1))
        for m, t in enumerate((outer, inner, down, up, wz, RELAXATION / d)):
            slab[s, m] = t


def apply_level(v, before, after, gy, ends, lv, w, emit, wide=None):
    cx, cy, cz, wn = w[:4]
    n = PLANES[lv]
    tl = Tile(lv)

    def plane(s, i, here, fx, nxt, row):
        fnext = cx[s, i + 2] * (nxt - here)
        wrow = wn[s, pl.ds(i + 1, 1), :]
        fy = cy[s, i + 1] * (here - tl.south(here, row))
        fn = tl.north(fy, wrow * (row - here))
        fz = cz[s, i + 1] * (here - tl.below(here))
        return (fx - fnext) + (fy - fn) + (fz - tl.above(fz)), fnext

    first = []
    for s in range(SLOTS):
        v0, west = v[s, 0], before(s, 0)
        if wide:
            fx = cx[s, 0] * (west - before(s, 1))
            av, fx = plane(s, -1, west, fx, v0, ends[s, 0:1, :])
            wide(s, 0, west, av)
        else:
            fx = cx[s, 1] * (v0 - west)
        first.append((v0, fx))

    def body(i, carry, at_end):
        out = []
        for s in range(SLOTS):
            here, fx = carry[s]
            nxt = following(v, s, i, n, after(s, 0), at_end)
            av, fnext = plane(s, i, here, fx, nxt, gy[s, pl.ds(i, 1), :])
            emit(s, i, here, av)
            out.append((nxt, fnext))
        return tuple(out)

    last = planes_loop(n, body, tuple(first))
    if wide:
        for s in range(SLOTS):
            here, fx = last[s]
            av, fx = plane(s, n, here, fx, after(s, 1), ends[s, 1:2, :])
            wide(s, 1, here, av)


def apply_slab(yg, v, s, ends, lv, slab):
    n = PLANES[lv]
    zs = 1 << lv
    y = yg[s]
    outer, inner, down, up = slab_sides(y, v, s, ends, n)
    fz = slab[s, 4] * (y - roll(y, zs, 1))
    a = slab[s, 0] * (y - outer) + slab[s, 1] * (y - inner)
    b = slab[s, 2] * (y - down) + slab[s, 3] * (y - up)
    return y, a + b + (fz - roll(fz, 128 - zs, 1))


def sweep_wide(v, xg, yg, ends, gy, lv, w, first, first_x, first_y, out, out_x, out_y):
    rd, slab = w[4:]
    n = PLANES[lv]
    set_near(yg, gy, n)

    def emit(s, i, here, av):
        out[s, i] = here + (first[s, i] - av * rd[s, i + 1])

    def wide(s, e, here, av):
        out_x[s, e] = here + (first_x(s, e) - av * rd[s, (n + 1) * e])

    apply_level(v, lambda s, g: xg[s, 1 - g], lambda s, g: xg[s, 2 + g], gy, ends, lv, w, emit, wide)
    for s in range(SLOTS):
        y, a = apply_slab(yg, v, s, ends, lv, slab)
        out_y[s] = y + (first_y(s) - a * slab[s, 5])


def apply_near(v, gx, yg, gy, lv, w, emit):
    set_near(yg, gy, PLANES[lv])
    apply_level(v, lambda s, g: gx[s, 0], lambda s, g: gx[s, 1], gy, None, lv, w, emit)


def restrict_planes(v, s, lv, scale):
    out = []
    for c in range(PLANES[lv] // 2):
        out.append(pair_sum(v[s, 2 * c] + v[s, 2 * c + 1], lv) * scale)
    return out


def pack_bottom(planes, out):
    lane = lanes()
    at = (lane & 7) * 4
    part = lane >> 3
    top = None
    for s in range(2):
        for i in range(8):
            g = lane_take(planes[s][i], at)
            top = g if top is None else jnp.where(part == s * 8 + i, g, top)
    low = None
    for i in range(8):
        g = lane_take(planes[2][i], at)
        low = g if low is None else jnp.where((part & 7) == i, g, low)
    low = jnp.where(lane < 64, low, roll(low, 4, 0))
    out[0:8, :] = top
    out[8:16, :] = low


PART0, PART1 = Part(0), Part(1)
FIRST = (Part(0), Part(1, 24, 42))
FIRST_NOTES = (33, 60)


def place_of_device():
    dev = lax.axis_index("gx") * 16 + lax.axis_index("gy")
    return dev, 1 - ((dev >> 2) & 1), dev & 3, dev >> 2


def used(count, s):
    return jnp.where(s < count, 1.0, 0.0)


def load_beta(inv, s, b, b1):
    b[s] = inv[:, s, :].reshape(32, 8, 128)
    for c, t in enumerate(restrict_planes(b, s, 0, 0.125)):
        b1[s, c] = t


def k_start(ghost, count, inv, faces, gathered, place, b, b1):
    bottom = []
    dev = place_of_device()[0]
    lane = lanes()
    note = jnp.where(lane == 12, jnp.full((8, 128), count[0]), 0)
    codes = jnp.zeros((8, 128), I32)
    for s in range(SLOTS):
        for f in range(4):
            k = s * 4 + f
            g = ghost[s, f]
            has = g >= 0
            owner = jnp.where(has, (g * 21846) >> 16, dev)
            local = jnp.where(has, g - 3 * owner, 0)
            place[k] = owner
            place[12 + k] = local
            note = jnp.where(lane == k, jnp.full((8, 128), g), note)
            codes = jnp.where(lane == k, jnp.full((8, 128), jnp.where(has, owner * 4 + local, -1)), codes)
    place[24] = dev
    note = note.astype(F32)
    for s in range(SLOTS):
        load_beta(inv, s, b, b1)
        bottom.append(restrict_planes(b1, s, 1, 0.125))
        pack_faces(b, s, FIRST[0], faces)
        pack_faces(b1, s, FIRST[1], faces)
    faces[FIRST_NOTES[0]] = codes.astype(F32)
    pack_bottom(bottom, gathered)
    gathered[16:24, :] = note


def fill_table(win, rows, notes, sem, tab):
    _, even, place, block = place_of_device()
    own, side = FIRST_NOTES
    rows[...] = jnp.zeros((16, 128), I32)
    for m in range(4):
        rows[m : m + 1, :] = win[m][own][0:1].astype(I32)
        for x in range(2):
            rows[4 + 4 * x + m : 5 + 4 * x + m, :] = win[4 + x][side + m][0:1].astype(I32)
    copy = pltpu.make_async_copy(rows, notes, sem)
    copy.start()
    copy.wait()

    def entry(k, code):
        owner = code >> 2
        delta = jnp.where(code >= 0, (owner >> 2) - block, 0)
        m = jnp.where(code >= 0, (owner & 3) ^ place, 0)
        slot = jnp.where(code >= 0, code & 3, 0)
        r = jnp.where(delta == 0, m, jnp.where(delta == 2 * even - 1, 4, 5))
        for x, value in enumerate((r, slot, m, delta, jnp.where(code >= 0, 1, 0))):
            tab[x * BOXES + k] = value
        return jnp.where(r < 4, 0, r - 3) * 4 + m, slot * 4

    for s in range(SLOTS):
        codes = [notes[0, s * 4 + f] for f in range(4)]
        found = [entry(s * 4 + f, codes[f]) for f in range(4)]
        for q, (f, g) in enumerate(TWO_FACES):
            entry(12 + s * 8 + q, jnp.where(codes[f] >= 0, notes[found[f][0], found[f][1] + g], -1))


def k_weights(count, src, inv, *refs):
    win, refs = refs[:6], refs[6:]
    w, s_out, u, b1, faces, tab, (b, xg, yg, ends, gy, rows, notes, sem) = (
        refs[:6], refs[6], refs[7], refs[8], refs[9], refs[10], refs[11:]
    )
    fill_table(win, rows, notes, sem, tab)
    for s in range(SLOTS):
        s_out[s] = src[:, s, :].reshape(32, 8, 128) * used(count[0], s)
        load_beta(inv, s, b, b1)
    take_ghosts(tab, win, FIRST[0], xg, yg, ends)

    def first(s, i, r):
        u[s, i] = s_out[s, i] * r

    make_weights(b, xg, yg, ends, gy, tab, 0, w, first)
    for s in range(SLOTS):
        pack_faces(u, s, PART0, faces)


def k_weights_next(tab, b1, *refs):
    win, w1, (xg, yg, ends, gy) = refs[:6], refs[6:12], refs[12:]
    take_ghosts(tab, win, FIRST[1], xg, yg, ends)
    make_weights(b1, xg, yg, ends, gy, tab, 1, w1, lambda s, i, r: None)


def k_down(tab, t, u, *refs):
    win, w, rd1 = refs[:6], refs[6:12], refs[12]
    out, out_x, out_y, first_x, first_y, f1, u1, faces, xg, yg, ends, gy, res = refs[13:]
    take_ghosts(tab, win, PART0, xg, yg, ends)
    for s in range(SLOTS):
        for e in range(2):
            first_x[s, e] = xg[s, 1 + e]
        first_y[s] = yg[s]
    sweep_wide(u, xg, yg, ends, gy, 0, w, u, lambda s, e: xg[s, 1 + e], lambda s: yg[s], out, out_x, out_y)

    def emit(s, i, here, av):
        res[s, i] = t[s, i] - av

    apply_near(out, out_x, out_y, gy, 0, w, emit)
    for s in range(SLOTS):
        for c, p in enumerate(restrict_planes(res, s, 0, 0.125)):
            f1[s, c] = p
            u1[s, c] = p * rd1[s, c + 1]
        pack_faces(u1, s, PART1, faces)


def k_bottom_rhs(tab, t, u, *refs):
    win, w = refs[:6], refs[6:12]
    out, out_x, out_y, first_x, first_y, packed, xg, yg, ends, gy, res = refs[12:]
    take_ghosts(tab, win, PART1, xg, yg, ends)
    for s in range(SLOTS):
        for e in range(2):
            first_x[s, e] = xg[s, 1 + e]
        first_y[s] = yg[s]
    sweep_wide(u, xg, yg, ends, gy, 1, w, u, lambda s, e: xg[s, 1 + e], lambda s: yg[s], out, out_x, out_y)

    def emit(s, i, here, av):
        res[s, i] = t[s, i] - av

    apply_near(out, out_x, out_y, gy, 1, w, emit)
    pack_bottom([restrict_planes(res, s, 1, 0.125) for s in range(SLOTS)], packed)


def total(v):
    return jnp.sum(v, axis=(0, 1), keepdims=True)


def unpack_bottom(rows, put):
    for r in range(12):
        t = rows[:, r, :].T
        for half in range(2):
            s, j = (half, r) if r < 8 else (2, r - 8 + 4 * half)
            for i in range(8):
                put(s, j, i, t[half * 64 + i * 8 : half * 64 + i * 8 + 8, :])


def face_gather(dev_at, slot_at, place):
    out = lane_take(place(0), dev_at)
    for other in range(1, SLOTS):
        out = jnp.where(slot_at == other, lane_take(place(other), dev_at), out)
    return out


def fill_bottom_ghosts(p, at, slot):
    for s in range(SLOTS):
        for f, (src, dst) in enumerate(((7, 0), (0, 9))):
            k = s * 4 + f
            for m in range(1, 9):
                p[s, m, dst] = face_gather(at[k], slot[k], lambda o: p[o, m, src + 1])
            k = s * 4 + 2 + f
            for m in range(1, 9):
                p[s, dst, m] = face_gather(at[k], slot[k], lambda o: p[o, src + 1, m])


def k_bottom_weights(beta_rows, cx, cy, cz, at_out, slot_out, counts_out, p):
    note = beta_rows[:, 16, :].T
    at, slot, pres = [], [], []
    for f in range(12):
        gf = jnp.broadcast_to(note[f : f + 1, :], (8, 128))
        has = gf >= 0.0
        gf = jnp.where(has, gf, 0.0)
        dv = ((gf + 0.5) * (1.0 / 3.0)).astype(I32)
        at.append(dv)
        slot.append(gf.astype(I32) - 3 * dv)
        pres.append(jnp.where(has, 1.0, 0.0))
        at_out[f] = dv.astype(F32)
        slot_out[f] = slot[f].astype(F32)
    counts_out[...] = jnp.broadcast_to(note[12:13, :], (8, 128))

    def put_beta(s, j, i, tile):
        p[s, j + 1, i + 1] = tile

    unpack_bottom(beta_rows, put_beta)
    fill_bottom_ghosts(p, at, slot)
    h = 0.5 * 0.0625
    low = subs() == 0

    def weights(m, _):
        for s in range(SLOTS):
            for i in range(9):
                w = h * (p[s, m + 1, i] + p[s, m + 1, i + 1])
                if i == 0:
                    w = w * pres[s * 4]
                if i == 8:
                    w = w * pres[s * 4 + 1]
                cx[s, m, i] = w
                w = h * (p[s, i, m + 1] + p[s, i + 1, m + 1])
                if i == 0:
                    w = w * pres[s * 4 + 2]
                if i == 8:
                    w = w * pres[s * 4 + 3]
                cy[s, i, m] = w
            for i in range(8):
                b = p[s, m + 1, i + 1]
                cz[s, m, i] = jnp.where(low, 0.0, h * (b + roll(b, 1, 0)))
        return 0

    lax.fori_loop(0, 8, weights, 0)


def k_bottom(place, cx, cy, cz, at_in, slot_in, counts_in, mine64, other64, *refs):
    far, (out, faces, boxes_out) = refs[:9], refs[9:12]
    p, r, x, q, back, sq, rhs_rows, v1, gx, yg, gy = refs[12:23]
    kept, sem = refs[23:32], refs[32]
    copies = [pltpu.make_async_copy(a, b, sem.at[n]) for n, (a, b) in enumerate(zip(far, kept))]
    for c in copies:
        c.start()
    first, u, gx0, gy0 = kept[:4]
    w1 = kept[4:]
    me = place[24]
    for m in range(64):
        here = me ^ ((m & 15) | ((m >> 4) << 5))
        rhs_rows[here] = mine64[m]
        rhs_rows[here ^ 16] = other64[m]
    at = [at_in[f].astype(I32) for f in range(12)]
    slot = [slot_in[f].astype(I32) for f in range(12)]
    counts = counts_in[...]
    boxes = jnp.sum(counts[0:1], axis=1, keepdims=True)
    boxes_out[...] = jnp.broadcast_to(boxes, (8, 128))

    def fill_ghosts():
        fill_bottom_ghosts(p, at, slot)

    def put_rhs(s, j, i, tile):
        r[s, j, i] = tile

    unpack_bottom(rhs_rows, put_rhs)

    zero = jnp.zeros((8, 128), F32)

    def each(fn):
        def step(j, acc):
            acc = list(acc)
            for s in range(SLOTS):
                for i in range(8):
                    acc[i] = fn(s, j, i, acc[i])
            return tuple(acc)

        a = lax.fori_loop(0, 8, step, (zero,) * 8, unroll=2)
        a = ((a[0] + a[1]) + (a[2] + a[3])) + ((a[4] + a[5]) + (a[6] + a[7]))
        return jnp.broadcast_to(total(a), (8, 128))

    mean = each(lambda s, j, i, acc: acc + r[s, j, i]) / jnp.broadcast_to(boxes * 512.0, (8, 128))
    valid = [jnp.where(counts > s + 0.5, 1.0, 0.0) for s in range(SLOTS)]

    def shift(s, j, i, acc):
        v = (r[s, j, i] - mean) * valid[s]
        r[s, j, i] = v
        p[s, j + 1, i + 1] = v
        x[s, j, i] = zero
        return acc + v * v

    rr = each(shift)

    def image(s, j, i, acc):
        here = p[s, j + 1, i + 1]
        a = cx[s, j, i] * (here - p[s, j + 1, i]) + cx[s, j, i + 1] * (here - p[s, j + 1, i + 2])
        b = cy[s, j, i] * (here - p[s, j, i + 1]) + cy[s, j + 1, i] * (here - p[s, j + 2, i + 1])
        fz = cz[s, j, i] * (here - roll(here, 1, 0))
        v = a + b + (fz - roll(fz, 7, 0))
        q[s, j, i] = v
        return acc + here * v

    def iteration(it, rr):
        fill_ghosts()
        alpha = rr / each(image)

        def step(s, j, i, acc):
            x[s, j, i] = x[s, j, i] + alpha * p[s, j + 1, i + 1]
            v = r[s, j, i] - alpha * q[s, j, i]
            r[s, j, i] = v
            return acc + v * v

        rr_next = each(step)
        ratio = rr_next / rr

        def turn(j, _):
            for s in range(SLOTS):
                for i in range(8):
                    p[s, j + 1, i + 1] = r[s, j, i] + ratio * p[s, j + 1, i + 1]
            return 0

        lax.fori_loop(0, 8, turn, 0)
        return rr_next

    rr = lax.fori_loop(0, BOTTOM_ITERS - 1, iteration, rr)
    fill_ghosts()
    alpha = rr / each(image)

    for row in range(12):
        for half in range(2):
            s, j = (half, row) if row < 8 else (2, row - 8 + 4 * half)
            for i in range(8):
                sq[half * 64 + i * 8 : half * 64 + i * 8 + 8, :] = x[s, j, i] + alpha * p[s, j + 1, i + 1]
        tr = sq[...].T
        if row < 8:
            back[:, row, :] = tr
            back[:, 8 + row, :] = roll(tr, 64, 1)
        else:
            back[:, 8 + row, :] = tr
            back[:, 12 + row, :] = roll(tr, 64, 1)

    for c in copies:
        c.wait()
    lane, sub = lanes(), subs()
    kat = (lane & 31) >> 2

    def box(dev, s):
        return back[dev, pl.ds(pl.multiple_of(8 * s, 8), 8), :]

    for s in range(SLOTS):
        mine = box(me, s)
        for i in range(8):
            g = lane_take(mine, kat + i * 8)
            v1[s, 2 * i] = u[s, 2 * i] + g
            v1[s, 2 * i + 1] = u[s, 2 * i + 1] + g
        near = [box(place[s * 4 + f], place[12 + s * 4 + f]) for f in range(4)]
        for f, i in ((0, 7), (1, 0)):
            gx[s, f] = gx0[s, f] + lane_take(near[f], kat + i * 8)
        sb = jnp.broadcast_to(near[2][7:8, :], (8, 128))
        nb = jnp.broadcast_to(near[3][0:1, :], (8, 128))
        for part in range(2):
            idx = kat + (part * 4 + (sub >> 1)) * 8
            g = jnp.where(lane < 64, lane_take(sb, idx), lane_take(nb, idx))
            yg[s, 8 * part : 8 * part + 8, :] = gy0[s, 8 * part : 8 * part + 8, :] + g

    def emit(s, i, here, av):
        out[s, i] = here + (first[s, i] - av * w1[4][s, i + 1])

    apply_near(v1, gx, yg, gy, 1, w1, emit)
    for s in range(SLOTS):
        pack_faces(out, s, PART1, faces)


def k_up(tab, first1, first1_x, first1_y, u1, first, u0, u0_x, u0_y, *refs):
    win, w1, w = refs[:6], refs[6:12], refs[12:18]
    out, faces, c, c_x, c_y, xg, yg, ends, gy1, v, gx, y0, gy = refs[18:]
    take_ghosts(tab, win, PART1, xg, yg, ends)
    sweep_wide(u1, xg, yg, ends, gy1, 1, w1, first1, lambda s, e: first1_x[s, e], lambda s: first1_y[s], c, c_x, c_y)
    for s in range(SLOTS):
        for f in range(2):
            gx[s, f] = u0_x[s, f] + c_x[s, f]
        for i in range(16):
            t = c[s, i]
            v[s, 2 * i] = u0[s, 2 * i] + t
            v[s, 2 * i + 1] = u0[s, 2 * i + 1] + t
            y0[s, 2 * i : 2 * i + 2, :] = u0_y[s, 2 * i : 2 * i + 2, :] + c_y[s, i : i + 1, :]

    def emit(s, i, here, av):
        out[s, i] = here + (first[s, i] - av * w[4][s, i + 1])

    apply_near(v, gx, y0, gy, 0, w, emit)
    for s in range(SLOTS):
        pack_faces(out, s, PART0, faces)


def k_residual(tab, t, u, first, first_x, first_y, *refs):
    win, w = refs[:6], refs[6:12]
    out, res_out, sums, out_x, out_y, xg, yg, ends, gy, res = refs[12:]
    take_ghosts(tab, win, PART0, xg, yg, ends)
    sweep_wide(u, xg, yg, ends, gy, 0, w, first, lambda s, e: first_x[s, e], lambda s: first_y[s], out, out_x, out_y)

    def emit(s, i, here, av):
        res[s, i] = t[s, i] - av

    apply_near(out, out_x, out_y, gy, 0, w, emit)
    su = jnp.zeros((8, 128), F32)
    sr = jnp.zeros((8, 128), F32)
    for s in range(SLOTS):
        for i in range(32):
            d = res[s, i]
            sr = sr + d * d
            su = su + out[s, i]
        res_out[:, s, :] = res[s].reshape(256, 128)
    lane = iota((1, 128), 1)
    sums[...] = jnp.where(lane == 0, total(su), jnp.where(lane == 1, total(sr), 0.0))


def k_finish(count, u, sums, boxes, corr, norm):
    tot = jnp.sum(sums[...], axis=0, keepdims=True)
    cells = boxes[0:1, 0:1] * 32768.0
    mean = tot[:, 0:1] / cells
    for s in range(SLOTS):
        corr[:, s, :] = ((u[s] - mean) * used(count[0], s)).reshape(256, 128)
    norm[...] = jnp.broadcast_to(jnp.sqrt(tot[:, 1:2] / cells), (1, 128))


VMEM = pl.BlockSpec(memory_space=pltpu.VMEM)
SMEM = pl.BlockSpec(memory_space=pltpu.SMEM)
HBM = pl.BlockSpec(memory_space=pltpu.HBM)


def call(kernel, smem, args, outs, scratch=(), vmem=16, tables=(), hbm=0, extra=()):
    shape = lambda s: jax.ShapeDtypeStruct(s, F32)
    return pl.pallas_call(
        kernel,
        out_shape=[shape(s) for s in outs] + [jax.ShapeDtypeStruct(s, I32) for s in tables],
        in_specs=[SMEM] * smem + [VMEM] * (len(args) - smem - hbm) + [HBM] * hbm,
        out_specs=[VMEM] * len(outs) + [SMEM] * len(tables),
        scratch_shapes=[pltpu.VMEM(s, F32) for s in scratch] + list(extra),
        compiler_params=pltpu.CompilerParams(vmem_limit_bytes=vmem * 1024 * 1024),
    )(*args)


def swapped(block, pairs):
    route = sorted([(a, b) for a, b in pairs] + [(b, a) for a, b in pairs])
    return lax.ppermute(block, AX, route)


def xor_pairs(m):
    return [(i, i ^ m) for i in range(DEVICES) if i < i ^ m]


def exchange(faces, parts, notes=()):
    got = [faces]
    for m in (1, 2, 3):
        got.append(swapped(faces, xor_pairs(m)))
    tiles = parts[-1].side + parts[-1].side_tiles + (4 if notes else 0)
    sides = call(functools.partial(k_relay, parts, notes), 0, got, [(tiles, 8, 128)] * 2)
    for odd in (0, 1):
        pairs = [(i, i + 4) for i in range(DEVICES - 4) if (i // 4) % 2 == odd]
        got.append(swapped(sides[odd], pairs))
    return tuple(got)


def k_join(*refs):
    n = refs[0].shape[0]
    for m in range(4):
        refs[4][m * n : (m + 1) * n] = refs[m][...]


def gather_rows(rows, beside):
    rows = rows[None]
    for unit in (1, 4, 32):
        if unit == 32:
            rows, beside = lax.optimization_barrier((rows, beside))
        got = [rows] + [swapped(rows, xor_pairs(m * unit)) for m in (1, 2, 3)]
        rows = call(k_join, 0, got, [(4 * rows.shape[0],) + rows.shape[1:]])[0]
    return tuple(beside) + (rows, swapped(rows, xor_pairs(16)))


def to_all(rows):
    spread = jnp.broadcast_to(rows[None], (DEVICES,) + rows.shape)
    return lax.all_to_all(spread, AX, 0, 0)


def shards(source_term, inverse_density, box_counts, ghost_from):
    view = lambda a: a.reshape(SLOTS, 256, 128).transpose(1, 0, 2)
    fine, mid = (SLOTS, 32, 8, 128), (SLOTS, 16, 8, 128)
    gx, xg, ends = (SLOTS, 2, 8, 128), (SLOTS, 4, 8, 128), (SLOTS, 8, 128)
    gyf, gym = (SLOTS, 32, 128), (SLOTS, 16, 128)
    face0, face1 = (PART0.own_tiles, 8, 128), (PART1.own_tiles, 8, 128)

    def weight_shapes(n):
        wide = (SLOTS, n + 2, 8, 128)
        return [(SLOTS, n + 3, 8, 128), wide, wide, (SLOTS, n + 2, 128), wide, (SLOTS, 6, n, 128)]

    faces, notes, place = call(
        k_start, 2, (ghost_from, box_counts, view(inverse_density)),
        [(FIRST_NOTES[0] + 1, 8, 128), (24, 128)], [fine, mid], tables=[(25,)],
    )
    beta_rows = lax.all_gather(notes, AX)
    win = exchange(faces, FIRST, FIRST_NOTES)
    outs = call(
        k_weights, 1, (box_counts, view(source_term), view(inverse_density)) + win,
        weight_shapes(32) + [fine, fine, mid, face0], [fine, xg, gyf, ends, gyf], tables=[(5 * BOXES,)],
        extra=[pltpu.VMEM((16, 128), I32), pltpu.SMEM((16, 128), I32), pltpu.SemaphoreType.DMA],
    )
    w, (source, first, beta1, faces, tab) = tuple(outs[:6]), outs[6:]
    w1 = tuple(call(k_weights_next, 1, (tab, beta1) + win, weight_shapes(16), [xg, gym, ends, gym]))
    u, u_x, u_y, first_x, first_y, f1, first1, faces = call(
        k_down, 1, (tab, source, first) + exchange(faces, [PART0]) + w + (w1[4],),
        [fine, gx, gyf, gx, gyf, mid, mid, face1], [xg, gyf, ends, gyf, fine],
    )
    u1, u1_x, u1_y, first1_x, first1_y, rows = call(
        k_bottom_rhs, 1, (tab, f1, first1) + exchange(faces, [PART1]) + w1,
        [mid, gx, gym, gx, gym, (16, 128)], [xg, gym, ends, gym, mid],
    )
    cube, padded = (SLOTS, 8, 8, 8, 128), (SLOTS, 10, 10, 8, 128)
    bottom_w = call(
        k_bottom_weights, 0, (beta_rows,),
        [(SLOTS, 8, 9, 8, 128), (SLOTS, 9, 8, 8, 128), cube, (12, 8, 128), (12, 8, 128), (8, 128)], [padded],
    )
    kept = [first1, u1, u1_x, u1_y] + list(w1[:5])
    u1, faces, boxes = call(
        k_bottom, 1, (place,) + gather_rows(rows, tuple(bottom_w)) + tuple(kept), [mid, face1, (8, 128)],
        [padded, cube, cube, cube, (DEVICES, 24, 128), (128, 128), (DEVICES, 16, 128), mid, gx, gym, gym]
        + [a.shape for a in kept],
        hbm=len(kept), extra=[pltpu.SemaphoreType.DMA((len(kept),))],
    )
    u, faces = call(
        k_up, 1,
        (tab, first1, first1_x, first1_y, u1, first, u, u_x, u_y) + exchange(faces, [PART1]) + w1 + w,
        [fine, face0], [mid, gx, gym, xg, gym, ends, gym, fine, gx, gyf, gyf],
    )
    u, residual, sums = call(
        k_residual, 1, (tab, source, u, first, first_x, first_y) + exchange(faces, [PART0]) + w,
        [fine, (256, SLOTS, 128), (1, 128)], [gx, gyf, xg, gyf, ends, gyf, fine],
    )
    parts = to_all(sums).reshape(DEVICES, 128)
    correction, norm = call(k_finish, 1, (box_counts, u, parts, boxes), [(256, SLOTS, 128), (1, 128)])
    back = lambda a: a.transpose(1, 0, 2).reshape(SLOTS, 32768)
    return back(correction), back(residual), norm[0, 0]


def solution(mesh):
    rows = P(AX, None)
    return jax.shard_map(
        shards, mesh=mesh, in_specs=(rows, rows, P(AX), rows), out_specs=(rows, rows, P()), check_vma=False
    )
```

```python
import functools

import jax
import jax.numpy as jnp
from jax import lax
from jax.experimental import pallas as pl
from jax.experimental.pallas import tpu as pltpu
from jax.sharding import PartitionSpec as P

AX = ("gx", "gy")
DEVICES = 128
SLOTS = 3
BOTTOM_ITERS = 8
RELAXATION = 2.0 / 3.0
F32 = jnp.float32
I32 = jnp.int32

PLANES = (32, 16)


def iota(shape, dim):
    return lax.broadcasted_iota(I32, shape, dim)


def lanes():
    return iota((8, 128), 1)


def subs():
    return iota((8, 128), 0)


def roll(x, shift, axis):
    return pltpu.roll(x, shift, axis)


def lane_take(x, at):
    return jnp.take_along_axis(x, at, axis=1, mode="promise_in_bounds")


class Tile:
    def __init__(self, lv):
        self.zs, self.ys = 1 << lv, 32 << lv
        lane, sub = lanes(), subs()
        self.south_in = lane >= self.ys
        self.north_in = lane < 128 - self.ys
        self.first_row = sub == 0
        self.last_row = sub == 7
        self.south_edge = self.first_row & (lane < self.ys)
        self.z_low = (lane & 31) < self.zs

    def south(self, v, row):
        r = roll(v, self.ys, 1)
        return jnp.where(self.south_in, r, jnp.where(self.first_row, row, roll(r, 1, 0)))

    def north(self, v, edge):
        r = roll(v, 128 - self.ys, 1)
        return jnp.where(self.north_in, r, jnp.where(self.last_row, edge, roll(r, 7, 0)))

    def below(self, v):
        return roll(v, self.zs, 1)

    def above(self, v):
        return roll(v, 128 - self.zs, 1)


def pair_sum(t, lv):
    lane = lanes()
    zs, ys = 1 << lv, 32 << lv
    t = t + jnp.where((lane & zs) == 0, roll(t, 128 - zs, 1), roll(t, zs, 1))
    return t + jnp.where((lane & ys) == 0, roll(t, 128 - ys, 1), roll(t, ys, 1))


BOXES = 36
TWO_FACES = ((0, 2), (0, 3), (1, 2), (1, 3), (2, 0), (2, 1), (3, 0), (3, 1))


class Part:
    def __init__(self, lv, own=0, side=0):
        self.lv, self.own, self.side = lv, own, side
        self.tiles = (8, 3)[lv]
        self.ys = (4, 1)[lv]
        self.own_tiles = SLOTS * self.tiles
        self.side_tiles = (42, 18)[lv]


def pack_faces(v, s, part, out):
    lv = part.lv
    n = PLANES[lv]
    base = part.own + s * part.tiles
    planes = [v[s, 0], v[s, 1], v[s, n - 2], v[s, n - 1]]
    y0 = v[s, :, 0, :]
    y7 = v[s, :, 7, :]
    lane = iota((n, 128), 1)
    if lv == 0:
        for m in range(4):
            out[base + m] = planes[m]
        q = roll(jnp.where(lane >= 64, y7, y0), 64, 1)
    else:
        odd_k, odd_j = (lanes() & 1) == 1, (lanes() & 32) == 32
        out[base] = jnp.where(
            odd_k, jnp.where(odd_j, planes[3], planes[2]), jnp.where(odd_j, planes[1], planes[0])
        )
        q = jnp.where(
            lane < 32, y7, jnp.where(lane < 64, roll(y7, 96, 1), jnp.where(lane < 96, roll(y0, 64, 1), y0))
        )
    for t in range(n // 8):
        out[base + part.ys + t] = q[8 * t : 8 * t + 8]


def k_relay(parts, notes, *refs):
    got, (near, far) = refs[:4], refs[4:]
    _, even, place, _ = place_of_device()
    even = even == 1

    def of(m, t):
        low = jnp.where((m & 1) == 0, got[0][t], got[1][t])
        high = jnp.where((m & 1) == 0, got[2][t], got[3][t])
        return jnp.where(m < 2, low, high)

    def put(at, fwd, bwd):
        near[at] = jnp.where(even, fwd, bwd)
        far[at] = jnp.where(even, bwd, fwd)

    for part in parts:
        for s in range(SLOTS):
            base = part.own + s * part.tiles
            for m in range(4):
                box = m * SLOTS + s
                if part.lv == 0:
                    for x in range(2):
                        put(part.side + box * 2 + x, got[m][base + 2 + x], got[m][base + x])
                else:
                    put(part.side + box, got[m][base], got[m][base])
            if part.lv == 0:
                for x in range(2):
                    put(part.side + 24 + s * 6 + x, of(place ^ 3, base + x), of(place, base + 2 + x))
            for t in range(part.tiles - part.ys):
                at = part.side + (24 + s * 6 + 2 + t if part.lv == 0 else 12 + s * 2 + t)
                put(at, of(place ^ 3, base + part.ys + t), of(place, base + part.ys + t))
    if notes:
        own, side = notes
        for m in range(4):
            near[side + m] = got[m][own]
            far[side + m] = got[m][own]


def pick(tab, win, k, own, side):
    r = tab[k]
    low = jnp.where((r & 1) == 0, win[0][own], win[1][own])
    high = jnp.where((r & 1) == 0, win[2][own], win[3][own])
    beside = jnp.where((r & 1) == 0, win[4][side], win[5][side])
    return jnp.where(r < 4, jnp.where(r < 2, low, high), beside)


def pick_plane(tab, win, k, part, p):
    slot, m, delta = tab[BOXES + k], tab[2 * BOXES + k], tab[3 * BOXES + k]
    own = part.own + slot * part.tiles
    box = m * SLOTS + slot
    if part.lv == 0:
        x = p & 1
        direct = -1 if p >= 2 else 1
        side = part.side + jnp.where(delta == direct, box * 2 + x, 24 + slot * 6 + x)
        return pick(tab, win, k, own + p, side)
    lane = lanes()
    t = pick(tab, win, k, own, part.side + box)
    t = jnp.where(((lane & 1) == p >> 1) & ((lane & 32) == (p & 1) * 32), t, 0.0)
    return pair_sum(t, 0)


def pick_rows(tab, win, k, part, t):
    slot = tab[BOXES + k]
    own = part.own + slot * part.tiles + part.ys + t
    side = part.side + (24 + slot * 6 + 2 + t if part.lv == 0 else 12 + slot * 2 + t)
    return pick(tab, win, k, own, side)


def near_rows(y):
    lane = iota(y.shape, 1)
    return jnp.where(lane < 32, roll(y, 96, 1), jnp.where(lane < 96, y, roll(y, 32, 1)))


def take_ghosts(tab, win, part, xg, yg, ends):
    ys = 32 << part.lv
    low = iota((1, 128), 1) < 64
    for s in range(SLOTS):
        for g, (f, p) in enumerate(((0, 2), (0, 3), (1, 0), (1, 1))):
            xg[s, g] = pick_plane(tab, win, s * 4 + f, part, p)
        for t in range(part.tiles - part.ys):
            sv = pick_rows(tab, win, s * 4 + 2, part, t)
            nv = pick_rows(tab, win, s * 4 + 3, part, t)
            yg[s, 8 * t : 8 * t + 8, :] = jnp.where(lanes() < 64, sv, nv)

        def corner(q, p):
            return pick_plane(tab, win, 12 + s * 8 + q, part, p)

        for e, p in ((0, 3), (1, 0)):
            sp = corner(2 * e, p)[7:8]
            np = corner(2 * e + 1, p)[0:1]
            ends[s, e : e + 1, :] = jnp.where(low, roll(sp, ys, 1), roll(np, 128 - ys, 1))
            sp = corner(4 + e, p)[7:8]
            np = corner(6 + e, p)[0:1]
            ends[s, 2 + e : 3 + e, :] = jnp.where(low, roll(sp, 64, 1), roll(np, 64, 1))


def set_near(yg, gy, n):
    for s in range(SLOTS):
        for t in range(n // 8):
            gy[s, 8 * t : 8 * t + 8, :] = near_rows(yg[s, 8 * t : 8 * t + 8, :])


def planes_loop(n, body, carry, unroll=8):
    def chunk(c, carry):
        for u in range(unroll):
            carry = body(c * unroll + u, carry, u == unroll - 1)
        return carry

    return lax.fori_loop(0, n // unroll, chunk, carry)


def following(ref, s, i, n, edge, at_end):
    if not at_end:
        return ref[s, i + 1]
    return jnp.where(i == n - 1, edge, ref[s, jnp.minimum(i + 1, n - 1)])


def slab_sides(y, v, s, ends, n):
    lane = iota((n, 128), 1)
    row = iota((n, 128), 0)
    inner = jnp.where(lane < 64, roll(v[s, :, 0, :], 32, 1), roll(v[s, :, 7, :], 96, 1))
    outer = jnp.where(lane < 64, roll(y, 32, 1), roll(y, 96, 1))
    down = jnp.where(row == 0, ends[s, 2:3, :], roll(y, 1, 0))
    up = jnp.where(row == n - 1, ends[s, 3:4, :], roll(y, n - 1, 0))
    return outer, inner, down, up


def make_weights(b, xg, yg, ends, gy, tab, lv, w, extra):
    cx, cy, cz, wn, rd, slab = w
    n = PLANES[lv]
    h = 0.5 * 0.25**lv
    tl = Tile(lv)
    set_near(yg, gy, n)

    def has(k):
        return jnp.where(tab[4 * BOXES + k] == 1, 1.0, 0.0)

    def plane(s, i, here, w, nxt, wnext, row, south, north):
        wy = h * (here + tl.south(here, row))
        wy = jnp.where(tl.south_edge, wy * south, wy)
        wrow = h * (here + row) * north
        wz = jnp.where(tl.z_low, 0.0, h * (here + tl.below(here)))
        d = (w + wnext) + (wy + tl.north(wy, wrow)) + (wz + tl.above(wz))
        r = RELAXATION / d
        cx[s, i + 2] = wnext
        cy[s, i + 1] = wy
        cz[s, i + 1] = wz
        wn[s, pl.ds(i + 1, 1), :] = wrow[7:8, :]
        rd[s, i + 1] = r
        return r

    first = []
    for s in range(SLOTS):
        here, v = xg[s, 1], b[s, 0]
        w = h * (here + xg[s, 0])
        cx[s, 0] = w
        wnext = h * (here + v) * has(s * 4)
        plane(s, -1, here, w, v, wnext, ends[s, 0:1, :], has(12 + s * 8), has(13 + s * 8))
        first.append((v, wnext))

    def body(i, carry, at_end):
        out = []
        for s in range(SLOTS):
            v, w = carry[s]
            nxt = following(b, s, i, n, xg[s, 2], at_end)
            wnext = h * (v + nxt)
            if at_end:
                wnext = wnext * jnp.where(i == n - 1, has(s * 4 + 1), 1.0)
            r = plane(s, i, v, w, nxt, wnext, gy[s, pl.ds(i, 1), :], has(s * 4 + 2), has(s * 4 + 3))
            extra(s, i, r)
            out.append((nxt, wnext))
        return tuple(out)

    last = planes_loop(n, body, tuple(first))
    lane = iota((n, 128), 1)
    row = iota((n, 128), 0)
    for s in range(SLOTS):
        here, w = last[s]
        far = xg[s, 3]
        plane(s, n, here, w, far, h * (here + far), ends[s, 1:2, :], has(14 + s * 8), has(15 + s * 8))
        y = yg[s]
        outer, inner, down, up = (h * (y + t) for t in slab_sides(y, b, s, ends, n))
        k = 12 + s * 8
        down = down * jnp.where(row == 0, jnp.where(lane < 64, has(k + 4), has(k + 6)), 1.0)
        up = up * jnp.where(row == n - 1, jnp.where(lane < 64, has(k + 5), has(k + 7)), 1.0)
        zs = tl.zs
        wz = jnp.where((lane & 31) < zs, 0.0, h * (y + roll(y, zs, 1)))
        d = (outer + inner) + (down + up) + (wz + roll(wz, 128 - zs, 1))
        for m, t in enumerate((outer, inner, down, up, wz, RELAXATION / d)):
            slab[s, m] = t


def apply_level(v, before, after, gy, ends, lv, w, emit, wide=None):
    cx, cy, cz, wn = w[:4]
    n = PLANES[lv]
    tl = Tile(lv)

    def plane(s, i, here, fx, nxt, row):
        fnext = cx[s, i + 2] * (nxt - here)
        wrow = wn[s, pl.ds(i + 1, 1), :]
        fy = cy[s, i + 1] * (here - tl.south(here, row))
        fn = tl.north(fy, wrow * (row - here))
        fz = cz[s, i + 1] * (here - tl.below(here))
        return (fx - fnext) + (fy - fn) + (fz - tl.above(fz)), fnext

    first = []
    for s in range(SLOTS):
        v0, west = v[s, 0], before(s, 0)
        if wide:
            fx = cx[s, 0] * (west - before(s, 1))
            av, fx = plane(s, -1, west, fx, v0, ends[s, 0:1, :])
            wide(s, 0, west, av)
        else:
            fx = cx[s, 1] * (v0 - west)
        first.append((v0, fx))

    def body(i, carry, at_end):
        out = []
        for s in range(SLOTS):
            here, fx = carry[s]
            nxt = following(v, s, i, n, after(s, 0), at_end)
            av, fnext = plane(s, i, here, fx, nxt, gy[s, pl.ds(i, 1), :])
            emit(s, i, here, av)
            out.append((nxt, fnext))
        return tuple(out)

    last = planes_loop(n, body, tuple(first))
    if wide:
        for s in range(SLOTS):
            here, fx = last[s]
            av, fx = plane(s, n, here, fx, after(s, 1), ends[s, 1:2, :])
            wide(s, 1, here, av)


def apply_slab(yg, v, s, ends, lv, slab):
    n = PLANES[lv]
    zs = 1 << lv
    y = yg[s]
    outer, inner, down, up = slab_sides(y, v, s, ends, n)
    fz = slab[s, 4] * (y - roll(y, zs, 1))
    a = slab[s, 0] * (y - outer) + slab[s, 1] * (y - inner)
    b = slab[s, 2] * (y - down) + slab[s, 3] * (y - up)
    return y, a + b + (fz - roll(fz, 128 - zs, 1))


def sweep_wide(v, xg, yg, ends, gy, lv, w, first, first_x, first_y, out, out_x, out_y):
    rd, slab = w[4:]
    n = PLANES[lv]
    set_near(yg, gy, n)

    def emit(s, i, here, av):
        out[s, i] = here + (first[s, i] - av * rd[s, i + 1])

    def wide(s, e, here, av):
        out_x[s, e] = here + (first_x(s, e) - av * rd[s, (n + 1) * e])

    apply_level(v, lambda s, g: xg[s, 1 - g], lambda s, g: xg[s, 2 + g], gy, ends, lv, w, emit, wide)
    for s in range(SLOTS):
        y, a = apply_slab(yg, v, s, ends, lv, slab)
        out_y[s] = y + (first_y(s) - a * slab[s, 5])


def apply_near(v, gx, yg, gy, lv, w, emit):
    set_near(yg, gy, PLANES[lv])
    apply_level(v, lambda s, g: gx[s, 0], lambda s, g: gx[s, 1], gy, None, lv, w, emit)


def restrict_planes(v, s, lv, scale):
    out = []
    for c in range(PLANES[lv] // 2):
        out.append(pair_sum(v[s, 2 * c] + v[s, 2 * c + 1], lv) * scale)
    return out


def pack_bottom(planes, out):
    lane = lanes()
    at = (lane & 7) * 4
    part = lane >> 3
    top = None
    for s in range(2):
        for i in range(8):
            g = lane_take(planes[s][i], at)
            top = g if top is None else jnp.where(part == s * 8 + i, g, top)
    low = None
    for i in range(8):
        g = lane_take(planes[2][i], at)
        low = g if low is None else jnp.where((part & 7) == i, g, low)
    low = jnp.where(lane < 64, low, roll(low, 4, 0))
    out[0:8, :] = top
    out[8:16, :] = low


PART0, PART1 = Part(0), Part(1)
FIRST = (Part(0), Part(1, 24, 42))
FIRST_NOTES = (33, 60)


def place_of_device():
    dev = lax.axis_index("gx") * 16 + lax.axis_index("gy")
    return dev, 1 - ((dev >> 2) & 1), dev & 3, dev >> 2


def used(count, s):
    return jnp.where(s < count, 1.0, 0.0)


def k_source(count, src, out):
    for s in range(SLOTS):
        out[s] = src[:, s, :].reshape(32, 8, 128) * used(count[0], s)


def k_start(ghost, count, inv, b, b1, faces, gathered, place):
    bottom = []
    dev = place_of_device()[0]
    lane = lanes()
    note = jnp.where(lane == 12, jnp.full((8, 128), count[0]), 0)
    codes = jnp.zeros((8, 128), I32)
    for s in range(SLOTS):
        for f in range(4):
            k = s * 4 + f
            g = ghost[s, f]
            has = g >= 0
            owner = jnp.where(has, (g * 21846) >> 16, dev)
            local = jnp.where(has, g - 3 * owner, 0)
            place[k] = owner
            place[12 + k] = local
            note = jnp.where(lane == k, jnp.full((8, 128), g), note)
            codes = jnp.where(lane == k, jnp.full((8, 128), jnp.where(has, owner * 4 + local, -1)), codes)
    place[24] = dev
    note = note.astype(F32)
    for s in range(SLOTS):
        b[s] = inv[:, s, :].reshape(32, 8, 128)
        for c, t in enumerate(restrict_planes(b, s, 0, 0.125)):
            b1[s, c] = t
        bottom.append(restrict_planes(b1, s, 1, 0.125))
        pack_faces(b, s, FIRST[0], faces)
        pack_faces(b1, s, FIRST[1], faces)
    faces[FIRST_NOTES[0]] = codes.astype(F32)
    pack_bottom(bottom, gathered)
    gathered[16:24, :] = note


def fill_table(win, rows, notes, sem, tab):
    _, even, place, block = place_of_device()
    own, side = FIRST_NOTES
    rows[...] = jnp.zeros((16, 128), I32)
    for m in range(4):
        rows[m : m + 1, :] = win[m][own][0:1].astype(I32)
        for x in range(2):
            rows[4 + 4 * x + m : 5 + 4 * x + m, :] = win[4 + x][side + m][0:1].astype(I32)
    copy = pltpu.make_async_copy(rows, notes, sem)
    copy.start()
    copy.wait()

    def entry(k, code):
        owner = code >> 2
        delta = jnp.where(code >= 0, (owner >> 2) - block, 0)
        m = jnp.where(code >= 0, (owner & 3) ^ place, 0)
        slot = jnp.where(code >= 0, code & 3, 0)
        r = jnp.where(delta == 0, m, jnp.where(delta == 2 * even - 1, 4, 5))
        for x, value in enumerate((r, slot, m, delta, jnp.where(code >= 0, 1, 0))):
            tab[x * BOXES + k] = value
        return jnp.where(r < 4, 0, r - 3) * 4 + m, slot * 4

    for s in range(SLOTS):
        codes = [notes[0, s * 4 + f] for f in range(4)]
        found = [entry(s * 4 + f, codes[f]) for f in range(4)]
        for q, (f, g) in enumerate(TWO_FACES):
            entry(12 + s * 8 + q, jnp.where(codes[f] >= 0, notes[found[f][0], found[f][1] + g], -1))


def k_weights(source, b, *refs):
    win, refs = refs[:6], refs[6:]
    w, u, faces, tab, (xg, yg, ends, gy, rows, notes, sem) = refs[:6], refs[6], refs[7], refs[8], refs[9:]
    fill_table(win, rows, notes, sem, tab)
    take_ghosts(tab, win, FIRST[0], xg, yg, ends)

    def first(s, i, r):
        u[s, i] = source[s, i] * r

    make_weights(b, xg, yg, ends, gy, tab, 0, w, first)
    for s in range(SLOTS):
        pack_faces(u, s, PART0, faces)


def k_weights_next(tab, b1, *refs):
    win, w1, (xg, yg, ends, gy) = refs[:6], refs[6:12], refs[12:]
    take_ghosts(tab, win, FIRST[1], xg, yg, ends)
    make_weights(b1, xg, yg, ends, gy, tab, 1, w1, lambda s, i, r: None)


def k_down(tab, t, u, *refs):
    win, w, rd1 = refs[:6], refs[6:12], refs[12]
    out, out_x, out_y, first_x, first_y, f1, u1, faces, xg, yg, ends, gy, res = refs[13:]
    take_ghosts(tab, win, PART0, xg, yg, ends)
    for s in range(SLOTS):
        for e in range(2):
            first_x[s, e] = xg[s, 1 + e]
        first_y[s] = yg[s]
    sweep_wide(u, xg, yg, ends, gy, 0, w, u, lambda s, e: xg[s, 1 + e], lambda s: yg[s], out, out_x, out_y)

    def emit(s, i, here, av):
        res[s, i] = t[s, i] - av

    apply_near(out, out_x, out_y, gy, 0, w, emit)
    for s in range(SLOTS):
        for c, p in enumerate(restrict_planes(res, s, 0, 0.125)):
            f1[s, c] = p
            u1[s, c] = p * rd1[s, c + 1]
        pack_faces(u1, s, PART1, faces)


def k_bottom_rhs(tab, t, u, beta_rows, *refs):
    win, w = refs[:6], refs[6:12]
    out, out_x, out_y, first_x, first_y, packed, xg, yg, ends, gy, res = refs[12:]
    take_ghosts(tab, win, PART1, xg, yg, ends)
    for s in range(SLOTS):
        for e in range(2):
            first_x[s, e] = xg[s, 1 + e]
        first_y[s] = yg[s]
    sweep_wide(u, xg, yg, ends, gy, 1, w, u, lambda s, e: xg[s, 1 + e], lambda s: yg[s], out, out_x, out_y)

    def emit(s, i, here, av):
        res[s, i] = t[s, i] - av

    apply_near(out, out_x, out_y, gy, 1, w, emit)
    pack_bottom([restrict_planes(res, s, 1, 0.125) for s in range(SLOTS)], packed)
    packed[12:24, :] = beta_rows[0:12, :]
    packed[24:32, :] = beta_rows[16:24, :]


def total(v):
    return jnp.sum(v, axis=(0, 1), keepdims=True)


def unpack_bottom(rows, at, put):
    for r in range(12):
        t = rows[:, at + r, :].T
        for half in range(2):
            s, j = (half, r) if r < 8 else (2, r - 8 + 4 * half)
            for i in range(8):
                put(s, j, i, t[half * 64 + i * 8 : half * 64 + i * 8 + 8, :])


def face_gather(dev_at, slot_at, place):
    out = lane_take(place(0), dev_at)
    for other in range(1, SLOTS):
        out = jnp.where(slot_at == other, lane_take(place(other), dev_at), out)
    return out


def fill_bottom_ghosts(p, at, slot):
    for s in range(SLOTS):
        for f, (src, dst) in enumerate(((7, 0), (0, 9))):
            k = s * 4 + f
            for m in range(1, 9):
                p[s, m, dst] = face_gather(at[k], slot[k], lambda o: p[o, m, src + 1])
            k = s * 4 + 2 + f
            for m in range(1, 9):
                p[s, dst, m] = face_gather(at[k], slot[k], lambda o: p[o, src + 1, m])


def k_bottom(place, mine64, other64, *refs):
    far, (out, faces, boxes_out) = refs[:9], refs[9:12]
    p, r, x, q, cx, cy, cz, back, sq, rows, v1, gx, yg, gy = refs[12:26]
    kept, sem = refs[26:35], refs[35]
    copies = [pltpu.make_async_copy(a, b, sem.at[n]) for n, (a, b) in enumerate(zip(far, kept))]
    for c in copies:
        c.start()
    first, u, gx0, gy0 = kept[:4]
    w1 = kept[4:]
    me = place[24]
    for m in range(64):
        here = me ^ ((m & 15) | ((m >> 4) << 5))
        for half, there in ((mine64, here), (other64, here ^ 16)):
            rows[there] = half[24 * m : 24 * m + 24, :]
            sq[pl.ds(there, 1), :] = half[1536 + m : 1537 + m, :]
    note = sq[...].T
    at, slot, pres = [], [], []
    for f in range(12):
        gf = jnp.broadcast_to(note[f : f + 1, :], (8, 128))
        has = gf >= 0.0
        gf = jnp.where(has, gf, 0.0)
        dv = ((gf + 0.5) * (1.0 / 3.0)).astype(I32)
        at.append(dv)
        slot.append(gf.astype(I32) - 3 * dv)
        pres.append(jnp.where(has, 1.0, 0.0))
    counts = jnp.broadcast_to(note[12:13, :], (8, 128))
    boxes = jnp.sum(counts[0:1], axis=1, keepdims=True)
    boxes_out[...] = jnp.broadcast_to(boxes, (8, 128))

    def fill_ghosts():
        fill_bottom_ghosts(p, at, slot)

    def put_beta(s, j, i, tile):
        p[s, j + 1, i + 1] = tile

    unpack_bottom(rows, 12, put_beta)
    fill_ghosts()
    h = 0.5 * 0.0625
    low = subs() == 0

    def weights(m, _):
        for s in range(SLOTS):
            for i in range(9):
                w = h * (p[s, m + 1, i] + p[s, m + 1, i + 1])
                if i == 0:
                    w = w * pres[s * 4]
                if i == 8:
                    w = w * pres[s * 4 + 1]
                cx[s, m, i] = w
                w = h * (p[s, i, m + 1] + p[s, i + 1, m + 1])
                if i == 0:
                    w = w * pres[s * 4 + 2]
                if i == 8:
                    w = w * pres[s * 4 + 3]
                cy[s, i, m] = w
            for i in range(8):
                b = p[s, m + 1, i + 1]
                cz[s, m, i] = jnp.where(low, 0.0, h * (b + roll(b, 1, 0)))
        return 0

    lax.fori_loop(0, 8, weights, 0)

    def put_rhs(s, j, i, tile):
        r[s, j, i] = tile

    unpack_bottom(rows, 0, put_rhs)

    zero = jnp.zeros((8, 128), F32)

    def each(fn):
        def step(j, acc):
            acc = list(acc)
            for s in range(SLOTS):
                for i in range(8):
                    acc[i] = fn(s, j, i, acc[i])
            return tuple(acc)

        a = lax.fori_loop(0, 8, step, (zero,) * 8, unroll=2)
        a = ((a[0] + a[1]) + (a[2] + a[3])) + ((a[4] + a[5]) + (a[6] + a[7]))
        return jnp.broadcast_to(total(a), (8, 128))

    mean = each(lambda s, j, i, acc: acc + r[s, j, i]) / jnp.broadcast_to(boxes * 512.0, (8, 128))
    valid = [jnp.where(counts > s + 0.5, 1.0, 0.0) for s in range(SLOTS)]

    def shift(s, j, i, acc):
        v = (r[s, j, i] - mean) * valid[s]
        r[s, j, i] = v
        p[s, j + 1, i + 1] = v
        x[s, j, i] = zero
        return acc + v * v

    rr = each(shift)

    def image(s, j, i, acc):
        here = p[s, j + 1, i + 1]
        a = cx[s, j, i] * (here - p[s, j + 1, i]) + cx[s, j, i + 1] * (here - p[s, j + 1, i + 2])
        b = cy[s, j, i] * (here - p[s, j, i + 1]) + cy[s, j + 1, i] * (here - p[s, j + 2, i + 1])
        fz = cz[s, j, i] * (here - roll(here, 1, 0))
        v = a + b + (fz - roll(fz, 7, 0))
        q[s, j, i] = v
        return acc + here * v

    def iteration(it, rr):
        fill_ghosts()
        alpha = rr / each(image)

        def step(s, j, i, acc):
            x[s, j, i] = x[s, j, i] + alpha * p[s, j + 1, i + 1]
            v = r[s, j, i] - alpha * q[s, j, i]
            r[s, j, i] = v
            return acc + v * v

        rr_next = each(step)
        ratio = rr_next / rr

        def turn(j, _):
            for s in range(SLOTS):
                for i in range(8):
                    p[s, j + 1, i + 1] = r[s, j, i] + ratio * p[s, j + 1, i + 1]
            return 0

        lax.fori_loop(0, 8, turn, 0)
        return rr_next

    rr = lax.fori_loop(0, BOTTOM_ITERS - 1, iteration, rr)
    fill_ghosts()
    alpha = rr / each(image)

    for row in range(12):
        for half in range(2):
            s, j = (half, row) if row < 8 else (2, row - 8 + 4 * half)
            for i in range(8):
                sq[half * 64 + i * 8 : half * 64 + i * 8 + 8, :] = x[s, j, i] + alpha * p[s, j + 1, i + 1]
        tr = sq[...].T
        if row < 8:
            back[:, row, :] = tr
            back[:, 8 + row, :] = roll(tr, 64, 1)
        else:
            back[:, 8 + row, :] = tr
            back[:, 12 + row, :] = roll(tr, 64, 1)

    for c in copies:
        c.wait()
    lane, sub = lanes(), subs()
    kat = (lane & 31) >> 2

    def box(dev, s):
        return back[dev, pl.ds(pl.multiple_of(8 * s, 8), 8), :]

    for s in range(SLOTS):
        mine = box(me, s)
        for i in range(8):
            g = lane_take(mine, kat + i * 8)
            v1[s, 2 * i] = u[s, 2 * i] + g
            v1[s, 2 * i + 1] = u[s, 2 * i + 1] + g
        near = [box(place[s * 4 + f], place[12 + s * 4 + f]) for f in range(4)]
        for f, i in ((0, 7), (1, 0)):
            gx[s, f] = gx0[s, f] + lane_take(near[f], kat + i * 8)
        sb = jnp.broadcast_to(near[2][7:8, :], (8, 128))
        nb = jnp.broadcast_to(near[3][0:1, :], (8, 128))
        for part in range(2):
            idx = kat + (part * 4 + (sub >> 1)) * 8
            g = jnp.where(lane < 64, lane_take(sb, idx), lane_take(nb, idx))
            yg[s, 8 * part : 8 * part + 8, :] = gy0[s, 8 * part : 8 * part + 8, :] + g

    def emit(s, i, here, av):
        out[s, i] = here + (first[s, i] - av * w1[4][s, i + 1])

    apply_near(v1, gx, yg, gy, 1, w1, emit)
    for s in range(SLOTS):
        pack_faces(out, s, PART1, faces)


def k_up(tab, first1, first1_x, first1_y, u1, first, u0, u0_x, u0_y, *refs):
    win, w1, w = refs[:6], refs[6:12], refs[12:18]
    out, faces, c, c_x, c_y, xg, yg, ends, gy1, v, gx, y0, gy = refs[18:]
    take_ghosts(tab, win, PART1, xg, yg, ends)
    sweep_wide(u1, xg, yg, ends, gy1, 1, w1, first1, lambda s, e: first1_x[s, e], lambda s: first1_y[s], c, c_x, c_y)
    for s in range(SLOTS):
        for f in range(2):
            gx[s, f] = u0_x[s, f] + c_x[s, f]
        for i in range(16):
            t = c[s, i]
            v[s, 2 * i] = u0[s, 2 * i] + t
            v[s, 2 * i + 1] = u0[s, 2 * i + 1] + t
            y0[s, 2 * i : 2 * i + 2, :] = u0_y[s, 2 * i : 2 * i + 2, :] + c_y[s, i : i + 1, :]

    def emit(s, i, here, av):
        out[s, i] = here + (first[s, i] - av * w[4][s, i + 1])

    apply_near(v, gx, y0, gy, 0, w, emit)
    for s in range(SLOTS):
        pack_faces(out, s, PART0, faces)


def k_residual(tab, t, u, first, first_x, first_y, *refs):
    win, w = refs[:6], refs[6:12]
    out, res_out, sums, out_x, out_y, xg, yg, ends, gy, res = refs[12:]
    take_ghosts(tab, win, PART0, xg, yg, ends)
    sweep_wide(u, xg, yg, ends, gy, 0, w, first, lambda s, e: first_x[s, e], lambda s: first_y[s], out, out_x, out_y)

    def emit(s, i, here, av):
        res[s, i] = t[s, i] - av

    apply_near(out, out_x, out_y, gy, 0, w, emit)
    su = jnp.zeros((8, 128), F32)
    sr = jnp.zeros((8, 128), F32)
    for s in range(SLOTS):
        for i in range(32):
            d = res[s, i]
            sr = sr + d * d
            su = su + out[s, i]
        res_out[:, s, :] = res[s].reshape(256, 128)
    lane = iota((1, 128), 1)
    sums[...] = jnp.where(lane == 0, total(su), jnp.where(lane == 1, total(sr), 0.0))


def k_finish(count, u, sums, boxes, corr, norm):
    tot = jnp.sum(sums[...], axis=0, keepdims=True)
    cells = boxes[0:1, 0:1] * 32768.0
    mean = tot[:, 0:1] / cells
    for s in range(SLOTS):
        corr[:, s, :] = ((u[s] - mean) * used(count[0], s)).reshape(256, 128)
    norm[...] = jnp.broadcast_to(jnp.sqrt(tot[:, 1:2] / cells), (1, 128))


VMEM = pl.BlockSpec(memory_space=pltpu.VMEM)
SMEM = pl.BlockSpec(memory_space=pltpu.SMEM)
HBM = pl.BlockSpec(memory_space=pltpu.HBM)


def call(kernel, smem, args, outs, scratch=(), vmem=16, tables=(), hbm=0, extra=()):
    shape = lambda s: jax.ShapeDtypeStruct(s, F32)
    return pl.pallas_call(
        kernel,
        out_shape=[shape(s) for s in outs] + [jax.ShapeDtypeStruct(s, I32) for s in tables],
        in_specs=[SMEM] * smem + [VMEM] * (len(args) - smem - hbm) + [HBM] * hbm,
        out_specs=[VMEM] * len(outs) + [SMEM] * len(tables),
        scratch_shapes=[pltpu.VMEM(s, F32) for s in scratch] + list(extra),
        compiler_params=pltpu.CompilerParams(vmem_limit_bytes=vmem * 1024 * 1024),
    )(*args)


def swapped(block, pairs):
    route = sorted([(a, b) for a, b in pairs] + [(b, a) for a, b in pairs])
    return lax.ppermute(block, AX, route)


def xor_pairs(m):
    return [(i, i ^ m) for i in range(DEVICES) if i < i ^ m]


def exchange(faces, parts, notes=()):
    got = [faces]
    for m in (1, 2, 3):
        got.append(swapped(faces, xor_pairs(m)))
    tiles = parts[-1].side + parts[-1].side_tiles + (4 if notes else 0)
    sides = call(functools.partial(k_relay, parts, notes), 0, got, [(tiles, 8, 128)] * 2)
    for odd in (0, 1):
        pairs = [(i, i + 4) for i in range(DEVICES - 4) if (i // 4) % 2 == odd]
        got.append(swapped(sides[odd], pairs))
    return tuple(got)


def k_join(*refs):
    out = refs[4]
    each = (out.shape[0] // 100) * 24
    notes = each // 24
    for m in range(4):
        out[m * each : (m + 1) * each, :] = refs[m][0:each, :]
        at = 4 * each + m * notes
        out[at : at + notes, :] = refs[m][each : each + notes, :]


def gather_rows(rows):
    for unit, count in ((1, 104), (4, 400), (32, 1600)):
        got = [rows] + [swapped(rows, xor_pairs(m * unit)) for m in (1, 2, 3)]
        rows = call(k_join, 0, got, [(count, 128)])[0]
    return rows, swapped(rows, xor_pairs(16))


def to_all(rows):
    spread = jnp.broadcast_to(rows[None], (DEVICES,) + rows.shape)
    return lax.all_to_all(spread, AX, 0, 0)


def shards(source_term, inverse_density, box_counts, ghost_from):
    view = lambda a: a.reshape(SLOTS, 256, 128).transpose(1, 0, 2)
    fine, mid = (SLOTS, 32, 8, 128), (SLOTS, 16, 8, 128)
    gx, xg, ends = (SLOTS, 2, 8, 128), (SLOTS, 4, 8, 128), (SLOTS, 8, 128)
    gyf, gym = (SLOTS, 32, 128), (SLOTS, 16, 128)
    face0, face1 = (PART0.own_tiles, 8, 128), (PART1.own_tiles, 8, 128)

    def weight_shapes(n):
        wide = (SLOTS, n + 2, 8, 128)
        return [(SLOTS, n + 3, 8, 128), wide, wide, (SLOTS, n + 2, 128), wide, (SLOTS, 6, n, 128)]

    beta, beta1, faces, beta_rows, place = call(
        k_start, 2, (ghost_from, box_counts, view(inverse_density)),
        [fine, mid, (FIRST_NOTES[0] + 1, 8, 128), (24, 128)], tables=[(25,)],
    )
    later, faces = lax.optimization_barrier((view(source_term), faces))
    source = call(k_source, 1, (box_counts, later), [fine])[0]
    win = exchange(faces, FIRST, FIRST_NOTES)
    outs = call(
        k_weights, 0, (source, beta) + win, weight_shapes(32) + [fine, face0], [xg, gyf, ends, gyf],
        tables=[(5 * BOXES,)],
        extra=[pltpu.VMEM((16, 128), I32), pltpu.SMEM((16, 128), I32), pltpu.SemaphoreType.DMA],
    )
    w, (first, faces, tab) = tuple(outs[:6]), outs[6:]
    w1 = tuple(call(k_weights_next, 1, (tab, beta1) + win, weight_shapes(16), [xg, gym, ends, gym]))
    u, u_x, u_y, first_x, first_y, f1, first1, faces = call(
        k_down, 1, (tab, source, first) + exchange(faces, [PART0]) + w + (w1[4],),
        [fine, gx, gyf, gx, gyf, mid, mid, face1], [xg, gyf, ends, gyf, fine],
    )
    u1, u1_x, u1_y, first1_x, first1_y, rows = call(
        k_bottom_rhs, 1, (tab, f1, first1, beta_rows) + exchange(faces, [PART1]) + w1,
        [mid, gx, gym, gx, gym, (32, 128)], [xg, gym, ends, gym, mid],
    )
    cube, padded = (SLOTS, 8, 8, 8, 128), (SLOTS, 10, 10, 8, 128)
    kept = [first1, u1, u1_x, u1_y] + list(w1[:5])
    u1, faces, boxes = call(
        k_bottom, 1, (place,) + gather_rows(rows) + tuple(kept), [mid, face1, (8, 128)],
        [padded, cube, cube, cube, (SLOTS, 8, 9, 8, 128), (SLOTS, 9, 8, 8, 128), cube, (DEVICES, 24, 128),
         (128, 128), (DEVICES, 24, 128), mid, gx, gym, gym] + [a.shape for a in kept],
        hbm=len(kept), extra=[pltpu.SemaphoreType.DMA((len(kept),))],
    )
    u, faces = call(
        k_up, 1,
        (tab, first1, first1_x, first1_y, u1, first, u, u_x, u_y) + exchange(faces, [PART1]) + w1 + w,
        [fine, face0], [mid, gx, gym, xg, gym, ends, gym, fine, gx, gyf, gyf],
    )
    u, residual, sums = call(
        k_residual, 1, (tab, source, u, first, first_x, first_y) + exchange(faces, [PART0]) + w,
        [fine, (256, SLOTS, 128), (1, 128)], [gx, gyf, xg, gyf, ends, gyf, fine],
    )
    parts = to_all(sums).reshape(DEVICES, 128)
    correction, norm = call(k_finish, 1, (box_counts, u, parts, boxes), [(256, SLOTS, 128), (1, 128)])
    back = lambda a: a.transpose(1, 0, 2).reshape(SLOTS, 32768)
    return back(correction), back(residual), norm[0, 0]


def solution(mesh):
    rows = P(AX, None)
    return jax.shard_map(
        shards, mesh=mesh, in_specs=(rows, rows, P(AX), rows), out_specs=(rows, rows, P()), check_vma=False
    )
```

```python
import functools

import jax
import jax.numpy as jnp
from jax import lax
from jax.experimental import pallas as pl
from jax.experimental.pallas import tpu as pltpu
from jax.sharding import PartitionSpec as P

AX = ("gx", "gy")
DEVICES = 128
SLOTS = 3
BOTTOM_ITERS = 8
RELAXATION = 2.0 / 3.0
F32 = jnp.float32
I32 = jnp.int32

PLANES = (32, 16)


def iota(shape, dim):
    return lax.broadcasted_iota(I32, shape, dim)


def lanes():
    return iota((8, 128), 1)


def subs():
    return iota((8, 128), 0)


def roll(x, shift, axis):
    return pltpu.roll(x, shift, axis)


def lane_take(x, at):
    return jnp.take_along_axis(x, at, axis=1, mode="promise_in_bounds")


class Tile:
    def __init__(self, lv):
        self.zs, self.ys = 1 << lv, 32 << lv
        lane, sub = lanes(), subs()
        self.south_in = lane >= self.ys
        self.north_in = lane < 128 - self.ys
        self.first_row = sub == 0
        self.last_row = sub == 7
        self.south_edge = self.first_row & (lane < self.ys)
        self.z_low = (lane & 31) < self.zs

    def south(self, v, row):
        r = roll(v, self.ys, 1)
        return jnp.where(self.south_in, r, jnp.where(self.first_row, row, roll(r, 1, 0)))

    def north(self, v, edge):
        r = roll(v, 128 - self.ys, 1)
        return jnp.where(self.north_in, r, jnp.where(self.last_row, edge, roll(r, 7, 0)))

    def below(self, v):
        return roll(v, self.zs, 1)

    def above(self, v):
        return roll(v, 128 - self.zs, 1)


def pair_sum(t, lv):
    lane = lanes()
    zs, ys = 1 << lv, 32 << lv
    t = t + jnp.where((lane & zs) == 0, roll(t, 128 - zs, 1), roll(t, zs, 1))
    return t + jnp.where((lane & ys) == 0, roll(t, 128 - ys, 1), roll(t, ys, 1))


BOXES = 36
TWO_FACES = ((0, 2), (0, 3), (1, 2), (1, 3), (2, 0), (2, 1), (3, 0), (3, 1))


class Part:
    def __init__(self, lv, own=0, side=0):
        self.lv, self.own, self.side = lv, own, side
        self.tiles = (8, 3)[lv]
        self.ys = (4, 1)[lv]
        self.own_tiles = SLOTS * self.tiles
        self.side_tiles = (42, 18)[lv]


def pack_faces(v, s, part, out):
    lv = part.lv
    n = PLANES[lv]
    base = part.own + s * part.tiles
    planes = [v[s, 0], v[s, 1], v[s, n - 2], v[s, n - 1]]
    y0 = v[s, :, 0, :]
    y7 = v[s, :, 7, :]
    lane = iota((n, 128), 1)
    if lv == 0:
        for m in range(4):
            out[base + m] = planes[m]
        q = roll(jnp.where(lane >= 64, y7, y0), 64, 1)
    else:
        odd_k, odd_j = (lanes() & 1) == 1, (lanes() & 32) == 32
        out[base] = jnp.where(
            odd_k, jnp.where(odd_j, planes[3], planes[2]), jnp.where(odd_j, planes[1], planes[0])
        )
        q = jnp.where(
            lane < 32, y7, jnp.where(lane < 64, roll(y7, 96, 1), jnp.where(lane < 96, roll(y0, 64, 1), y0))
        )
    for t in range(n // 8):
        out[base + part.ys + t] = q[8 * t : 8 * t + 8]


def k_relay(parts, notes, *refs):
    got, (near, far) = refs[:4], refs[4:]
    _, even, place, _ = place_of_device()
    even = even == 1

    def of(m, t):
        low = jnp.where((m & 1) == 0, got[0][t], got[1][t])
        high = jnp.where((m & 1) == 0, got[2][t], got[3][t])
        return jnp.where(m < 2, low, high)

    def put(at, fwd, bwd):
        near[at] = jnp.where(even, fwd, bwd)
        far[at] = jnp.where(even, bwd, fwd)

    for part in parts:
        for s in range(SLOTS):
            base = part.own + s * part.tiles
            for m in range(4):
                box = m * SLOTS + s
                if part.lv == 0:
                    for x in range(2):
                        put(part.side + box * 2 + x, got[m][base + 2 + x], got[m][base + x])
                else:
                    put(part.side + box, got[m][base], got[m][base])
            if part.lv == 0:
                for x in range(2):
                    put(part.side + 24 + s * 6 + x, of(place ^ 3, base + x), of(place, base + 2 + x))
            for t in range(part.tiles - part.ys):
                at = part.side + (24 + s * 6 + 2 + t if part.lv == 0 else 12 + s * 2 + t)
                put(at, of(place ^ 3, base + part.ys + t), of(place, base + part.ys + t))
    if notes:
        own, side = notes
        for m in range(4):
            near[side + m] = got[m][own]
            far[side + m] = got[m][own]


def pick(tab, win, k, own, side):
    r = tab[k]
    low = jnp.where((r & 1) == 0, win[0][own], win[1][own])
    high = jnp.where((r & 1) == 0, win[2][own], win[3][own])
    beside = jnp.where((r & 1) == 0, win[4][side], win[5][side])
    return jnp.where(r < 4, jnp.where(r < 2, low, high), beside)


def pick_plane(tab, win, k, part, p):
    slot, m, delta = tab[BOXES + k], tab[2 * BOXES + k], tab[3 * BOXES + k]
    own = part.own + slot * part.tiles
    box = m * SLOTS + slot
    if part.lv == 0:
        x = p & 1
        direct = -1 if p >= 2 else 1
        side = part.side + jnp.where(delta == direct, box * 2 + x, 24 + slot * 6 + x)
        return pick(tab, win, k, own + p, side)
    lane = lanes()
    t = pick(tab, win, k, own, part.side + box)
    t = jnp.where(((lane & 1) == p >> 1) & ((lane & 32) == (p & 1) * 32), t, 0.0)
    return pair_sum(t, 0)


def pick_rows(tab, win, k, part, t):
    slot = tab[BOXES + k]
    own = part.own + slot * part.tiles + part.ys + t
    side = part.side + (24 + slot * 6 + 2 + t if part.lv == 0 else 12 + slot * 2 + t)
    return pick(tab, win, k, own, side)


def near_rows(y):
    lane = iota(y.shape, 1)
    return jnp.where(lane < 32, roll(y, 96, 1), jnp.where(lane < 96, y, roll(y, 32, 1)))


def take_ghosts(tab, win, part, xg, yg, ends):
    ys = 32 << part.lv
    low = iota((1, 128), 1) < 64
    for s in range(SLOTS):
        for g, (f, p) in enumerate(((0, 2), (0, 3), (1, 0), (1, 1))):
            xg[s, g] = pick_plane(tab, win, s * 4 + f, part, p)
        for t in range(part.tiles - part.ys):
            sv = pick_rows(tab, win, s * 4 + 2, part, t)
            nv = pick_rows(tab, win, s * 4 + 3, part, t)
            yg[s, 8 * t : 8 * t + 8, :] = jnp.where(lanes() < 64, sv, nv)

        def corner(q, p):
            return pick_plane(tab, win, 12 + s * 8 + q, part, p)

        for e, p in ((0, 3), (1, 0)):
            sp = corner(2 * e, p)[7:8]
            np = corner(2 * e + 1, p)[0:1]
            ends[s, e : e + 1, :] = jnp.where(low, roll(sp, ys, 1), roll(np, 128 - ys, 1))
            sp = corner(4 + e, p)[7:8]
            np = corner(6 + e, p)[0:1]
            ends[s, 2 + e : 3 + e, :] = jnp.where(low, roll(sp, 64, 1), roll(np, 64, 1))


def set_near(yg, gy, n):
    for s in range(SLOTS):
        for t in range(n // 8):
            gy[s, 8 * t : 8 * t + 8, :] = near_rows(yg[s, 8 * t : 8 * t + 8, :])


def planes_loop(n, body, carry, unroll=8):
    def chunk(c, carry):
        for u in range(unroll):
            carry = body(c * unroll + u, carry, u == unroll - 1)
        return carry

    return lax.fori_loop(0, n // unroll, chunk, carry)


def following(ref, s, i, n, edge, at_end):
    if not at_end:
        return ref[s, i + 1]
    return jnp.where(i == n - 1, edge, ref[s, jnp.minimum(i + 1, n - 1)])


def slab_sides(y, v, s, ends, n):
    lane = iota((n, 128), 1)
    row = iota((n, 128), 0)
    inner = jnp.where(lane < 64, roll(v[s, :, 0, :], 32, 1), roll(v[s, :, 7, :], 96, 1))
    outer = jnp.where(lane < 64, roll(y, 32, 1), roll(y, 96, 1))
    down = jnp.where(row == 0, ends[s, 2:3, :], roll(y, 1, 0))
    up = jnp.where(row == n - 1, ends[s, 3:4, :], roll(y, n - 1, 0))
    return outer, inner, down, up


def make_weights(b, xg, yg, ends, gy, tab, lv, w, extra):
    cx, cy, cz, wn, rd, slab = w
    n = PLANES[lv]
    h = 0.5 * 0.25**lv
    tl = Tile(lv)
    set_near(yg, gy, n)

    def has(k):
        return jnp.where(tab[4 * BOXES + k] == 1, 1.0, 0.0)

    def plane(s, i, here, w, nxt, wnext, row, south, north):
        wy = h * (here + tl.south(here, row))
        wy = jnp.where(tl.south_edge, wy * south, wy)
        wrow = h * (here + row) * north
        wz = jnp.where(tl.z_low, 0.0, h * (here + tl.below(here)))
        d = (w + wnext) + (wy + tl.north(wy, wrow)) + (wz + tl.above(wz))
        r = RELAXATION / d
        cx[s, i + 2] = wnext
        cy[s, i + 1] = wy
        cz[s, i + 1] = wz
        wn[s, pl.ds(i + 1, 1), :] = wrow[7:8, :]
        rd[s, i + 1] = r
        return r

    first = []
    for s in range(SLOTS):
        here, v = xg[s, 1], b[s, 0]
        w = h * (here + xg[s, 0])
        cx[s, 0] = w
        wnext = h * (here + v) * has(s * 4)
        plane(s, -1, here, w, v, wnext, ends[s, 0:1, :], has(12 + s * 8), has(13 + s * 8))
        first.append((v, wnext))

    def body(i, carry, at_end):
        out = []
        for s in range(SLOTS):
            v, w = carry[s]
            nxt = following(b, s, i, n, xg[s, 2], at_end)
            wnext = h * (v + nxt)
            if at_end:
                wnext = wnext * jnp.where(i == n - 1, has(s * 4 + 1), 1.0)
            r = plane(s, i, v, w, nxt, wnext, gy[s, pl.ds(i, 1), :], has(s * 4 + 2), has(s * 4 + 3))
            extra(s, i, r)
            out.append((nxt, wnext))
        return tuple(out)

    last = planes_loop(n, body, tuple(first))
    lane = iota((n, 128), 1)
    row = iota((n, 128), 0)
    for s in range(SLOTS):
        here, w = last[s]
        far = xg[s, 3]
        plane(s, n, here, w, far, h * (here + far), ends[s, 1:2, :], has(14 + s * 8), has(15 + s * 8))
        y = yg[s]
        outer, inner, down, up = (h * (y + t) for t in slab_sides(y, b, s, ends, n))
        k = 12 + s * 8
        down = down * jnp.where(row == 0, jnp.where(lane < 64, has(k + 4), has(k + 6)), 1.0)
        up = up * jnp.where(row == n - 1, jnp.where(lane < 64, has(k + 5), has(k + 7)), 1.0)
        zs = tl.zs
        wz = jnp.where((lane & 31) < zs, 0.0, h * (y + roll(y, zs, 1)))
        d = (outer + inner) + (down + up) + (wz + roll(wz, 128 - zs, 1))
        for m, t in enumerate((outer, inner, down, up, wz, RELAXATION / d)):
            slab[s, m] = t


def apply_level(v, before, after, gy, ends, lv, w, emit, wide=None, unroll=8):
    cx, cy, cz, wn = w[:4]
    n = PLANES[lv]
    tl = Tile(lv)

    def plane(s, i, here, fx, nxt, row):
        fnext = cx[s, i + 2] * (nxt - here)
        wrow = wn[s, pl.ds(i + 1, 1), :]
        fy = cy[s, i + 1] * (here - tl.south(here, row))
        fn = tl.north(fy, wrow * (row - here))
        fz = cz[s, i + 1] * (here - tl.below(here))
        return (fx - fnext) + (fy - fn) + (fz - tl.above(fz)), fnext

    first = []
    for s in range(SLOTS):
        v0, west = v[s, 0], before(s, 0)
        if wide:
            fx = cx[s, 0] * (west - before(s, 1))
            av, fx = plane(s, -1, west, fx, v0, ends[s, 0:1, :])
            wide(s, 0, west, av)
        else:
            fx = cx[s, 1] * (v0 - west)
        first.append((v0, fx))

    def body(i, carry, at_end):
        out = []
        for s in range(SLOTS):
            here, fx = carry[s]
            nxt = following(v, s, i, n, after(s, 0), at_end)
            av, fnext = plane(s, i, here, fx, nxt, gy[s, pl.ds(i, 1), :])
            emit(s, i, here, av)
            out.append((nxt, fnext))
        return tuple(out)

    last = planes_loop(n, body, tuple(first), unroll)
    if wide:
        for s in range(SLOTS):
            here, fx = last[s]
            av, fx = plane(s, n, here, fx, after(s, 1), ends[s, 1:2, :])
            wide(s, 1, here, av)


def apply_slab(yg, v, s, ends, lv, slab):
    n = PLANES[lv]
    zs = 1 << lv
    y = yg[s]
    outer, inner, down, up = slab_sides(y, v, s, ends, n)
    fz = slab[s, 4] * (y - roll(y, zs, 1))
    a = slab[s, 0] * (y - outer) + slab[s, 1] * (y - inner)
    b = slab[s, 2] * (y - down) + slab[s, 3] * (y - up)
    return y, a + b + (fz - roll(fz, 128 - zs, 1))


def sweep_wide(v, xg, yg, ends, gy, lv, w, first, first_x, first_y, out, out_x, out_y, unroll=8):
    rd, slab = w[4:]
    n = PLANES[lv]
    set_near(yg, gy, n)

    def emit(s, i, here, av):
        out[s, i] = here + (first[s, i] - av * rd[s, i + 1])

    def wide(s, e, here, av):
        out_x[s, e] = here + (first_x(s, e) - av * rd[s, (n + 1) * e])

    apply_level(v, lambda s, g: xg[s, 1 - g], lambda s, g: xg[s, 2 + g], gy, ends, lv, w, emit, wide, unroll)
    for s in range(SLOTS):
        y, a = apply_slab(yg, v, s, ends, lv, slab)
        out_y[s] = y + (first_y(s) - a * slab[s, 5])


def apply_near(v, gx, yg, gy, lv, w, emit, unroll=8):
    set_near(yg, gy, PLANES[lv])
    apply_level(v, lambda s, g: gx[s, 0], lambda s, g: gx[s, 1], gy, None, lv, w, emit, None, unroll)


def restrict_planes(v, s, lv, scale):
    out = []
    for c in range(PLANES[lv] // 2):
        out.append(pair_sum(v[s, 2 * c] + v[s, 2 * c + 1], lv) * scale)
    return out


def pack_bottom(planes, out):
    lane = lanes()
    at = (lane & 7) * 4
    part = lane >> 3
    top = None
    for s in range(2):
        for i in range(8):
            g = lane_take(planes[s][i], at)
            top = g if top is None else jnp.where(part == s * 8 + i, g, top)
    low = None
    for i in range(8):
        g = lane_take(planes[2][i], at)
        low = g if low is None else jnp.where((part & 7) == i, g, low)
    low = jnp.where(lane < 64, low, roll(low, 4, 0))
    out[0:8, :] = top
    out[8:16, :] = low


PART0, PART1 = Part(0), Part(1)
FIRST = (Part(0), Part(1, 24, 42))
FIRST_NOTES = (33, 60)


def place_of_device():
    dev = lax.axis_index("gx") * 16 + lax.axis_index("gy")
    return dev, 1 - ((dev >> 2) & 1), dev & 3, dev >> 2


def used(count, s):
    return jnp.where(s < count, 1.0, 0.0)


def k_source(count, src, out):
    for s in range(SLOTS):
        out[s] = src[:, s, :].reshape(32, 8, 128) * used(count[0], s)


def k_bottom_beta(ghost, count, b1, out):
    lane = lanes()
    note = jnp.where(lane == 12, jnp.full((8, 128), count[0]), 0)
    for s in range(SLOTS):
        for f in range(4):
            note = jnp.where(lane == s * 4 + f, jnp.full((8, 128), ghost[s, f]), note)
    pack_bottom([restrict_planes(b1, s, 1, 0.125) for s in range(SLOTS)], out)
    out[16:24, :] = note.astype(F32)


def k_start(ghost, inv, b, b1, faces, place):
    dev = place_of_device()[0]
    lane = lanes()
    codes = jnp.zeros((8, 128), I32)
    for s in range(SLOTS):
        for f in range(4):
            k = s * 4 + f
            g = ghost[s, f]
            has = g >= 0
            owner = jnp.where(has, (g * 21846) >> 16, dev)
            local = jnp.where(has, g - 3 * owner, 0)
            place[k] = owner
            place[12 + k] = local
            codes = jnp.where(lane == k, jnp.full((8, 128), jnp.where(has, owner * 4 + local, -1)), codes)
    place[24] = dev
    for s in range(SLOTS):
        b[s] = inv[:, s, :].reshape(32, 8, 128)
        for c, t in enumerate(restrict_planes(b, s, 0, 0.125)):
            b1[s, c] = t
        pack_faces(b, s, FIRST[0], faces)
        pack_faces(b1, s, FIRST[1], faces)
    faces[FIRST_NOTES[0]] = codes.astype(F32)


def fill_table(win, rows, notes, sem, tab):
    _, even, place, block = place_of_device()
    own, side = FIRST_NOTES
    rows[...] = jnp.zeros((16, 128), I32)
    for m in range(4):
        rows[m : m + 1, :] = win[m][own][0:1].astype(I32)
        for x in range(2):
            rows[4 + 4 * x + m : 5 + 4 * x + m, :] = win[4 + x][side + m][0:1].astype(I32)
    copy = pltpu.make_async_copy(rows, notes, sem)
    copy.start()
    copy.wait()

    def entry(k, code):
        owner = code >> 2
        delta = jnp.where(code >= 0, (owner >> 2) - block, 0)
        m = jnp.where(code >= 0, (owner & 3) ^ place, 0)
        slot = jnp.where(code >= 0, code & 3, 0)
        r = jnp.where(delta == 0, m, jnp.where(delta == 2 * even - 1, 4, 5))
        for x, value in enumerate((r, slot, m, delta, jnp.where(code >= 0, 1, 0))):
            tab[x * BOXES + k] = value
        return jnp.where(r < 4, 0, r - 3) * 4 + m, slot * 4

    for s in range(SLOTS):
        codes = [notes[0, s * 4 + f] for f in range(4)]
        found = [entry(s * 4 + f, codes[f]) for f in range(4)]
        for q, (f, g) in enumerate(TWO_FACES):
            entry(12 + s * 8 + q, jnp.where(codes[f] >= 0, notes[found[f][0], found[f][1] + g], -1))


def k_weights(source, b, *refs):
    win, refs = refs[:6], refs[6:]
    w, u, faces, tab, (xg, yg, ends, gy, rows, notes, sem) = refs[:6], refs[6], refs[7], refs[8], refs[9:]
    fill_table(win, rows, notes, sem, tab)
    take_ghosts(tab, win, FIRST[0], xg, yg, ends)

    def first(s, i, r):
        u[s, i] = source[s, i] * r

    make_weights(b, xg, yg, ends, gy, tab, 0, w, first)
    for s in range(SLOTS):
        pack_faces(u, s, PART0, faces)


def k_weights_next(tab, b1, *refs):
    win, w1, (xg, yg, ends, gy) = refs[:6], refs[6:12], refs[12:]
    take_ghosts(tab, win, FIRST[1], xg, yg, ends)
    make_weights(b1, xg, yg, ends, gy, tab, 1, w1, lambda s, i, r: None)


def k_down(tab, t, u, *refs):
    win, w, rd1 = refs[:6], refs[6:12], refs[12]
    out, out_x, out_y, first_x, first_y, f1, u1, faces, xg, yg, ends, gy, res = refs[13:]
    take_ghosts(tab, win, PART0, xg, yg, ends)
    for s in range(SLOTS):
        for e in range(2):
            first_x[s, e] = xg[s, 1 + e]
        first_y[s] = yg[s]
    sweep_wide(u, xg, yg, ends, gy, 0, w, u, lambda s, e: xg[s, 1 + e], lambda s: yg[s], out, out_x, out_y)

    def emit(s, i, here, av):
        res[s, i] = t[s, i] - av

    apply_near(out, out_x, out_y, gy, 0, w, emit)
    for s in range(SLOTS):
        for c, p in enumerate(restrict_planes(res, s, 0, 0.125)):
            f1[s, c] = p
            u1[s, c] = p * rd1[s, c + 1]
        pack_faces(u1, s, PART1, faces)


def k_bottom_rhs(tab, t, u, beta_rows, *refs):
    win, w = refs[:6], refs[6:12]
    out, out_x, out_y, first_x, first_y, packed, xg, yg, ends, gy, res = refs[12:]
    take_ghosts(tab, win, PART1, xg, yg, ends)
    for s in range(SLOTS):
        for e in range(2):
            first_x[s, e] = xg[s, 1 + e]
        first_y[s] = yg[s]
    sweep_wide(u, xg, yg, ends, gy, 1, w, u, lambda s, e: xg[s, 1 + e], lambda s: yg[s], out, out_x, out_y)

    def emit(s, i, here, av):
        res[s, i] = t[s, i] - av

    apply_near(out, out_x, out_y, gy, 1, w, emit)
    pack_bottom([restrict_planes(res, s, 1, 0.125) for s in range(SLOTS)], packed)
    packed[12:24, :] = beta_rows[0:12, :]
    packed[24:32, :] = beta_rows[16:24, :]


def total(v):
    return jnp.sum(v, axis=(0, 1), keepdims=True)


def unpack_bottom(rows, at, put):
    for r in range(12):
        t = rows[:, at + r, :].T
        for half in range(2):
            s, j = (half, r) if r < 8 else (2, r - 8 + 4 * half)
            for i in range(8):
                put(s, j, i, t[half * 64 + i * 8 : half * 64 + i * 8 + 8, :])


def face_gather(dev_at, slot_at, place):
    out = lane_take(place(0), dev_at)
    for other in range(1, SLOTS):
        out = jnp.where(slot_at == other, lane_take(place(other), dev_at), out)
    return out


def fill_bottom_ghosts(p, at, slot):
    for s in range(SLOTS):
        for f, (src, dst) in enumerate(((7, 0), (0, 9))):
            k = s * 4 + f
            for m in range(1, 9):
                p[s, m, dst] = face_gather(at[k], slot[k], lambda o: p[o, m, src + 1])
            k = s * 4 + 2 + f
            for m in range(1, 9):
                p[s, dst, m] = face_gather(at[k], slot[k], lambda o: p[o, src + 1, m])


def k_bottom(place, mine64, other64, *refs):
    far, (out, faces, boxes_out) = refs[:9], refs[9:12]
    p, r, x, q, cx, cy, cz, back, sq, rows, v1, gx, yg, gy = refs[12:26]
    kept, sem = refs[26:35], refs[35]
    copies = [pltpu.make_async_copy(a, b, sem.at[n]) for n, (a, b) in enumerate(zip(far, kept))]
    for c in copies:
        c.start()
    first, u, gx0, gy0 = kept[:4]
    w1 = kept[4:]
    me = place[24]
    for m in range(64):
        here = me ^ ((m & 15) | ((m >> 4) << 5))
        for half, there in ((mine64, here), (other64, here ^ 16)):
            rows[there] = half[24 * m : 24 * m + 24, :]
            sq[pl.ds(there, 1), :] = half[1536 + m : 1537 + m, :]
    note = sq[...].T
    at, slot, pres = [], [], []
    for f in range(12):
        gf = jnp.broadcast_to(note[f : f + 1, :], (8, 128))
        has = gf >= 0.0
        gf = jnp.where(has, gf, 0.0)
        dv = ((gf + 0.5) * (1.0 / 3.0)).astype(I32)
        at.append(dv)
        slot.append(gf.astype(I32) - 3 * dv)
        pres.append(jnp.where(has, 1.0, 0.0))
    counts = jnp.broadcast_to(note[12:13, :], (8, 128))
    boxes = jnp.sum(counts[0:1], axis=1, keepdims=True)
    boxes_out[...] = jnp.broadcast_to(boxes, (8, 128))

    def fill_ghosts():
        fill_bottom_ghosts(p, at, slot)

    def put_beta(s, j, i, tile):
        p[s, j + 1, i + 1] = tile

    unpack_bottom(rows, 12, put_beta)
    fill_ghosts()
    h = 0.5 * 0.0625
    low = subs() == 0

    def weights(m, _):
        for s in range(SLOTS):
            for i in range(9):
                w = h * (p[s, m + 1, i] + p[s, m + 1, i + 1])
                if i == 0:
                    w = w * pres[s * 4]
                if i == 8:
                    w = w * pres[s * 4 + 1]
                cx[s, m, i] = w
                w = h * (p[s, i, m + 1] + p[s, i + 1, m + 1])
                if i == 0:
                    w = w * pres[s * 4 + 2]
                if i == 8:
                    w = w * pres[s * 4 + 3]
                cy[s, i, m] = w
            for i in range(8):
                b = p[s, m + 1, i + 1]
                cz[s, m, i] = jnp.where(low, 0.0, h * (b + roll(b, 1, 0)))
        return 0

    lax.fori_loop(0, 8, weights, 0, unroll=8)

    def put_rhs(s, j, i, tile):
        r[s, j, i] = tile

    unpack_bottom(rows, 0, put_rhs)

    zero = jnp.zeros((8, 128), F32)

    def whole(a):
        a = ((a[0] + a[1]) + (a[2] + a[3])) + ((a[4] + a[5]) + (a[6] + a[7]))
        for sh in (4, 2, 1):
            a = a + roll(a, sh, 0)
        return jnp.broadcast_to(jnp.sum(a, axis=1, keepdims=True), (8, 128))

    def each(fn):
        def step(j, acc):
            acc = list(acc)
            for s in range(SLOTS):
                for i in range(8):
                    acc[i] = fn(s, j, i, acc[i])
            return tuple(acc)

        return whole(lax.fori_loop(0, 8, step, (zero,) * 8, unroll=8))

    mean = each(lambda s, j, i, acc: acc + r[s, j, i]) / jnp.broadcast_to(boxes * 512.0, (8, 128))
    valid = [jnp.where(counts > s + 0.5, 1.0, 0.0) for s in range(SLOTS)]

    def shift(s, j, i, acc):
        v = (r[s, j, i] - mean) * valid[s]
        r[s, j, i] = v
        p[s, j + 1, i + 1] = v
        x[s, j, i] = zero
        return acc + v * v

    rr = each(shift)

    def image():
        def step(j, acc):
            acc = list(acc)
            for s in range(SLOTS):
                here = p[s, j + 1, 1]
                fx = cx[s, j, 0] * (here - p[s, j + 1, 0])
                for i in range(8):
                    nxt = p[s, j + 1, i + 2]
                    fnext = cx[s, j, i + 1] * (nxt - here)
                    b = cy[s, j, i] * (here - p[s, j, i + 1]) + cy[s, j + 1, i] * (here - p[s, j + 2, i + 1])
                    fz = cz[s, j, i] * (here - roll(here, 1, 0))
                    v = (fx - fnext) + b + (fz - roll(fz, 7, 0))
                    q[s, j, i] = v
                    acc[i] = acc[i] + here * v
                    here, fx = nxt, fnext
            return tuple(acc)

        return whole(lax.fori_loop(0, 8, step, (zero,) * 8, unroll=8))

    def iteration(it, rr):
        fill_ghosts()
        alpha = rr / image()

        def step(s, j, i, acc):
            x[s, j, i] = x[s, j, i] + alpha * p[s, j + 1, i + 1]
            v = r[s, j, i] - alpha * q[s, j, i]
            r[s, j, i] = v
            return acc + v * v

        rr_next = each(step)
        ratio = rr_next / rr

        def turn(j, _):
            for s in range(SLOTS):
                for i in range(8):
                    p[s, j + 1, i + 1] = r[s, j, i] + ratio * p[s, j + 1, i + 1]
            return 0

        lax.fori_loop(0, 8, turn, 0, unroll=8)
        return rr_next

    rr = lax.fori_loop(0, BOTTOM_ITERS - 1, iteration, rr)
    fill_ghosts()
    alpha = rr / image()

    for row in range(12):
        for half in range(2):
            s, j = (half, row) if row < 8 else (2, row - 8 + 4 * half)
            for i in range(8):
                sq[half * 64 + i * 8 : half * 64 + i * 8 + 8, :] = x[s, j, i] + alpha * p[s, j + 1, i + 1]
        tr = sq[...].T
        if row < 8:
            back[:, row, :] = tr
            back[:, 8 + row, :] = roll(tr, 64, 1)
        else:
            back[:, 8 + row, :] = tr
            back[:, 12 + row, :] = roll(tr, 64, 1)

    for c in copies:
        c.wait()
    lane, sub = lanes(), subs()
    kat = (lane & 31) >> 2

    def box(dev, s):
        return back[dev, pl.ds(pl.multiple_of(8 * s, 8), 8), :]

    for s in range(SLOTS):
        mine = box(me, s)
        for i in range(8):
            g = lane_take(mine, kat + i * 8)
            v1[s, 2 * i] = u[s, 2 * i] + g
            v1[s, 2 * i + 1] = u[s, 2 * i + 1] + g
        near = [box(place[s * 4 + f], place[12 + s * 4 + f]) for f in range(4)]
        for f, i in ((0, 7), (1, 0)):
            gx[s, f] = gx0[s, f] + lane_take(near[f], kat + i * 8)
        sb = jnp.broadcast_to(near[2][7:8, :], (8, 128))
        nb = jnp.broadcast_to(near[3][0:1, :], (8, 128))
        for part in range(2):
            idx = kat + (part * 4 + (sub >> 1)) * 8
            g = jnp.where(lane < 64, lane_take(sb, idx), lane_take(nb, idx))
            yg[s, 8 * part : 8 * part + 8, :] = gy0[s, 8 * part : 8 * part + 8, :] + g

    def emit(s, i, here, av):
        out[s, i] = here + (first[s, i] - av * w1[4][s, i + 1])

    apply_near(v1, gx, yg, gy, 1, w1, emit)
    for s in range(SLOTS):
        pack_faces(out, s, PART1, faces)


def k_up(tab, first1, first1_x, first1_y, u1, first, u0, u0_x, u0_y, *refs):
    win, w1, w = refs[:6], refs[6:12], refs[12:18]
    out, faces, c, c_x, c_y, xg, yg, ends, gy1, v, gx, y0, gy = refs[18:]
    take_ghosts(tab, win, PART1, xg, yg, ends)
    sweep_wide(u1, xg, yg, ends, gy1, 1, w1, first1, lambda s, e: first1_x[s, e], lambda s: first1_y[s], c, c_x, c_y)
    for s in range(SLOTS):
        for f in range(2):
            gx[s, f] = u0_x[s, f] + c_x[s, f]
        for i in range(16):
            t = c[s, i]
            v[s, 2 * i] = u0[s, 2 * i] + t
            v[s, 2 * i + 1] = u0[s, 2 * i + 1] + t
            y0[s, 2 * i : 2 * i + 2, :] = u0_y[s, 2 * i : 2 * i + 2, :] + c_y[s, i : i + 1, :]

    def emit(s, i, here, av):
        out[s, i] = here + (first[s, i] - av * w[4][s, i + 1])

    apply_near(v, gx, y0, gy, 0, w, emit)
    for s in range(SLOTS):
        pack_faces(out, s, PART0, faces)


def k_residual(tab, t, u, first, first_x, first_y, *refs):
    win, w = refs[:6], refs[6:12]
    out, res_out, sums, out_x, out_y, xg, yg, ends, gy, res = refs[12:]
    take_ghosts(tab, win, PART0, xg, yg, ends)
    sweep_wide(u, xg, yg, ends, gy, 0, w, first, lambda s, e: first_x[s, e], lambda s: first_y[s], out, out_x, out_y, 32)

    def emit(s, i, here, av):
        res[s, i] = t[s, i] - av

    apply_near(out, out_x, out_y, gy, 0, w, emit, 32)
    su = jnp.zeros((8, 128), F32)
    sr = jnp.zeros((8, 128), F32)
    for s in range(SLOTS):
        for i in range(32):
            d = res[s, i]
            sr = sr + d * d
            su = su + out[s, i]
        res_out[:, s, :] = res[s].reshape(256, 128)
    lane = iota((1, 128), 1)
    sums[...] = jnp.where(lane == 0, total(su), jnp.where(lane == 1, total(sr), 0.0))


def k_finish(count, u, sums, boxes, corr, norm):
    tot = jnp.sum(sums[...], axis=0, keepdims=True)
    cells = boxes[0:1, 0:1] * 32768.0
    mean = tot[:, 0:1] / cells
    for s in range(SLOTS):
        corr[:, s, :] = ((u[s] - mean) * used(count[0], s)).reshape(256, 128)
    norm[...] = jnp.broadcast_to(jnp.sqrt(tot[:, 1:2] / cells), (1, 128))


VMEM = pl.BlockSpec(memory_space=pltpu.VMEM)
SMEM = pl.BlockSpec(memory_space=pltpu.SMEM)
HBM = pl.BlockSpec(memory_space=pltpu.HBM)


def call(kernel, smem, args, outs, scratch=(), vmem=16, tables=(), hbm=0, extra=()):
    shape = lambda s: jax.ShapeDtypeStruct(s, F32)
    return pl.pallas_call(
        kernel,
        out_shape=[shape(s) for s in outs] + [jax.ShapeDtypeStruct(s, I32) for s in tables],
        in_specs=[SMEM] * smem + [VMEM] * (len(args) - smem - hbm) + [HBM] * hbm,
        out_specs=[VMEM] * len(outs) + [SMEM] * len(tables),
        scratch_shapes=[pltpu.VMEM(s, F32) for s in scratch] + list(extra),
        compiler_params=pltpu.CompilerParams(vmem_limit_bytes=vmem * 1024 * 1024),
    )(*args)


def swapped(block, pairs):
    route = sorted([(a, b) for a, b in pairs] + [(b, a) for a, b in pairs])
    return lax.ppermute(block, AX, route)


def xor_pairs(m):
    return [(i, i ^ m) for i in range(DEVICES) if i < i ^ m]


def exchange(faces, parts, notes=()):
    got = [faces]
    for m in (1, 2, 3):
        got.append(swapped(faces, xor_pairs(m)))
    tiles = parts[-1].side + parts[-1].side_tiles + (4 if notes else 0)
    sides = call(functools.partial(k_relay, parts, notes), 0, got, [(tiles, 8, 128)] * 2)
    beside = [None, None]
    for odd in (1, 0):
        pairs = [(i, i + 4) for i in range(DEVICES - 4) if (i // 4) % 2 == odd]
        beside[odd] = swapped(sides[odd], pairs)
    return tuple(got + beside)


def k_join(*refs):
    out = refs[4]
    each = (out.shape[0] // 100) * 24
    notes = each // 24
    for m in range(4):
        out[m * each : (m + 1) * each, :] = refs[m][0:each, :]
        at = 4 * each + m * notes
        out[at : at + notes, :] = refs[m][each : each + notes, :]


def gather_rows(rows):
    for unit, count in ((1, 104), (4, 400), (32, 1600)):
        got = [rows] + [swapped(rows, xor_pairs(m * unit)) for m in (1, 2, 3)]
        rows = call(k_join, 0, got, [(count, 128)])[0]
    return rows, swapped(rows, xor_pairs(16))


def to_all(rows):
    spread = jnp.broadcast_to(rows[None], (DEVICES,) + rows.shape)
    return lax.all_to_all(spread, AX, 0, 0)


def shards(source_term, inverse_density, box_counts, ghost_from):
    view = lambda a: a.reshape(SLOTS, 256, 128).transpose(1, 0, 2)
    fine, mid = (SLOTS, 32, 8, 128), (SLOTS, 16, 8, 128)
    gx, xg, ends = (SLOTS, 2, 8, 128), (SLOTS, 4, 8, 128), (SLOTS, 8, 128)
    gyf, gym = (SLOTS, 32, 128), (SLOTS, 16, 128)
    face0, face1 = (PART0.own_tiles, 8, 128), (PART1.own_tiles, 8, 128)

    def weight_shapes(n):
        wide = (SLOTS, n + 2, 8, 128)
        return [(SLOTS, n + 3, 8, 128), wide, wide, (SLOTS, n + 2, 128), wide, (SLOTS, 6, n, 128)]

    beta, beta1, faces, place = call(
        k_start, 1, (ghost_from, view(inverse_density)),
        [fine, mid, (FIRST_NOTES[0] + 1, 8, 128)], tables=[(25,)],
    )
    beta_rows = call(k_bottom_beta, 2, (ghost_from, box_counts, beta1), [(24, 128)])[0]
    later, faces = lax.optimization_barrier((view(source_term), faces))
    source = call(k_source, 1, (box_counts, later), [fine])[0]
    win = exchange(faces, FIRST, FIRST_NOTES)
    outs = call(
        k_weights, 0, (source, beta) + win, weight_shapes(32) + [fine, face0], [xg, gyf, ends, gyf],
        tables=[(5 * BOXES,)],
        extra=[pltpu.VMEM((16, 128), I32), pltpu.SMEM((16, 128), I32), pltpu.SemaphoreType.DMA],
    )
    w, (first, faces, tab) = tuple(outs[:6]), outs[6:]
    w1 = tuple(call(k_weights_next, 1, (tab, beta1) + win, weight_shapes(16), [xg, gym, ends, gym]))
    u, u_x, u_y, first_x, first_y, f1, first1, faces = call(
        k_down, 1, (tab, source, first) + exchange(faces, [PART0]) + w + (w1[4],),
        [fine, gx, gyf, gx, gyf, mid, mid, face1], [xg, gyf, ends, gyf, fine],
    )
    u1, u1_x, u1_y, first1_x, first1_y, rows = call(
        k_bottom_rhs, 1, (tab, f1, first1, beta_rows) + exchange(faces, [PART1]) + w1,
        [mid, gx, gym, gx, gym, (32, 128)], [xg, gym, ends, gym, mid],
    )
    cube, padded = (SLOTS, 8, 8, 8, 128), (SLOTS, 10, 10, 8, 128)
    kept = [first1, u1, u1_x, u1_y] + list(w1[:5])
    u1, faces, boxes = call(
        k_bottom, 1, (place,) + gather_rows(rows) + tuple(kept), [mid, face1, (8, 128)],
        [padded, cube, cube, cube, (SLOTS, 8, 9, 8, 128), (SLOTS, 9, 8, 8, 128), cube, (DEVICES, 24, 128),
         (128, 128), (DEVICES, 24, 128), mid, gx, gym, gym] + [a.shape for a in kept],
        hbm=len(kept), extra=[pltpu.SemaphoreType.DMA((len(kept),))],
    )
    u, faces = call(
        k_up, 1,
        (tab, first1, first1_x, first1_y, u1, first, u, u_x, u_y) + exchange(faces, [PART1]) + w1 + w,
        [fine, face0], [mid, gx, gym, xg, gym, ends, gym, fine, gx, gyf, gyf],
    )
    u, residual, sums = call(
        k_residual, 1, (tab, source, u, first, first_x, first_y) + exchange(faces, [PART0]) + w,
        [fine, (256, SLOTS, 128), (1, 128)], [gx, gyf, xg, gyf, ends, gyf, fine],
    )
    parts = to_all(sums).reshape(DEVICES, 128)
    correction, norm = call(k_finish, 1, (box_counts, u, parts, boxes), [(256, SLOTS, 128), (1, 128)])
    back = lambda a: a.transpose(1, 0, 2).reshape(SLOTS, 32768)
    return back(correction), back(residual), norm[0, 0]


def solution(mesh):
    rows = P(AX, None)
    return jax.shard_map(
        shards, mesh=mesh, in_specs=(rows, rows, P(AX), rows), out_specs=(rows, rows, P()), check_vma=False
    )
```

```python
import functools

import jax
import jax.numpy as jnp
from jax import lax
from jax.experimental import pallas as pl
from jax.experimental.pallas import tpu as pltpu
from jax.sharding import PartitionSpec as P

AX = ("gx", "gy")
DEVICES = 128
SLOTS = 3
BOTTOM_ITERS = 8
RELAXATION = 2.0 / 3.0
F32 = jnp.float32
I32 = jnp.int32

PLANES = (32, 16)


def iota(shape, dim):
    return lax.broadcasted_iota(I32, shape, dim)


def lanes():
    return iota((8, 128), 1)


def subs():
    return iota((8, 128), 0)


def roll(x, shift, axis):
    return pltpu.roll(x, shift, axis)


def lane_take(x, at):
    return jnp.take_along_axis(x, at, axis=1, mode="promise_in_bounds")


class Tile:
    def __init__(self, lv):
        self.zs, self.ys = 1 << lv, 32 << lv
        lane, sub = lanes(), subs()
        self.south_in = lane >= self.ys
        self.north_in = lane < 128 - self.ys
        self.first_row = sub == 0
        self.last_row = sub == 7
        self.south_edge = self.first_row & (lane < self.ys)
        self.z_low = (lane & 31) < self.zs

    def south(self, v, row):
        r = roll(v, self.ys, 1)
        return jnp.where(self.south_in, r, jnp.where(self.first_row, row, roll(r, 1, 0)))

    def north(self, v, edge):
        r = roll(v, 128 - self.ys, 1)
        return jnp.where(self.north_in, r, jnp.where(self.last_row, edge, roll(r, 7, 0)))

    def below(self, v):
        return roll(v, self.zs, 1)

    def above(self, v):
        return roll(v, 128 - self.zs, 1)


def pair_sum(t, lv):
    lane = iota(t.shape, 1)
    zs, ys = 1 << lv, 32 << lv
    t = t + jnp.where((lane & zs) == 0, roll(t, 128 - zs, 1), roll(t, zs, 1))
    return t + jnp.where((lane & ys) == 0, roll(t, 128 - ys, 1), roll(t, ys, 1))


BOXES = 36
TWO_FACES = ((0, 2), (0, 3), (1, 2), (1, 3), (2, 0), (2, 1), (3, 0), (3, 1))


class Part:
    def __init__(self, lv, own=0, side=0):
        self.lv, self.own, self.side = lv, own, side
        self.tiles = (8, 3)[lv]
        self.ys = (4, 1)[lv]
        self.own_tiles = SLOTS * self.tiles
        self.side_tiles = (42, 18)[lv]


def pack_faces(v, s, part, out):
    n = PLANES[part.lv]
    pack_tiles([v[s, 0], v[s, 1], v[s, n - 2], v[s, n - 1]], v[s, :, 0, :], v[s, :, 7, :], s, part, out)


def pack_tiles(planes, y0, y7, s, part, out):
    lv = part.lv
    n = PLANES[lv]
    base = part.own + s * part.tiles
    lane = iota((n, 128), 1)
    if lv == 0:
        for m in range(4):
            out[base + m] = planes[m]
        q = roll(jnp.where(lane >= 64, y7, y0), 64, 1)
    else:
        odd_k, odd_j = (lanes() & 1) == 1, (lanes() & 32) == 32
        out[base] = jnp.where(
            odd_k, jnp.where(odd_j, planes[3], planes[2]), jnp.where(odd_j, planes[1], planes[0])
        )
        q = jnp.where(
            lane < 32, y7, jnp.where(lane < 64, roll(y7, 96, 1), jnp.where(lane < 96, roll(y0, 64, 1), y0))
        )
    for t in range(n // 8):
        out[base + part.ys + t] = q[8 * t : 8 * t + 8]


def k_relay(parts, notes, *refs):
    got, (near, far) = refs[:4], refs[4:]
    _, even, place, _ = place_of_device()
    even = even == 1

    def of(m, t):
        low = jnp.where((m & 1) == 0, got[0][t], got[1][t])
        high = jnp.where((m & 1) == 0, got[2][t], got[3][t])
        return jnp.where(m < 2, low, high)

    def put(at, fwd, bwd):
        near[at] = jnp.where(even, fwd, bwd)
        far[at] = jnp.where(even, bwd, fwd)

    for part in parts:
        for s in range(SLOTS):
            base = part.own + s * part.tiles
            for m in range(4):
                box = m * SLOTS + s
                if part.lv == 0:
                    for x in range(2):
                        put(part.side + box * 2 + x, got[m][base + 2 + x], got[m][base + x])
                else:
                    put(part.side + box, got[m][base], got[m][base])
            if part.lv == 0:
                for x in range(2):
                    put(part.side + 24 + s * 6 + x, of(place ^ 3, base + x), of(place, base + 2 + x))
            for t in range(part.tiles - part.ys):
                at = part.side + (24 + s * 6 + 2 + t if part.lv == 0 else 12 + s * 2 + t)
                put(at, of(place ^ 3, base + part.ys + t), of(place, base + part.ys + t))
    if notes:
        own, side = notes
        for m in range(4):
            near[side + m] = got[m][own]
            far[side + m] = got[m][own]


def pick(tab, win, k, own, side):
    r = tab[k]
    low = jnp.where((r & 1) == 0, win[0][own], win[1][own])
    high = jnp.where((r & 1) == 0, win[2][own], win[3][own])
    beside = jnp.where((r & 1) == 0, win[4][side], win[5][side])
    return jnp.where(r < 4, jnp.where(r < 2, low, high), beside)


def pick_plane(tab, win, k, part, p):
    slot, m, delta = tab[BOXES + k], tab[2 * BOXES + k], tab[3 * BOXES + k]
    own = part.own + slot * part.tiles
    box = m * SLOTS + slot
    if part.lv == 0:
        x = p & 1
        direct = -1 if p >= 2 else 1
        side = part.side + jnp.where(delta == direct, box * 2 + x, 24 + slot * 6 + x)
        return pick(tab, win, k, own + p, side)
    lane = lanes()
    t = pick(tab, win, k, own, part.side + box)
    t = jnp.where(((lane & 1) == p >> 1) & ((lane & 32) == (p & 1) * 32), t, 0.0)
    return pair_sum(t, 0)


def pick_rows(tab, win, k, part, t):
    slot = tab[BOXES + k]
    own = part.own + slot * part.tiles + part.ys + t
    side = part.side + (24 + slot * 6 + 2 + t if part.lv == 0 else 12 + slot * 2 + t)
    return pick(tab, win, k, own, side)


def near_rows(y):
    lane = iota(y.shape, 1)
    return jnp.where(lane < 32, roll(y, 96, 1), jnp.where(lane < 96, y, roll(y, 32, 1)))


def take_ghosts(tab, win, part, xg, yg, ends):
    ys = 32 << part.lv
    low = iota((1, 128), 1) < 64
    for s in range(SLOTS):
        for g, (f, p) in enumerate(((0, 2), (0, 3), (1, 0), (1, 1))):
            xg[s, g] = pick_plane(tab, win, s * 4 + f, part, p)
        for t in range(part.tiles - part.ys):
            sv = pick_rows(tab, win, s * 4 + 2, part, t)
            nv = pick_rows(tab, win, s * 4 + 3, part, t)
            yg[s, 8 * t : 8 * t + 8, :] = jnp.where(lanes() < 64, sv, nv)

        def corner(q, p):
            return pick_plane(tab, win, 12 + s * 8 + q, part, p)

        for e, p in ((0, 3), (1, 0)):
            sp = corner(2 * e, p)[7:8]
            np = corner(2 * e + 1, p)[0:1]
            ends[s, e : e + 1, :] = jnp.where(low, roll(sp, ys, 1), roll(np, 128 - ys, 1))
            sp = corner(4 + e, p)[7:8]
            np = corner(6 + e, p)[0:1]
            ends[s, 2 + e : 3 + e, :] = jnp.where(low, roll(sp, 64, 1), roll(np, 64, 1))


def set_near(yg, gy, n):
    for s in range(SLOTS):
        for t in range(n // 8):
            gy[s, 8 * t : 8 * t + 8, :] = near_rows(yg[s, 8 * t : 8 * t + 8, :])


def planes_loop(n, body, carry, unroll=8):
    def chunk(c, carry):
        for u in range(unroll):
            carry = body(c * unroll + u, carry, u == unroll - 1)
        return carry

    return lax.fori_loop(0, n // unroll, chunk, carry)


def following(ref, s, i, n, edge, at_end):
    if not at_end:
        return ref[s, i + 1]
    return jnp.where(i == n - 1, edge, ref[s, jnp.minimum(i + 1, n - 1)])


def slab_sides(y, v, s, ends, n):
    lane = iota((n, 128), 1)
    row = iota((n, 128), 0)
    inner = jnp.where(lane < 64, roll(v[s, :, 0, :], 32, 1), roll(v[s, :, 7, :], 96, 1))
    outer = jnp.where(lane < 64, roll(y, 32, 1), roll(y, 96, 1))
    down = jnp.where(row == 0, ends[s, 2:3, :], roll(y, 1, 0))
    up = jnp.where(row == n - 1, ends[s, 3:4, :], roll(y, n - 1, 0))
    return outer, inner, down, up


def make_weights(b, xg, yg, ends, gy, tab, lv, w, extra):
    cx, cy, cz, wn, rd, slab = w
    n = PLANES[lv]
    h = 0.5 * 0.25**lv
    tl = Tile(lv)
    set_near(yg, gy, n)

    def has(k):
        return jnp.where(tab[4 * BOXES + k] == 1, 1.0, 0.0)

    def plane(s, i, here, w, nxt, wnext, row, south, north):
        wy = h * (here + tl.south(here, row))
        wy = jnp.where(tl.south_edge, wy * south, wy)
        wrow = h * (here + row) * north
        wz = jnp.where(tl.z_low, 0.0, h * (here + tl.below(here)))
        d = (w + wnext) + (wy + tl.north(wy, wrow)) + (wz + tl.above(wz))
        r = RELAXATION / d
        cx[s, i + 2] = wnext
        cy[s, i + 1] = wy
        cz[s, i + 1] = wz
        wn[s, pl.ds(i + 1, 1), :] = wrow[7:8, :]
        rd[s, i + 1] = r
        return r

    first = []
    for s in range(SLOTS):
        here, v = xg[s, 1], b[s, 0]
        w = h * (here + xg[s, 0])
        cx[s, 0] = w
        wnext = h * (here + v) * has(s * 4)
        plane(s, -1, here, w, v, wnext, ends[s, 0:1, :], has(12 + s * 8), has(13 + s * 8))
        first.append((v, wnext))

    def body(i, carry, at_end):
        out = []
        for s in range(SLOTS):
            v, w = carry[s]
            nxt = following(b, s, i, n, xg[s, 2], at_end)
            wnext = h * (v + nxt)
            if at_end:
                wnext = wnext * jnp.where(i == n - 1, has(s * 4 + 1), 1.0)
            r = plane(s, i, v, w, nxt, wnext, gy[s, pl.ds(i, 1), :], has(s * 4 + 2), has(s * 4 + 3))
            extra(s, i, r)
            out.append((nxt, wnext))
        return tuple(out)

    last = planes_loop(n, body, tuple(first))
    lane = iota((n, 128), 1)
    row = iota((n, 128), 0)
    for s in range(SLOTS):
        here, w = last[s]
        far = xg[s, 3]
        plane(s, n, here, w, far, h * (here + far), ends[s, 1:2, :], has(14 + s * 8), has(15 + s * 8))
        y = yg[s]
        outer, inner, down, up = (h * (y + t) for t in slab_sides(y, b, s, ends, n))
        k = 12 + s * 8
        down = down * jnp.where(row == 0, jnp.where(lane < 64, has(k + 4), has(k + 6)), 1.0)
        up = up * jnp.where(row == n - 1, jnp.where(lane < 64, has(k + 5), has(k + 7)), 1.0)
        zs = tl.zs
        wz = jnp.where((lane & 31) < zs, 0.0, h * (y + roll(y, zs, 1)))
        d = (outer + inner) + (down + up) + (wz + roll(wz, 128 - zs, 1))
        for m, t in enumerate((outer, inner, down, up, wz, RELAXATION / d)):
            slab[s, m] = t


def apply_level(v, before, after, gy, ends, lv, w, emit, wide=None, unroll=8):
    cx, cy, cz, wn = w[:4]
    n = PLANES[lv]
    tl = Tile(lv)

    def plane(s, i, here, fx, nxt, row):
        fnext = cx[s, i + 2] * (nxt - here)
        wrow = wn[s, pl.ds(i + 1, 1), :]
        fy = cy[s, i + 1] * (here - tl.south(here, row))
        fn = tl.north(fy, wrow * (row - here))
        fz = cz[s, i + 1] * (here - tl.below(here))
        return (fx - fnext) + (fy - fn) + (fz - tl.above(fz)), fnext

    first = []
    for s in range(SLOTS):
        v0, west = v[s, 0], before(s, 0)
        if wide:
            fx = cx[s, 0] * (west - before(s, 1))
            av, fx = plane(s, -1, west, fx, v0, ends[s, 0:1, :])
            wide(s, 0, west, av)
        else:
            fx = cx[s, 1] * (v0 - west)
        first.append((v0, fx))

    def body(i, carry, at_end):
        out = []
        for s in range(SLOTS):
            here, fx = carry[s]
            nxt = following(v, s, i, n, after(s, 0), at_end)
            av, fnext = plane(s, i, here, fx, nxt, gy[s, pl.ds(i, 1), :])
            emit(s, i, here, av)
            out.append((nxt, fnext))
        return tuple(out)

    last = planes_loop(n, body, tuple(first), unroll)
    if wide:
        for s in range(SLOTS):
            here, fx = last[s]
            av, fx = plane(s, n, here, fx, after(s, 1), ends[s, 1:2, :])
            wide(s, 1, here, av)


def apply_slab(yg, v, s, ends, lv, slab):
    n = PLANES[lv]
    zs = 1 << lv
    y = yg[s]
    outer, inner, down, up = slab_sides(y, v, s, ends, n)
    fz = slab[s, 4] * (y - roll(y, zs, 1))
    a = slab[s, 0] * (y - outer) + slab[s, 1] * (y - inner)
    b = slab[s, 2] * (y - down) + slab[s, 3] * (y - up)
    return y, a + b + (fz - roll(fz, 128 - zs, 1))


def sweep_wide(v, xg, yg, ends, gy, lv, w, first, first_x, first_y, out, out_x, out_y, unroll=8):
    rd, slab = w[4:]
    n = PLANES[lv]
    set_near(yg, gy, n)

    def emit(s, i, here, av):
        out[s, i] = here + (first[s, i] - av * rd[s, i + 1])

    def wide(s, e, here, av):
        out_x[s, e] = here + (first_x(s, e) - av * rd[s, (n + 1) * e])

    apply_level(v, lambda s, g: xg[s, 1 - g], lambda s, g: xg[s, 2 + g], gy, ends, lv, w, emit, wide, unroll)
    for s in range(SLOTS):
        y, a = apply_slab(yg, v, s, ends, lv, slab)
        out_y[s] = y + (first_y(s) - a * slab[s, 5])


def apply_near(v, gx, yg, gy, lv, w, emit, unroll=8):
    set_near(yg, gy, PLANES[lv])
    apply_level(v, lambda s, g: gx[s, 0], lambda s, g: gx[s, 1], gy, None, lv, w, emit, None, unroll)


def restrict_planes(v, s, lv, scale):
    out = []
    for c in range(PLANES[lv] // 2):
        out.append(pair_sum(v[s, 2 * c] + v[s, 2 * c + 1], lv) * scale)
    return out


def pack_bottom(planes, out):
    lane = lanes()
    at = (lane & 7) * 4
    part = lane >> 3
    top = None
    for s in range(2):
        for i in range(8):
            g = lane_take(planes[s][i], at)
            top = g if top is None else jnp.where(part == s * 8 + i, g, top)
    low = None
    for i in range(8):
        g = lane_take(planes[2][i], at)
        low = g if low is None else jnp.where((part & 7) == i, g, low)
    low = jnp.where(lane < 64, low, roll(low, 4, 0))
    out[0:8, :] = top
    out[8:16, :] = low


PART0, PART1 = Part(0), Part(1)
FIRST = (Part(0), Part(1, 24, 42))
FIRST_NOTES = (33, 60)


def place_of_device():
    dev = lax.axis_index("gx") * 16 + lax.axis_index("gy")
    return dev, 1 - ((dev >> 2) & 1), dev & 3, dev >> 2


def used(count, s):
    return jnp.where(s < count, 1.0, 0.0)


def k_load(count, src, inv, out, b, b1):
    for s in range(SLOTS):
        out[s] = src[:, s, :].reshape(32, 8, 128) * used(count[0], s)
        b[s] = inv[:, s, :].reshape(32, 8, 128)
        for c, t in enumerate(restrict_planes(b, s, 0, 0.125)):
            b1[s, c] = t


def k_bottom_beta(ghost, count, b1, out, place):
    lane = lanes()
    dev = place_of_device()[0]
    place[24] = dev
    note = jnp.where(lane == 12, jnp.full((8, 128), count[0]), 0)
    for s in range(SLOTS):
        for f in range(4):
            k, g = s * 4 + f, ghost[s, f]
            note = jnp.where(lane == k, jnp.full((8, 128), g), note)
            owner = jnp.where(g >= 0, (g * 21846) >> 16, dev)
            place[k] = owner
            place[12 + k] = jnp.where(g >= 0, g - 3 * owner, 0)
    pack_bottom([restrict_planes(b1, s, 1, 0.125) for s in range(SLOTS)], out)
    out[16:24, :] = note.astype(F32)


def k_start(ghost, inv, faces):
    g = ghost[...]
    owner = (g * 21846) >> 16
    codes = jnp.where(g >= 0, g + owner, -1)
    faces[FIRST_NOTES[0]] = jnp.zeros((8, 128), F32)
    faces[FIRST_NOTES[0], 0:SLOTS, 0:4] = codes.astype(F32)
    for s in range(SLOTS):
        plane = lambda i: inv[8 * i : 8 * i + 8, s, :]
        y = [inv[pl.ds(at, 32, stride=8), s, :] for at in (0, 7)]
        pack_tiles([plane(i) for i in (0, 1, 30, 31)], y[0], y[1], s, FIRST[0], faces)
        near = [pair_sum(plane(2 * c) + plane(2 * c + 1), 0) * 0.125 for c in (0, 1, 14, 15)]
        y = [
            pair_sum(inv[pl.ds(at, 16, stride=16), s, :] + inv[pl.ds(at + 8, 16, stride=16), s, :], 0) * 0.125
            for at in (0, 7)
        ]
        pack_tiles(near, y[0], y[1], s, FIRST[1], faces)


def fill_table(win, rows, notes, sem, tab):
    _, even, place, block = place_of_device()
    own, side = FIRST_NOTES
    rows[...] = jnp.zeros((40, 128), I32)
    for m in range(4):
        rows[3 * m : 3 * m + 3, :] = win[m][own][0:3].astype(I32)
        for x in range(2):
            at = 3 * (4 + 4 * x + m)
            rows[at : at + 3, :] = win[4 + x][side + m][0:3].astype(I32)
    copy = pltpu.make_async_copy(rows, notes, sem)
    copy.start()
    copy.wait()

    def entry(k, code):
        owner = code >> 2
        delta = jnp.where(code >= 0, (owner >> 2) - block, 0)
        m = jnp.where(code >= 0, (owner & 3) ^ place, 0)
        slot = jnp.where(code >= 0, code & 3, 0)
        r = jnp.where(delta == 0, m, jnp.where(delta == 2 * even - 1, 4, 5))
        for x, value in enumerate((r, slot, m, delta, jnp.where(code >= 0, 1, 0))):
            tab[x * BOXES + k] = value
        return (jnp.where(r < 4, 0, r - 3) * 4 + m) * 3 + slot

    for s in range(SLOTS):
        codes = [notes[s, f] for f in range(4)]
        found = [entry(s * 4 + f, codes[f]) for f in range(4)]
        for q, (f, g) in enumerate(TWO_FACES):
            entry(12 + s * 8 + q, jnp.where(codes[f] >= 0, notes[found[f], g], -1))


def k_weights(source, b, *refs):
    win, refs = refs[:6], refs[6:]
    w, u, faces, tab, (xg, yg, ends, gy, rows, notes, sem) = refs[:6], refs[6], refs[7], refs[8], refs[9:]
    fill_table(win, rows, notes, sem, tab)
    take_ghosts(tab, win, FIRST[0], xg, yg, ends)

    def first(s, i, r):
        u[s, i] = source[s, i] * r

    make_weights(b, xg, yg, ends, gy, tab, 0, w, first)
    for s in range(SLOTS):
        pack_faces(u, s, PART0, faces)


def k_weights_next(tab, b1, *refs):
    win, w1, (xg, yg, ends, gy) = refs[:6], refs[6:12], refs[12:]
    take_ghosts(tab, win, FIRST[1], xg, yg, ends)
    make_weights(b1, xg, yg, ends, gy, tab, 1, w1, lambda s, i, r: None)


def k_down(tab, t, u, *refs):
    win, w, rd1 = refs[:6], refs[6:12], refs[12]
    out, out_x, out_y, first_x, first_y, f1, u1, faces, xg, yg, ends, gy, res = refs[13:]
    take_ghosts(tab, win, PART0, xg, yg, ends)
    for s in range(SLOTS):
        for e in range(2):
            first_x[s, e] = xg[s, 1 + e]
        first_y[s] = yg[s]
    sweep_wide(u, xg, yg, ends, gy, 0, w, u, lambda s, e: xg[s, 1 + e], lambda s: yg[s], out, out_x, out_y)

    def emit(s, i, here, av):
        res[s, i] = t[s, i] - av

    apply_near(out, out_x, out_y, gy, 0, w, emit)
    for s in range(SLOTS):
        for c, p in enumerate(restrict_planes(res, s, 0, 0.125)):
            f1[s, c] = p
            u1[s, c] = p * rd1[s, c + 1]
        pack_faces(u1, s, PART1, faces)


def k_bottom_rhs(tab, t, u, beta_rows, *refs):
    win, w = refs[:6], refs[6:12]
    out, out_x, out_y, first_x, first_y, packed, xg, yg, ends, gy, res = refs[12:]
    take_ghosts(tab, win, PART1, xg, yg, ends)
    for s in range(SLOTS):
        for e in range(2):
            first_x[s, e] = xg[s, 1 + e]
        first_y[s] = yg[s]
    sweep_wide(u, xg, yg, ends, gy, 1, w, u, lambda s, e: xg[s, 1 + e], lambda s: yg[s], out, out_x, out_y)

    def emit(s, i, here, av):
        res[s, i] = t[s, i] - av

    apply_near(out, out_x, out_y, gy, 1, w, emit)
    pack_bottom([restrict_planes(res, s, 1, 0.125) for s in range(SLOTS)], packed)
    packed[12:24, :] = beta_rows[0:12, :]
    packed[24:32, :] = beta_rows[16:24, :]


def total(v):
    return jnp.sum(v, axis=(0, 1), keepdims=True)


def unpack_bottom(rows, at, put):
    for r in range(12):
        t = rows[:, at + r, :].T
        for half in range(2):
            s, j = (half, r) if r < 8 else (2, r - 8 + 4 * half)
            for i in range(8):
                put(s, j, i, t[half * 64 + i * 8 : half * 64 + i * 8 + 8, :])


def face_gather(dev_at, slot_at, place):
    out = lane_take(place(0), dev_at)
    for other in range(1, SLOTS):
        out = jnp.where(slot_at == other, lane_take(place(other), dev_at), out)
    return out


def fill_bottom_ghosts(p, at, slot):
    for s in range(SLOTS):
        for f, (src, dst) in enumerate(((7, 0), (0, 9))):
            k = s * 4 + f
            for m in range(1, 9):
                p[s, m, dst] = face_gather(at[k], slot[k], lambda o: p[o, m, src + 1])
            k = s * 4 + 2 + f
            for m in range(1, 9):
                p[s, dst, m] = face_gather(at[k], slot[k], lambda o: p[o, src + 1, m])


def k_bottom(place, mine64, other64, *refs):
    far, (out, faces, boxes_out) = refs[:9], refs[9:12]
    p, r, x, q, cx, cy, cz, back, sq, rows, v1, gx, yg, gy = refs[12:26]
    kept, sem = refs[26:35], refs[35]
    copies = [pltpu.make_async_copy(a, b, sem.at[n]) for n, (a, b) in enumerate(zip(far, kept))]
    for c in copies:
        c.start()
    first, u, gx0, gy0 = kept[:4]
    w1 = kept[4:]
    me = place[24]
    for m in range(64):
        here = me ^ ((m & 15) | ((m >> 4) << 5))
        for half, there in ((mine64, here), (other64, here ^ 16)):
            rows[there] = half[24 * m : 24 * m + 24, :]
            sq[pl.ds(there, 1), :] = half[1536 + m : 1537 + m, :]
    note = sq[...].T
    at, slot, pres = [], [], []
    for f in range(12):
        gf = jnp.broadcast_to(note[f : f + 1, :], (8, 128))
        has = gf >= 0.0
        gf = jnp.where(has, gf, 0.0)
        dv = ((gf + 0.5) * (1.0 / 3.0)).astype(I32)
        at.append(dv)
        slot.append(gf.astype(I32) - 3 * dv)
        pres.append(jnp.where(has, 1.0, 0.0))
    counts = jnp.broadcast_to(note[12:13, :], (8, 128))
    boxes = jnp.sum(counts[0:1], axis=1, keepdims=True)
    boxes_out[...] = jnp.broadcast_to(boxes, (8, 128))

    def fill_ghosts():
        fill_bottom_ghosts(p, at, slot)

    def put_beta(s, j, i, tile):
        p[s, j + 1, i + 1] = tile

    unpack_bottom(rows, 12, put_beta)
    fill_ghosts()
    h = 0.5 * 0.0625
    low = subs() == 0

    def weights(m, _):
        for s in range(SLOTS):
            for i in range(9):
                w = h * (p[s, m + 1, i] + p[s, m + 1, i + 1])
                if i == 0:
                    w = w * pres[s * 4]
                if i == 8:
                    w = w * pres[s * 4 + 1]
                cx[s, m, i] = w
                w = h * (p[s, i, m + 1] + p[s, i + 1, m + 1])
                if i == 0:
                    w = w * pres[s * 4 + 2]
                if i == 8:
                    w = w * pres[s * 4 + 3]
                cy[s, i, m] = w
            for i in range(8):
                b = p[s, m + 1, i + 1]
                cz[s, m, i] = jnp.where(low, 0.0, h * (b + roll(b, 1, 0)))
        return 0

    lax.fori_loop(0, 8, weights, 0, unroll=8)

    def put_rhs(s, j, i, tile):
        r[s, j, i] = tile

    unpack_bottom(rows, 0, put_rhs)

    zero = jnp.zeros((8, 128), F32)

    def whole(a):
        a = ((a[0] + a[1]) + (a[2] + a[3])) + ((a[4] + a[5]) + (a[6] + a[7]))
        for sh in (4, 2, 1):
            a = a + roll(a, sh, 0)
        return jnp.broadcast_to(jnp.sum(a, axis=1, keepdims=True), (8, 128))

    def each(fn):
        def step(j, acc):
            acc = list(acc)
            for s in range(SLOTS):
                for i in range(8):
                    acc[i] = fn(s, j, i, acc[i])
            return tuple(acc)

        return whole(lax.fori_loop(0, 8, step, (zero,) * 8, unroll=8))

    mean = each(lambda s, j, i, acc: acc + r[s, j, i]) / jnp.broadcast_to(boxes * 512.0, (8, 128))
    valid = [jnp.where(counts > s + 0.5, 1.0, 0.0) for s in range(SLOTS)]

    def shift(s, j, i, acc):
        v = (r[s, j, i] - mean) * valid[s]
        r[s, j, i] = v
        p[s, j + 1, i + 1] = v
        x[s, j, i] = zero
        return acc + v * v

    rr = each(shift)

    def image():
        def step(j, acc):
            acc = list(acc)
            for s in range(SLOTS):
                here = p[s, j + 1, 1]
                fx = cx[s, j, 0] * (here - p[s, j + 1, 0])
                for i in range(8):
                    nxt = p[s, j + 1, i + 2]
                    fnext = cx[s, j, i + 1] * (nxt - here)
                    b = cy[s, j, i] * (here - p[s, j, i + 1]) + cy[s, j + 1, i] * (here - p[s, j + 2, i + 1])
                    fz = cz[s, j, i] * (here - roll(here, 1, 0))
                    v = (fx - fnext) + b + (fz - roll(fz, 7, 0))
                    q[s, j, i] = v
                    acc[i] = acc[i] + here * v
                    here, fx = nxt, fnext
            return tuple(acc)

        return whole(lax.fori_loop(0, 8, step, (zero,) * 8, unroll=8))

    def iteration(it, rr):
        fill_ghosts()
        alpha = rr / image()

        def step(s, j, i, acc):
            x[s, j, i] = x[s, j, i] + alpha * p[s, j + 1, i + 1]
            v = r[s, j, i] - alpha * q[s, j, i]
            r[s, j, i] = v
            return acc + v * v

        rr_next = each(step)
        ratio = rr_next / rr

        def turn(j, _):
            for s in range(SLOTS):
                for i in range(8):
                    p[s, j + 1, i + 1] = r[s, j, i] + ratio * p[s, j + 1, i + 1]
            return 0

        lax.fori_loop(0, 8, turn, 0, unroll=8)
        return rr_next

    rr = lax.fori_loop(0, BOTTOM_ITERS - 1, iteration, rr)
    fill_ghosts()
    alpha = rr / image()

    for row in range(12):
        for half in range(2):
            s, j = (half, row) if row < 8 else (2, row - 8 + 4 * half)
            for i in range(8):
                sq[half * 64 + i * 8 : half * 64 + i * 8 + 8, :] = x[s, j, i] + alpha * p[s, j + 1, i + 1]
        tr = sq[...].T
        if row < 8:
            back[:, row, :] = tr
            back[:, 8 + row, :] = roll(tr, 64, 1)
        else:
            back[:, 8 + row, :] = tr
            back[:, 12 + row, :] = roll(tr, 64, 1)

    for c in copies:
        c.wait()
    lane, sub = lanes(), subs()
    kat = (lane & 31) >> 2

    def box(dev, s):
        return back[dev, pl.ds(pl.multiple_of(8 * s, 8), 8), :]

    for s in range(SLOTS):
        mine = box(me, s)
        for i in range(8):
            g = lane_take(mine, kat + i * 8)
            v1[s, 2 * i] = u[s, 2 * i] + g
            v1[s, 2 * i + 1] = u[s, 2 * i + 1] + g
        near = [box(place[s * 4 + f], place[12 + s * 4 + f]) for f in range(4)]
        for f, i in ((0, 7), (1, 0)):
            gx[s, f] = gx0[s, f] + lane_take(near[f], kat + i * 8)
        sb = jnp.broadcast_to(near[2][7:8, :], (8, 128))
        nb = jnp.broadcast_to(near[3][0:1, :], (8, 128))
        for part in range(2):
            idx = kat + (part * 4 + (sub >> 1)) * 8
            g = jnp.where(lane < 64, lane_take(sb, idx), lane_take(nb, idx))
            yg[s, 8 * part : 8 * part + 8, :] = gy0[s, 8 * part : 8 * part + 8, :] + g

    def emit(s, i, here, av):
        out[s, i] = here + (first[s, i] - av * w1[4][s, i + 1])

    apply_near(v1, gx, yg, gy, 1, w1, emit)
    for s in range(SLOTS):
        pack_faces(out, s, PART1, faces)


def k_up(tab, first1, first1_x, first1_y, u1, first, u0, u0_x, u0_y, *refs):
    win, w1, w = refs[:6], refs[6:12], refs[12:18]
    out, faces, c, c_x, c_y, xg, yg, ends, gy1, v, gx, y0, gy = refs[18:]
    take_ghosts(tab, win, PART1, xg, yg, ends)
    sweep_wide(u1, xg, yg, ends, gy1, 1, w1, first1, lambda s, e: first1_x[s, e], lambda s: first1_y[s], c, c_x, c_y)
    for s in range(SLOTS):
        for f in range(2):
            gx[s, f] = u0_x[s, f] + c_x[s, f]
        for i in range(16):
            t = c[s, i]
            v[s, 2 * i] = u0[s, 2 * i] + t
            v[s, 2 * i + 1] = u0[s, 2 * i + 1] + t
            y0[s, 2 * i : 2 * i + 2, :] = u0_y[s, 2 * i : 2 * i + 2, :] + c_y[s, i : i + 1, :]

    def emit(s, i, here, av):
        out[s, i] = here + (first[s, i] - av * w[4][s, i + 1])

    apply_near(v, gx, y0, gy, 0, w, emit)
    for s in range(SLOTS):
        pack_faces(out, s, PART0, faces)


def k_residual(tab, t, u, first, first_x, first_y, *refs):
    win, w = refs[:6], refs[6:12]
    out, res_out, sums, out_x, out_y, xg, yg, ends, gy, res = refs[12:]
    take_ghosts(tab, win, PART0, xg, yg, ends)
    sweep_wide(u, xg, yg, ends, gy, 0, w, first, lambda s, e: first_x[s, e], lambda s: first_y[s], out, out_x, out_y, 32)

    def emit(s, i, here, av):
        res[s, i] = t[s, i] - av

    apply_near(out, out_x, out_y, gy, 0, w, emit, 32)
    su = jnp.zeros((8, 128), F32)
    sr = jnp.zeros((8, 128), F32)
    for s in range(SLOTS):
        for i in range(32):
            d = res[s, i]
            sr = sr + d * d
            su = su + out[s, i]
        res_out[:, s, :] = res[s].reshape(256, 128)
    lane = iota((1, 128), 1)
    sums[...] = jnp.where(lane == 0, total(su), jnp.where(lane == 1, total(sr), 0.0))


def k_finish(count, u, sums, boxes, corr, norm):
    tot = jnp.sum(sums[...], axis=0, keepdims=True)
    cells = boxes[0:1, 0:1] * 32768.0
    mean = tot[:, 0:1] / cells
    for s in range(SLOTS):
        corr[:, s, :] = ((u[s] - mean) * used(count[0], s)).reshape(256, 128)
    norm[...] = jnp.broadcast_to(jnp.sqrt(tot[:, 1:2] / cells), (1, 128))


VMEM = pl.BlockSpec(memory_space=pltpu.VMEM)
SMEM = pl.BlockSpec(memory_space=pltpu.SMEM)
HBM = pl.BlockSpec(memory_space=pltpu.HBM)


def call(kernel, smem, args, outs, scratch=(), vmem=16, tables=(), hbm=0, extra=()):
    shape = lambda s: jax.ShapeDtypeStruct(s, F32)
    return pl.pallas_call(
        kernel,
        out_shape=[shape(s) for s in outs] + [jax.ShapeDtypeStruct(s, I32) for s in tables],
        in_specs=[SMEM] * smem + [VMEM] * (len(args) - smem - hbm) + [HBM] * hbm,
        out_specs=[VMEM] * len(outs) + [SMEM] * len(tables),
        scratch_shapes=[pltpu.VMEM(s, F32) for s in scratch] + list(extra),
        compiler_params=pltpu.CompilerParams(vmem_limit_bytes=vmem * 1024 * 1024),
    )(*args)


def swapped(block, pairs):
    route = sorted([(a, b) for a, b in pairs] + [(b, a) for a, b in pairs])
    return lax.ppermute(block, AX, route)


def xor_pairs(m):
    return [(i, i ^ m) for i in range(DEVICES) if i < i ^ m]


def exchange(faces, parts, notes=()):
    got = [faces]
    for m in (1, 2, 3):
        got.append(swapped(faces, xor_pairs(m)))
    tiles = parts[-1].side + parts[-1].side_tiles + (4 if notes else 0)
    sides = call(functools.partial(k_relay, parts, notes), 0, got, [(tiles, 8, 128)] * 2)
    beside = [None, None]
    for odd in (1, 0):
        pairs = [(i, i + 4) for i in range(DEVICES - 4) if (i // 4) % 2 == odd]
        beside[odd] = swapped(sides[odd], pairs)
    return tuple(got + beside)


def k_join(*refs):
    out = refs[4]
    each = (out.shape[0] // 100) * 24
    notes = each // 24
    for m in range(4):
        out[m * each : (m + 1) * each, :] = refs[m][0:each, :]
        at = 4 * each + m * notes
        out[at : at + notes, :] = refs[m][each : each + notes, :]


def gather_rows(rows):
    for unit, count in ((1, 104), (4, 400), (32, 1600)):
        got = [rows] + [swapped(rows, xor_pairs(m * unit)) for m in (1, 2, 3)]
        rows = call(k_join, 0, got, [(count, 128)])[0]
    return rows, swapped(rows, xor_pairs(16))


def to_all(rows):
    spread = jnp.broadcast_to(rows[None], (DEVICES,) + rows.shape)
    return lax.all_to_all(spread, AX, 0, 0)


def shards(source_term, inverse_density, box_counts, ghost_from):
    view = lambda a: a.reshape(SLOTS, 256, 128).transpose(1, 0, 2)
    fine, mid = (SLOTS, 32, 8, 128), (SLOTS, 16, 8, 128)
    gx, xg, ends = (SLOTS, 2, 8, 128), (SLOTS, 4, 8, 128), (SLOTS, 8, 128)
    gyf, gym = (SLOTS, 32, 128), (SLOTS, 16, 128)
    face0, face1 = (PART0.own_tiles, 8, 128), (PART1.own_tiles, 8, 128)

    def weight_shapes(n):
        wide = (SLOTS, n + 2, 8, 128)
        return [(SLOTS, n + 3, 8, 128), wide, wide, (SLOTS, n + 2, 128), wide, (SLOTS, 6, n, 128)]

    faces = call(k_start, 0, (ghost_from, view(inverse_density)), [(FIRST_NOTES[0] + 1, 8, 128)])[0]
    *later, faces = lax.optimization_barrier((view(source_term), view(inverse_density), faces))
    source, beta, beta1 = call(k_load, 1, (box_counts, *later), [fine, fine, mid])
    beta_rows, place = call(k_bottom_beta, 2, (ghost_from, box_counts, beta1), [(24, 128)], tables=[(25,)])
    win = exchange(faces, FIRST, FIRST_NOTES)
    outs = call(
        k_weights, 0, (source, beta) + win, weight_shapes(32) + [fine, face0], [xg, gyf, ends, gyf],
        tables=[(5 * BOXES,)],
        extra=[pltpu.VMEM((40, 128), I32), pltpu.SMEM((40, 128), I32), pltpu.SemaphoreType.DMA],
    )
    w, (first, faces, tab) = tuple(outs[:6]), outs[6:]
    w1 = tuple(call(k_weights_next, 1, (tab, beta1) + win, weight_shapes(16), [xg, gym, ends, gym]))
    u, u_x, u_y, first_x, first_y, f1, first1, faces = call(
        k_down, 1, (tab, source, first) + exchange(faces, [PART0]) + w + (w1[4],),
        [fine, gx, gyf, gx, gyf, mid, mid, face1], [xg, gyf, ends, gyf, fine],
    )
    u1, u1_x, u1_y, first1_x, first1_y, rows = call(
        k_bottom_rhs, 1, (tab, f1, first1, beta_rows) + exchange(faces, [PART1]) + w1,
        [mid, gx, gym, gx, gym, (32, 128)], [xg, gym, ends, gym, mid],
    )
    cube, padded = (SLOTS, 8, 8, 8, 128), (SLOTS, 10, 10, 8, 128)
    kept = [first1, u1, u1_x, u1_y] + list(w1[:5])
    u1, faces, boxes = call(
        k_bottom, 1, (place,) + gather_rows(rows) + tuple(kept), [mid, face1, (8, 128)],
        [padded, cube, cube, cube, (SLOTS, 8, 9, 8, 128), (SLOTS, 9, 8, 8, 128), cube, (DEVICES, 24, 128),
         (128, 128), (DEVICES, 24, 128), mid, gx, gym, gym] + [a.shape for a in kept],
        hbm=len(kept), extra=[pltpu.SemaphoreType.DMA((len(kept),))],
    )
    u, faces = call(
        k_up, 1,
        (tab, first1, first1_x, first1_y, u1, first, u, u_x, u_y) + exchange(faces, [PART1]) + w1 + w,
        [fine, face0], [mid, gx, gym, xg, gym, ends, gym, fine, gx, gyf, gyf],
    )
    u, residual, sums = call(
        k_residual, 1, (tab, source, u, first, first_x, first_y) + exchange(faces, [PART0]) + w,
        [fine, (256, SLOTS, 128), (1, 128)], [gx, gyf, xg, gyf, ends, gyf, fine],
    )
    parts = to_all(sums).reshape(DEVICES, 128)
    correction, norm = call(k_finish, 1, (box_counts, u, parts, boxes), [(256, SLOTS, 128), (1, 128)])
    back = lambda a: a.transpose(1, 0, 2).reshape(SLOTS, 32768)
    return back(correction), back(residual), norm[0, 0]


def solution(mesh):
    rows = P(AX, None)
    return jax.shard_map(
        shards, mesh=mesh, in_specs=(rows, rows, P(AX), rows), out_specs=(rows, rows, P()), check_vma=False
    )
```
